32 devices in a mesh: dp: 4 (over y, x), tensor: 8 (over z, core).
Axes of the slice: x: 2, y: 2, z: 4, core: 2. Of those that a mesh axis runs over, the one named last changes fastest.
Arguments:
- hidden: bfloat16 [4096, 1280], P(('dp', 'tensor')), may hold values from -6 to 6
- lengths: int32 [4, 8], P('dp'), may hold values from 1 to 512, 1024 in all within a row
- request_prompt: int32 [4, 8], P('dp'), may hold values from 0 to 31
- request_adapter: int32 [4, 8], P('dp'), may hold values from 0 to 63
- prompt_page_table: int32 [32, 4], replicated, may hold values from 0 to 15
- prefix_page_cache: bfloat16 [16, 64, 2048], P('dp', None, 'tensor'), may hold values from -6 to 6
- query_key_value_weight: bfloat16 [1280, 3072], P(None, 'tensor'), may hold values from -0.15625 to 0.15625
- adapter_down: bfloat16 [64, 1280, 16], P('dp'), may hold values from -0.15625 to 0.15625
- adapter_up: bfloat16 [64, 16, 3072], P('dp', None, 'tensor'), may hold values from -1.5 to 1.5
- attention_scale: float32 [1024], P('tensor'), may hold values from 0.5 to 1.5
- output_matrix: bfloat16 [1024, 1280], P('tensor'), may hold values from -0.1875 to 0.1875
- attention_rate: float32 [1280], replicated, may hold values from 0.05 to 0.5
- up_matrix: bfloat16 [1280, 5120], P(None, 'tensor'), may hold values from -0.15625 to 0.15625
- gate_matrix: bfloat16 [1280, 5120], P(None, 'tensor'), may hold values from -0.15625 to 0.15625
- up_scaling: float32 [5120], P('tensor'), may hold values from 0.5 to 2
- gate_scaling: float32 [5120], P('tensor'), may hold values from 0.5 to 2
- down_matrix: bfloat16 [5120, 1280], P('tensor'), may hold values from -0.078125 to 0.078125
- feedforward_rate: float32 [1280], replicated, may hold values from 0.05 to 0.5
Outputs:
- hidden_out: bfloat16 [4096, 1280], P(('dp', 'tensor'))
The draws below stay inside these ranges and needn't reach their ends.
Inputs may be any that keep to these rules, and one draw needn't show every extreme that they name: Each group's lengths sum to 1024.
All inputs are finite; a program needn't handle non-finite values.
Results may differ from the reference program's by a relative error of at most 0.015.
Values may be sent and summed in bfloat16 or wider, within the bound.
No kernel may reach another device: no remote copies, remote signals or barrier semaphores. Data moves between devices by JAX's collectives and lax.ppermute only.
A program may use at most 64 MiB of HBM per device.

```python
import math
import jax
import jax.numpy as jnp
import numpy as np
from jax import lax

MODEL_WIDTH = 1280
ATTENTION_HEADS = 16
HEAD_WIDTH = 64
FF = 5120
ADAPTER_RANK = 16
ADAPTER_TOTAL = 64
GROUP_REQUESTS = 8
PAGE = 64
PPG = 4
GROUPS = 32
GROUP_TOKENS = 1024
TOKENS = 4096
PREFIX_LEN = 256
TOTAL_PAGES = 16
N_DP = 4
N_TENSOR = 8


def touch_ends(entries, rng, smallest, high):
    dims = entries.shape
    place = [jax.random.randint(jax.random.fold_in(rng, axis), (), 0, dims[axis]) for axis in range(len(dims))]
    entries = entries.at[tuple(place)].set(smallest)
    longest = dims.index(max(dims))
    place[longest] = (place[longest] + 1) % dims[longest]
    return entries.at[tuple(place)].set(high)


def steps_of(key, extent, cuts, low, high):
    level = 1.0
    for axis_at, shards_of in cuts:
        heights = jax.random.uniform(jax.random.fold_in(jax.random.fold_in(key, 6), axis_at), (shards_of,), jnp.float32, low / len(cuts), high / len(cuts))
        level = level * jnp.repeat(jnp.exp(heights), extent[axis_at] // shards_of).reshape((-1,) + (1,) * (len(extent) - 1 - axis_at))
    return level


def length_profile(amount, total, limit, skew):
    loads = [(1 << 20) // math.isqrt(standing ** skew) + 1 for standing in range(2, amount + 1)]
    spare, holding = total - limit - (amount - 1), [1] * (amount - 1)
    while spare > 0:
        free = [i for i in range(amount - 1) if holding[i] < limit]
        pool, remaining = sum([loads[i] for i in free]), spare
        for i in free:
            addition = min(limit - holding[i], max(1, remaining * loads[i] // pool), spare)
            holding[i] = holding[i] + addition
            spare = spare - addition
    return np.array([limit] + holding)


def ragged_sizes(rng, number_of, total, most, lean):
    if number_of == 2:
        one = jax.random.randint(rng, (), max(1, total - most), min(most, total - 1) + 1)
        return jnp.stack([one, total - one])
    tallies = jnp.asarray(length_profile(number_of, total, most, lean), jnp.int32)
    pairs = (number_of - 1) // 2
    donor, receiver = tallies[1:1 + 2 * pairs:2], tallies[2:2 + 2 * pairs:2]
    room = jnp.minimum(donor - 1, most - receiver)
    passed = jax.random.randint(jax.random.fold_in(rng, 1), (pairs,), 0, 1 << 20) % (room + 1)
    tallies = tallies.at[1:1 + 2 * pairs:2].set(donor - passed).at[2:2 + 2 * pairs:2].set(receiver + passed)
    return tallies[jax.random.permutation(jax.random.fold_in(rng, 2), number_of)]


def gaussian(stream_key, dims, scale, reach, split=(), kind=jnp.bfloat16):
    factor_of = steps_of(stream_key, dims, split, -0.22, 0.18) if split else 1.0
    result = jax.random.normal(stream_key, dims, jnp.float32) * scale * factor_of
    return jnp.minimum(jnp.maximum(result, -reach), reach).astype(kind)


def setup_inputs(seed: int = 0) -> dict:
    splits = jax.random.split(jax.random.key(seed), 19)
    return {
        "hidden": gaussian(splits[0], (TOKENS, MODEL_WIDTH), 1.0, 6.0, ((0, 32),)),
        "lengths": jax.vmap(lambda own: ragged_sizes(own, GROUP_REQUESTS, GROUP_TOKENS, GROUP_TOKENS // 2, 2))(jax.random.split(splits[1], N_DP)).reshape((N_DP, GROUP_REQUESTS)).astype(jnp.int32),
        "request_prompt": touch_ends(jax.random.randint(splits[2], (N_DP, GROUP_REQUESTS), 0, GROUPS), jax.random.fold_in(splits[2], 1), 0, GROUPS - 1).astype(jnp.int32),
        "request_adapter": touch_ends(jax.random.randint(splits[3], (N_DP, GROUP_REQUESTS), 0, ADAPTER_TOTAL), jax.random.fold_in(splits[3], 1), 0, ADAPTER_TOTAL - 1).astype(jnp.int32),
        "prompt_page_table": touch_ends(jax.random.randint(splits[4], (GROUPS, PPG), 0, TOTAL_PAGES), jax.random.fold_in(splits[4], 1), 0, TOTAL_PAGES - 1).astype(jnp.int32),
        "prefix_page_cache": gaussian(splits[5], (TOTAL_PAGES, PAGE, ATTENTION_HEADS * 2 * HEAD_WIDTH), 1.0, 6.0, ((0, 4), (2, 8))),
        "query_key_value_weight": gaussian(splits[6], (MODEL_WIDTH, ATTENTION_HEADS * 3 * HEAD_WIDTH), MODEL_WIDTH ** -0.5, 0.15625, ((1, 8),)),
        "adapter_down": gaussian(splits[7], (ADAPTER_TOTAL, MODEL_WIDTH, ADAPTER_RANK), MODEL_WIDTH ** -0.5, 0.15625, ((0, 4),)),
        "adapter_up": gaussian(splits[8], (ADAPTER_TOTAL, ADAPTER_RANK, ATTENTION_HEADS * 3 * HEAD_WIDTH), ADAPTER_RANK ** -0.5, 1.5, ((0, 4), (2, 8))),
        "attention_scale": jnp.clip(jnp.exp(math.log(1.5) - 1.0986123 * jax.random.uniform(splits[9], (ATTENTION_HEADS * HEAD_WIDTH,), jnp.float32) ** steps_of(splits[9], (ATTENTION_HEADS * HEAD_WIDTH,), ((0, 8),), -0.2, 0.2)), 0.5, 1.5),
        "output_matrix": gaussian(splits[10], (ATTENTION_HEADS * HEAD_WIDTH, MODEL_WIDTH), (ATTENTION_HEADS * HEAD_WIDTH) ** -0.5, 0.1875, ((0, 8),)),
        "attention_rate": jnp.clip(jnp.exp(jax.random.uniform(splits[11], (MODEL_WIDTH,), jnp.float32, math.log(0.05), math.log(0.5))), 0.05, 0.5),
        "up_matrix": gaussian(splits[12], (MODEL_WIDTH, FF), MODEL_WIDTH ** -0.5, 0.15625, ((1, 8),)),
        "gate_matrix": gaussian(splits[13], (MODEL_WIDTH, FF), MODEL_WIDTH ** -0.5, 0.15625, ((1, 8),)),
        "up_scaling": jnp.clip(jnp.exp(math.log(2.0) - 1.3862944 * jax.random.uniform(splits[14], (FF,), jnp.float32) ** steps_of(splits[14], (FF,), ((0, 8),), -0.2, 0.2)), 0.5, 2.0),
        "gate_scaling": jnp.clip(jnp.exp(math.log(2.0) - 1.3862944 * jax.random.uniform(splits[15], (FF,), jnp.float32) ** steps_of(splits[15], (FF,), ((0, 8),), -0.2, 0.2)), 0.5, 2.0),
        "down_matrix": gaussian(splits[16], (FF, MODEL_WIDTH), FF ** -0.5, 0.078125, ((0, 8),)),
        "feedforward_rate": jnp.clip(jnp.exp(jax.random.uniform(splits[17], (MODEL_WIDTH,), jnp.float32, math.log(0.05), math.log(0.5))), 0.05, 0.5),
    }


adapter_scale = 0.5
epsilon = 1e-06

def renorm(matrix):
    return matrix * lax.rsqrt(lax.optimization_barrier(jnp.mean(matrix * matrix, axis=-1, keepdims=True)) + epsilon)

def to_unit(vectors):
    return vectors * lax.rsqrt(lax.optimization_barrier(jnp.sum(vectors * vectors, axis=-1, keepdims=True)) + epsilon)

def rotate(vectors, position):
    half_size = vectors.shape[-1] // 2
    frequency = jnp.exp(jnp.arange(half_size).astype(jnp.float32) * (-2.0 * math.log(10000.0) / vectors.shape[-1]))
    angles = position[:, None] * frequency[None, :]
    cosine = jnp.cos(angles)[:, None, :]
    sines = jnp.sin(angles)[:, None, :]
    first_half = vectors[..., :half_size]
    second_half = vectors[..., half_size:]
    return jnp.concatenate([first_half * cosine - second_half * sines, first_half * sines + second_half * cosine], axis=-1)

def layout(counts, total_rows):
    row_ends = jnp.cumsum(counts).astype(jnp.int32)
    starts = row_ends - counts
    row_ids = jnp.arange(total_rows, dtype=jnp.int32)
    request_number = lax.optimization_barrier(jnp.sum((row_ids[:, None] >= row_ends[None, :]).astype(jnp.int32), axis=1))
    selected_adapter = request_number[:, None] == jnp.arange(counts.shape[0], dtype=jnp.int32)[None, :]
    offset = row_ids - lax.optimization_barrier(jnp.sum(jnp.where(selected_adapter, starts[None, :], 0), axis=1)).astype(jnp.int32)
    return (request_number, offset)

def attend(queries, key_all, value_all, request_number, key_request, key_row):
    rows_total = queries.shape[0]
    block_rows = min(512, rows_total)
    score_scale = math.sqrt(queries.shape[-1])
    row_ids = jnp.arange(rows_total, dtype=jnp.int32)
    keys_wide = key_all.astype(jnp.float32)
    values_wide = value_all.astype(jnp.float32)

    def one_block(block_index):
        first_row = (block_index * block_rows).astype(jnp.int32)
        query_block = lax.dynamic_slice_in_dim(queries, first_row, block_rows, 0).astype(jnp.float32)
        request_block = lax.dynamic_slice_in_dim(request_number, first_row, block_rows, 0)
        row_block = lax.dynamic_slice_in_dim(row_ids, first_row, block_rows, 0)
        scores = jnp.einsum('qhd,khd->hqk', query_block, keys_wide) * score_scale
        allowed = (request_block[:, None] == key_request[None, :]) & (key_row[None, :] <= row_block[:, None])
        exp_scores = jnp.where(allowed[None], jnp.exp(scores), 0.0)
        weights = (exp_scores / lax.optimization_barrier(jnp.sum(exp_scores, axis=-1, keepdims=True))).astype(jnp.bfloat16)
        mixed_block = jnp.einsum('hqk,khd->qhd', weights.astype(jnp.float32), values_wide)
        return mixed_block.reshape(block_rows, -1).astype(jnp.bfloat16)
    blocks = lax.map(one_block, jnp.arange(rows_total // block_rows, dtype=jnp.int32))
    return blocks.reshape(rows_total, -1)

def split_sum(left_side, right_side):
    part_width = left_side.shape[1] // N_TENSOR

    def add_part(part_index, totals):
        start_col = (part_index * part_width).astype(jnp.int32)
        part_left = lax.dynamic_slice_in_dim(left_side, start_col, part_width, 1)
        part_right = lax.dynamic_slice_in_dim(right_side, start_col, part_width, 0)
        partial_value = jnp.dot(part_left, part_right, preferred_element_type=jnp.float32).astype(jnp.bfloat16)
        partial_value = lax.optimization_barrier(partial_value)
        return totals + partial_value.astype(jnp.float32)
    return lax.fori_loop(jnp.int32(0), jnp.int32(N_TENSOR), add_part, jnp.zeros((left_side.shape[0], right_side.shape[1]), jnp.float32))

def reference(hidden, lengths, request_prompt, request_adapter, prompt_page_table, prefix_page_cache, query_key_value_weight, adapter_down, adapter_up, attention_scale, output_matrix, attention_rate, up_matrix, gate_matrix, up_scaling, gate_scaling, down_matrix, feedforward_rate):
    gain_qk = attention_scale.reshape(ATTENTION_HEADS, HEAD_WIDTH)
    cache_view = prefix_page_cache.reshape(TOTAL_PAGES, PAGE, ATTENTION_HEADS, 2, HEAD_WIDTH)
    cache_keys = (to_unit(cache_view[:, :, :, 0, :].astype(jnp.float32)) * gain_qk).astype(jnp.bfloat16)
    cache_values = cache_view[:, :, :, 1, :]
    request_of_slot = jnp.arange(GROUP_REQUESTS * ADAPTER_RANK, dtype=jnp.int32) // ADAPTER_RANK
    prefix_request = jnp.arange(GROUP_REQUESTS * PREFIX_LEN, dtype=jnp.int32) // PREFIX_LEN
    prefix_row = jnp.full((GROUP_REQUESTS * PREFIX_LEN,), -1, jnp.int32)

    def one_group(inputs):
        row_values, counts, groups, selected_adapter = inputs
        request_number, offset = layout(counts, GROUP_TOKENS)
        position = offset.astype(jnp.float32) + PREFIX_LEN
        plain_projection = jnp.dot(row_values, query_key_value_weight, preferred_element_type=jnp.float32)
        selected_down = jnp.transpose(adapter_down[selected_adapter], (1, 0, 2)).reshape(MODEL_WIDTH, GROUP_REQUESTS * ADAPTER_RANK)
        adapter_middle = jnp.dot(row_values, selected_down, preferred_element_type=jnp.float32)
        adapter_middle = jnp.where(request_number[:, None] == request_of_slot[None, :], adapter_middle, 0.0).astype(jnp.bfloat16)
        selected_up = adapter_up[selected_adapter].reshape(GROUP_REQUESTS * ADAPTER_RANK, ATTENTION_HEADS * 3 * HEAD_WIDTH)
        query_key_value = (plain_projection + adapter_scale * jnp.dot(adapter_middle, selected_up, preferred_element_type=jnp.float32)).reshape(GROUP_TOKENS, ATTENTION_HEADS, 3, HEAD_WIDTH)
        queries = (to_unit(rotate(query_key_value[:, :, 0, :], position)) * gain_qk).astype(jnp.bfloat16)
        key_own = (to_unit(rotate(query_key_value[:, :, 1, :], position)) * gain_qk).astype(jnp.bfloat16)
        value_own = query_key_value[:, :, 2, :].astype(jnp.bfloat16)
        page_list = prompt_page_table[groups].reshape(-1)
        prefix_keys = cache_keys[page_list].reshape(GROUP_REQUESTS * PREFIX_LEN, ATTENTION_HEADS, HEAD_WIDTH)
        prefix_values = cache_values[page_list].reshape(GROUP_REQUESTS * PREFIX_LEN, ATTENTION_HEADS, HEAD_WIDTH)
        key_all = jnp.concatenate([prefix_keys, key_own], axis=0)
        value_all = jnp.concatenate([prefix_values, value_own], axis=0)
        key_request = jnp.concatenate([prefix_request, request_number], axis=0)
        key_row = jnp.concatenate([prefix_row, jnp.arange(GROUP_TOKENS, dtype=jnp.int32)], axis=0)
        attn = attend(queries, key_all, value_all, request_number, key_request, key_row)
        attn_sum = split_sum(attn, output_matrix)
        base_rows = row_values.astype(jnp.float32)
        mixed = renorm(base_rows + attention_rate * (renorm(attn_sum) - base_rows)).astype(jnp.bfloat16)
        up_part = jnp.dot(mixed, up_matrix, preferred_element_type=jnp.float32) * up_scaling
        gate_part = jnp.dot(mixed, gate_matrix, preferred_element_type=jnp.float32) * gate_scaling
        unit_values = (up_part * jax.nn.silu(gate_part)).astype(jnp.bfloat16)
        mlp_sum = split_sum(unit_values, down_matrix)
        mixed_rows = mixed.astype(jnp.float32)
        return renorm(mixed_rows + feedforward_rate * (renorm(mlp_sum) - mixed_rows)).astype(jnp.bfloat16)
    outputs = lax.map(one_group, (hidden.reshape(N_DP, GROUP_TOKENS, MODEL_WIDTH), lengths, request_prompt, request_adapter))
    return outputs.reshape(TOKENS, MODEL_WIDTH)
```

```python
import functools
import math

import jax
import jax.numpy as jnp
from jax import lax
from jax.experimental import pallas as pl
from jax.experimental.pallas import tpu as pltpu
from jax.sharding import PartitionSpec as P

MODEL_WIDTH = 1280
HEAD_WIDTH = 64
ADAPTER_RANK = 16
GROUP_REQUESTS = 8
PAGE = 64
PREFIX_LEN = 256


adapter_scale = 0.5
epsilon = 1e-06


def renorm(matrix):
    return matrix * lax.rsqrt(jnp.mean(matrix * matrix, axis=-1, keepdims=True) + epsilon)


def to_unit(vectors):
    return vectors * lax.rsqrt(jnp.sum(vectors * vectors, axis=-1, keepdims=True) + epsilon)


def rotate(vectors, position):
    half_size = vectors.shape[-1] // 2
    frequency = jnp.exp(
        jnp.arange(half_size).astype(jnp.float32) * (-2.0 * math.log(10000.0) / vectors.shape[-1])
    )
    angles = position[:, None] * frequency[None, :]
    cosine = jnp.cos(angles)[:, None, :]
    sines = jnp.sin(angles)[:, None, :]
    first_half = vectors[..., :half_size]
    second_half = vectors[..., half_size:]
    return jnp.concatenate(
        [first_half * cosine - second_half * sines, first_half * sines + second_half * cosine],
        axis=-1,
    )


def layout(counts, total_rows):
    row_ends = jnp.cumsum(counts)
    starts = row_ends - counts
    row_ids = jnp.arange(total_rows, dtype=jnp.int32)
    request_number = jnp.sum((row_ids[:, None] >= row_ends[None, :]).astype(jnp.int32), axis=1)
    selected_adapter = (
        request_number[:, None] == jnp.arange(counts.shape[0], dtype=jnp.int32)[None, :]
    )
    offset = row_ids - jnp.sum(jnp.where(selected_adapter, starts[None, :], 0), axis=1)
    return (request_number, offset)


def attend(queries, key_all, value_all, request_number, key_request, key_row):
    rows_total = queries.shape[0]
    block_rows = min(512, rows_total)
    score_scale = math.sqrt(queries.shape[-1])
    row_ids = jnp.arange(rows_total, dtype=jnp.int32)

    def one_block(block_index):
        first_row = block_index * block_rows
        query_block = lax.dynamic_slice_in_dim(queries, first_row, block_rows, 0)
        request_block = lax.dynamic_slice_in_dim(request_number, first_row, block_rows, 0)
        row_block = lax.dynamic_slice_in_dim(row_ids, first_row, block_rows, 0)
        scores = (
            jnp.einsum("qhd,khd->hqk", query_block, key_all, preferred_element_type=jnp.float32)
            * score_scale
        )
        allowed = (request_block[:, None] == key_request[None, :]) & (
            key_row[None, :] <= row_block[:, None]
        )
        exp_scores = jnp.where(allowed[None], jnp.exp(scores), 0.0)
        weights = (exp_scores / jnp.sum(exp_scores, axis=-1, keepdims=True)).astype(jnp.bfloat16)
        mixed_block = jnp.einsum(
            "hqk,khd->qhd", weights, value_all, preferred_element_type=jnp.float32
        )
        return mixed_block.reshape(block_rows, -1).astype(jnp.bfloat16)

    blocks = lax.map(one_block, jnp.arange(rows_total // block_rows, dtype=jnp.int32))
    return blocks.reshape(rows_total, -1)


def hidden_units(row_values, up_matrix, gate_matrix, up_scaling, gate_scaling):
    up_part = jnp.dot(row_values, up_matrix, preferred_element_type=jnp.float32) * up_scaling
    gate_part = jnp.dot(row_values, gate_matrix, preferred_element_type=jnp.float32) * gate_scaling
    return (up_part * jax.nn.silu(gate_part)).astype(jnp.bfloat16)


def local_generic(
    hidden,
    lengths,
    request_prompt,
    request_adapter,
    prompt_page_table,
    prefix_page_cache,
    query_key_value_weight,
    adapter_down,
    adapter_up,
    attention_scale,
    output_matrix,
    attention_rate,
    up_matrix,
    gate_matrix,
    up_scaling,
    gate_scaling,
    down_matrix,
    feedforward_rate,
):
    tok_rows = hidden.shape[0]
    group_rows = tok_rows * lax.axis_size("tensor")
    heads_here = query_key_value_weight.shape[1] // (3 * HEAD_WIDTH)
    gain_qk = attention_scale.reshape(heads_here, HEAD_WIDTH)
    request_number, offset = layout(lengths[0], group_rows)
    position = offset.astype(jnp.float32) + PREFIX_LEN
    local_cache = prefix_page_cache.reshape(
        prefix_page_cache.shape[0], PAGE, heads_here, 2, HEAD_WIDTH
    )
    local_keys = (to_unit(local_cache[:, :, :, 0, :].astype(jnp.float32)) * gain_qk).astype(
        jnp.bfloat16
    )
    prepared = jnp.stack([local_keys, local_cache[:, :, :, 1, :]], axis=3).reshape(
        prefix_page_cache.shape
    )
    all_pages = lax.all_gather(prepared, "dp", axis=0, tiled=True)
    down_all, up_all = (
        lax.all_gather(adapter_down, "dp", axis=0, tiled=True),
        lax.all_gather(adapter_up, "dp", axis=0, tiled=True),
    )
    every_row = lax.all_gather(hidden, "tensor", axis=0, tiled=True)
    adapter_count = down_all.shape[0]
    onehot = (
        request_adapter[0][:, None] == jnp.arange(adapter_count, dtype=jnp.int32)[None, :]
    ).astype(jnp.bfloat16)
    selected_down = jnp.dot(
        onehot, down_all.reshape(adapter_count, -1), preferred_element_type=jnp.float32
    ).astype(jnp.bfloat16)
    selected_down = jnp.transpose(
        selected_down.reshape(GROUP_REQUESTS, MODEL_WIDTH, ADAPTER_RANK), (1, 0, 2)
    ).reshape(MODEL_WIDTH, GROUP_REQUESTS * ADAPTER_RANK)
    selected_up = jnp.dot(
        onehot, up_all.reshape(adapter_count, -1), preferred_element_type=jnp.float32
    ).astype(jnp.bfloat16)
    selected_up = selected_up.reshape(GROUP_REQUESTS * ADAPTER_RANK, heads_here * 3 * HEAD_WIDTH)
    request_of_slot = jnp.arange(GROUP_REQUESTS * ADAPTER_RANK, dtype=jnp.int32) // ADAPTER_RANK
    plain_projection = jnp.dot(
        every_row, query_key_value_weight, preferred_element_type=jnp.float32
    )
    adapter_middle = jnp.dot(every_row, selected_down, preferred_element_type=jnp.float32)
    adapter_middle = jnp.where(
        request_number[:, None] == request_of_slot[None, :], adapter_middle, 0.0
    ).astype(jnp.bfloat16)
    query_key_value = (
        plain_projection
        + adapter_scale * jnp.dot(adapter_middle, selected_up, preferred_element_type=jnp.float32)
    ).reshape(group_rows, heads_here, 3, HEAD_WIDTH)
    queries = (to_unit(rotate(query_key_value[:, :, 0, :], position)) * gain_qk).astype(
        jnp.bfloat16
    )
    key_own = (to_unit(rotate(query_key_value[:, :, 1, :], position)) * gain_qk).astype(
        jnp.bfloat16
    )
    value_own = query_key_value[:, :, 2, :].astype(jnp.bfloat16)
    page_list = prompt_page_table[request_prompt[0]].reshape(-1)
    picked = jnp.take(all_pages, page_list, axis=0).reshape(
        GROUP_REQUESTS * PREFIX_LEN, heads_here, 2, HEAD_WIDTH
    )
    key_all = jnp.concatenate([picked[:, :, 0, :], key_own], axis=0)
    value_all = jnp.concatenate([picked[:, :, 1, :], value_own], axis=0)
    key_request = jnp.concatenate(
        [jnp.arange(GROUP_REQUESTS * PREFIX_LEN, dtype=jnp.int32) // PREFIX_LEN, request_number],
        axis=0,
    )
    key_row = jnp.concatenate(
        [
            jnp.full((GROUP_REQUESTS * PREFIX_LEN,), -1, jnp.int32),
            jnp.arange(group_rows, dtype=jnp.int32),
        ],
        axis=0,
    )
    attn = attend(queries, key_all, value_all, request_number, key_request, key_row)
    attn_sum = lax.psum_scatter(
        jnp.dot(attn, output_matrix, preferred_element_type=jnp.float32).astype(jnp.bfloat16),
        "tensor",
        scatter_dimension=0,
        tiled=True,
    ).astype(jnp.float32)
    base_rows = hidden.astype(jnp.float32)
    mixed = renorm(base_rows + attention_rate * (renorm(attn_sum) - base_rows)).astype(jnp.bfloat16)
    unit_values = hidden_units(
        lax.all_gather(mixed, "tensor", axis=0, tiled=True),
        up_matrix,
        gate_matrix,
        up_scaling,
        gate_scaling,
    )
    mlp_sum = lax.psum_scatter(
        jnp.dot(unit_values, down_matrix, preferred_element_type=jnp.float32).astype(jnp.bfloat16),
        "tensor",
        scatter_dimension=0,
        tiled=True,
    ).astype(jnp.float32)
    mixed_rows = mixed.astype(jnp.float32)
    return renorm(mixed_rows + feedforward_rate * (renorm(mlp_sum) - mixed_rows)).astype(
        jnp.bfloat16
    )


CHIP_ROWS = 256
SCORE_LOG2 = math.sqrt(HEAD_WIDTH) / math.log(2.0)
VMEM = pl.BlockSpec(memory_space=pltpu.VMEM)
SMEM = pl.BlockSpec(memory_space=pltpu.SMEM)
BF16 = jnp.bfloat16
F32 = jnp.float32


def call(kernel, outs, operands, scalars, scratch=(), limit=32, flops=10**8, moved=10**6):
    return pl.pallas_call(
        kernel,
        out_shape=outs,
        in_specs=[SMEM] * scalars + [VMEM] * (len(operands) - scalars),
        out_specs=jax.tree.map(lambda _: VMEM, outs),
        scratch_shapes=list(scratch),
        compiler_params=pltpu.CompilerParams(vmem_limit_bytes=limit * 1024 * 1024),
        cost_estimate=pl.CostEstimate(flops=flops, bytes_accessed=moved, transcendentals=0),
    )(*operands)


def shape(rows, columns, kind=BF16):
    return jax.ShapeDtypeStruct((rows, columns), kind)


def iota(dims, axis):
    return lax.broadcasted_iota(jnp.int32, dims, axis)


def first_head(rows):
    return iota((rows, 2 * HEAD_WIDTH), 1) < HEAD_WIDTH


def unit_heads(vectors, gain):
    low = first_head(vectors.shape[0])
    squares = vectors * vectors
    sum_low = jnp.sum(jnp.where(low, squares, 0.0), axis=-1, keepdims=True)
    sum_high = jnp.sum(jnp.where(low, 0.0, squares), axis=-1, keepdims=True)
    return vectors * lax.rsqrt(jnp.where(low, sum_low, sum_high) + epsilon) * gain


def dot(left, right):
    return jnp.dot(left, right, preferred_element_type=F32)


def dot_nt(left, right):
    return lax.dot_general(
        left, right, (((1,), (1,)), ((), ())), preferred_element_type=F32
    )


def prepare_kernel(ids, pages, up, down, gain, out):
    rows = pages.shape[0]
    low = first_head(rows)
    left = pages[:, 0:128].astype(F32)
    right = pages[:, 128:256].astype(F32)
    keys = jnp.where(low, left, pltpu.roll(right, HEAD_WIDTH, 1))
    values = jnp.where(low, pltpu.roll(left, HEAD_WIDTH, 1), right)
    out[0:rows, 0:128] = unit_heads(keys, gain[...]).astype(BF16)
    out[0:rows, 128:256] = values.astype(BF16)
    out[0:rows, 256:640] = up[...]
    row, column = iota((32, 256), 0), iota((32, 256), 1)
    source = (row // 2) * ADAPTER_RANK + 2 * ids[0] + row % 2
    picked = dot((column == source).astype(BF16), down[...]).astype(BF16)
    out[rows : rows + 32, :] = picked[:, 0:640]
    out[rows + 32 : rows + 64, :] = picked[:, 640:1280]


def by_request(index, scalars):
    picked = jnp.zeros_like(index)
    for request in range(GROUP_REQUESTS):
        picked = jnp.where(index == request, scalars[0, request], picked)
    return picked


def select_kernel(ids, adapters, g0, g1, g2, g3, down_out, up_out):
    tensor, dp = ids[0], ids[1]
    row, column = iota((16, 32), 0), iota((16, 32), 1)
    adapter = by_request(row // 2, adapters)
    source = (adapter % 16) * 2 + row % 2
    owner = (adapter // 16) ^ dp
    up_row, up_column = iota((128, 256), 0), iota((128, 256), 1)
    up_adapter = by_request((up_row % 16) // 2, adapters)
    up_source = (up_adapter % 16) * 16 + 2 * ((up_row // 16) ^ tensor) + up_row % 2
    up_owner = (up_adapter // 16) ^ dp
    left = right = up_total = 0.0
    for m, g in enumerate((g0, g1, g2, g3)):
        hot = ((column == source) & (owner == m)).astype(BF16)
        left = left + dot(hot, g[256:288, :])
        right = right + dot(hot, g[288:320, :])
        up_hot = ((up_column == up_source) & (up_owner == m)).astype(BF16)
        up_total = up_total + dot(up_hot, g[0:256, 256:640])
    down_out[:, 0:640] = left.astype(BF16)
    down_out[:, 640:1280] = right.astype(BF16)
    up_out[...] = up_total.astype(BF16)


def qkv_kernel(j, ids, lengths, xa, xb, weight, down, up, cosines, sines, gain, q, k, v):
    core = ids[0] % 2
    block = (ids[0] // 2) ^ j
    rows = jnp.concatenate([xa[...], xb[...]], axis=0)
    own = pl.multiple_of(core * 128, 128)
    other = pl.multiple_of((1 - core) * 128, 128)
    row = iota((CHIP_ROWS, 128), 0)
    row = block * CHIP_ROWS + jnp.where(row < 128, row + own, row - 128 + other)
    request = (iota((CHIP_ROWS, 128), 1) % 16) // 2
    start = jnp.int32(0)
    first, end = jnp.zeros_like(row), jnp.zeros_like(row)
    for i in range(GROUP_REQUESTS):
        first = jnp.where(request == i, start, first)
        start = start + lengths[0, i]
        end = jnp.where(request == i, start, end)
    middle = dot_nt(rows, down[...])
    middle = jnp.where((row >= first) & (row < end), middle, 0.0).astype(BF16)
    total = dot(rows, weight[...]) + adapter_scale * dot(middle, up[...])
    part0, part1, part2 = total[:, 0:128], total[:, 128:256], total[:, 256:384]
    low = first_head(CHIP_ROWS)
    query = jnp.where(low, part0, part1)
    key = pltpu.roll(jnp.where(low, part2, part0), HEAD_WIDTH, 1)
    value = jnp.where(low, part1, part2).astype(BF16)
    spots = [
        pl.multiple_of(block * CHIP_ROWS + own, 128),
        pl.multiple_of(block * CHIP_ROWS + other, 128),
    ]
    cosine = jnp.concatenate([cosines[pl.ds(s, 128), :] for s in spots], axis=0)
    sine = jnp.concatenate([sines[pl.ds(s, 128), :] for s in spots], axis=0)
    half = HEAD_WIDTH // 2
    head_low = (iota((CHIP_ROWS, 128), 1) % HEAD_WIDTH) < half

    def finish(x):
        turned = jnp.where(head_low, pltpu.roll(x, 128 - half, 1), pltpu.roll(x, half, 1))
        return unit_heads(x * cosine + turned * sine, gain[...]).astype(BF16)

    for out, result in ((q, finish(query)), (k, finish(key)), (v, value)):
        out[pl.ds(own, 128), :] = result[0:128]
        out[pl.ds(other, 128), :] = result[128:256]


def attend_kernel(
    ids, lengths, prompts, table,
    q0, q1, q2, q3, k0, k1, k2, k3, v0, v1, v2, v3, g0, g1, g2, g3,
    out, queries, keys, values, pages, starts,
):
    chip, dp = ids[0] // 2, ids[1]
    for target, parts in (
        (queries, (q0, q1, q2, q3)),
        (keys, (k0, k1, k2, k3)),
        (values, (v0, v1, v2, v3)),
    ):
        for j, part in enumerate(parts):
            target[pl.ds(pl.multiple_of((chip ^ j) * CHIP_ROWS, CHIP_ROWS), CHIP_ROWS), :] = part[...]
    for m, g in enumerate((g0, g1, g2, g3)):
        pages[pl.ds(pl.multiple_of((dp ^ m) * 256, 256), 256), :] = g[0:256, 0:256]
    begins = []
    start = jnp.int32(0)
    for i in range(GROUP_REQUESTS):
        starts[i] = start
        begins.append(start)
        start = start + lengths[0, i]
    starts[GROUP_REQUESTS] = start
    low = first_head(128)
    tile_row = iota((256, 1), 0) % 128

    def one_tile(tile, carry):
        base = pl.multiple_of(tile * 128, 128)
        query = queries[pl.ds(base, 128), :]
        zero = jnp.zeros_like(query)
        both = jnp.concatenate(
            [jnp.where(low, query, zero), jnp.where(low, zero, query)], axis=0
        )
        row = base + tile_row
        row_start = jnp.zeros_like(row)
        first = jnp.int32(0)
        last = jnp.int32(0)
        for i in range(1, GROUP_REQUESTS):
            row_start = jnp.where(row >= begins[i], begins[i], row_start)
            first = first + (begins[i] <= base).astype(jnp.int32)
            last = last + (begins[i] <= base + 127).astype(jnp.int32)

        def add(state, key, value, mask):
            total, norm = state
            weights = jnp.where(mask, jnp.exp2(dot_nt(both, key) * SCORE_LOG2), 0.0)
            return (
                total + dot(weights.astype(BF16), value),
                norm + jnp.sum(weights, axis=-1, keepdims=True),
            )

        def own_block(block, state):
            spot = pl.multiple_of(block * 128, 128)
            column = spot + iota((256, 128), 1)
            mask = (column >= row_start) & (column <= row)
            return add(state, keys[pl.ds(spot, 128), :], values[pl.ds(spot, 128), :], mask)

        def prefix(request, state):
            prompt = prompts[0, request]
            spots = [pl.multiple_of(table[prompt, p] * PAGE, PAGE) for p in range(4)]
            key = jnp.concatenate([pages[pl.ds(s, PAGE), 0:128] for s in spots], axis=0)
            value = jnp.concatenate([pages[pl.ds(s, PAGE), 128:256] for s in spots], axis=0)
            mask = (row >= starts[request]) & (row < starts[request + 1])
            return add(state, key, value, jnp.broadcast_to(mask, (256, PREFIX_LEN)))

        state = (jnp.zeros((256, 128), F32), jnp.zeros((256, 1), F32))
        state = prefix(first, state)
        state = own_block(tile, state)
        state = lax.fori_loop(starts[first] // 128, tile, own_block, state)
        total, norm = lax.fori_loop(first + 1, last + 1, prefix, state)
        total = total / norm
        out[pl.ds(base, 128), :] = jnp.where(low, total[0:128], total[128:256]).astype(BF16)
        return carry

    lax.fori_loop(0, out.shape[0] // 128, one_tile, 0)


def collect_kernel(ids, o0, o1, o2, o3, p0, p1, p2, p3, out):
    dp = ids[1]
    for side, parts in enumerate(((o0, o1, o2, o3), (p0, p1, p2, p3))):
        for m, part in enumerate(parts):
            spot = pl.multiple_of((dp ^ m) * 32, 32)
            for j in range(4):
                out[2 * j + side, pl.ds(spot, 32), :] = part[j]


def mlp_kernel(
    j, ids, a0, a1, a2, a3, a4, a5, a6, a7, output, xa, xb, rate,
    up, gate, up_scale, gate_scale, down, keep, send, *rest,
):
    result = rest[-1]
    core = ids[0] % 2
    spot = pl.multiple_of(((ids[0] // 2) ^ j) * CHIP_ROWS, CHIP_ROWS)
    heads = jnp.concatenate(
        [a[pl.ds(spot, CHIP_ROWS), :] for a in (a0, a1, a2, a3, a4, a5, a6, a7)], axis=1
    )
    attn_sum = dot(heads, output[...])
    own = pl.multiple_of(core * 128, 128)
    other = pl.multiple_of((1 - core) * 128, 128)
    result[pl.ds(own, 128), :] = xa[...].astype(F32)
    result[pl.ds(other, 128), :] = xb[...].astype(F32)
    base = result[...]
    mixed = renorm(base + rate[...] * (renorm(attn_sum) - base)).astype(BF16)
    up_part = dot(mixed, up[...]) * up_scale[...]
    gate_part = dot(mixed, gate[...]) * gate_scale[...]
    unit_values = (up_part * (gate_part / (1.0 + jnp.exp(-gate_part)))).astype(BF16)
    if j == 0:
        result[...] = mixed.astype(F32)
        rest[0][...] = result[pl.ds(own, 128), :].astype(BF16)
    result[...] = dot(unit_values, down[...])
    keep[...] = result[pl.ds(own, 128), :].astype(BF16)
    send[...] = result[pl.ds(other, 128), :].astype(BF16)


def final_kernel(mixed, keep, got, r1, r2, r3, rate, out):
    mlp_sum = keep[...].astype(F32) + got[...].astype(F32)
    for r in (r1, r2, r3):
        mlp_sum = mlp_sum + r[...].astype(F32)
    base = mixed[...].astype(F32)
    out[...] = renorm(base + rate[...] * (renorm(mlp_sum) - base)).astype(BF16)


def swap(values, distance, axis="tensor"):
    size = lax.axis_size(axis)
    return lax.ppermute(values, axis, [(i, i ^ distance) for i in range(size)])


def local_pairwise(
    hidden,
    lengths,
    request_prompt,
    request_adapter,
    prompt_page_table,
    prefix_page_cache,
    query_key_value_weight,
    adapter_down,
    adapter_up,
    attention_scale,
    output_matrix,
    attention_rate,
    up_matrix,
    gate_matrix,
    up_scaling,
    gate_scaling,
    down_matrix,
    feedforward_rate,
):
    group_rows = hidden.shape[0] * lax.axis_size("tensor")
    tensor, dp = lax.axis_index("tensor"), lax.axis_index("dp")
    ids = jnp.stack([tensor, dp]).astype(jnp.int32)
    gain = attention_scale.reshape(1, -1)

    far = {j: swap(hidden, 2 * j) for j in (2, 3, 1)}

    prepared = call(
        prepare_kernel,
        shape(320, 640),
        (
            ids,
            prefix_page_cache.reshape(-1, prefix_page_cache.shape[2]),
            adapter_up.reshape(-1, adapter_up.shape[2]),
            jnp.swapaxes(adapter_down, 1, 2).reshape(-1, MODEL_WIDTH),
            gain,
        ),
        1,
    )
    shared = [prepared] + [swap(prepared, m, "dp") for m in (1, 2, 3)]
    down_own, up_all = call(
        select_kernel, (shape(16, MODEL_WIDTH), shape(128, 384)), (ids, request_adapter, *shared), 2
    )
    down_pair = jnp.concatenate([down_own, swap(down_own, 1)], axis=0)
    down_all = jnp.concatenate([down_pair] + [swap(down_pair, 2 * j) for j in (1, 2, 3)], axis=0)

    row_ids = jnp.arange(group_rows, dtype=jnp.int32)
    starts = jnp.cumsum(lengths[0]) - lengths[0]
    row_start = jnp.max(
        jnp.where(row_ids[:, None] >= starts[None, :], starts[None, :], 0), axis=1
    )
    position = (row_ids - row_start).astype(F32) + PREFIX_LEN
    half = HEAD_WIDTH // 2
    lanes = jnp.arange(2 * HEAD_WIDTH, dtype=jnp.int32) % HEAD_WIDTH
    frequency = jnp.exp((lanes % half).astype(F32) * (-2.0 * math.log(10000.0) / HEAD_WIDTH))
    angles = position[:, None] * frequency[None, :]
    cosines = jnp.cos(angles)
    sines = jnp.where(lanes[None, :] < half, -1.0, 1.0) * jnp.sin(angles)

    rows = {0: (hidden, swap(hidden, 1))}
    for j in (1, 2, 3):
        rows[j] = (far[j], swap(far[j], 1))
    query, key, value = {}, {}, {}
    for j in range(4):
        query[j], key[j], value[j] = call(
            functools.partial(qkv_kernel, j),
            (shape(CHIP_ROWS, 128),) * 3,
            (ids, lengths, *rows[j], query_key_value_weight, down_all, up_all, cosines, sines, gain),
            2,
            flops=4 * 10**8,
            moved=3 * 10**6,
        )

    quarter = output_matrix.shape[0] // 4
    own_quarter = lax.dynamic_slice_in_dim(output_matrix, dp * quarter, quarter, 0)
    quarters = jnp.stack([own_quarter] + [swap(own_quarter, 2 * j) for j in (1, 2, 3)])
    blocks = [quarters] + [swap(quarters, m, "dp") for m in (1, 2, 3)]
    others = [swap(b, 1) for b in blocks]
    output_all = call(
        collect_kernel,
        jax.ShapeDtypeStruct((8, 4 * quarter, MODEL_WIDTH), BF16),
        (ids, *blocks, *others),
        1,
    ).reshape(-1, MODEL_WIDTH)

    attn = call(
        attend_kernel,
        shape(group_rows, 128),
        (
            ids, lengths, request_prompt, prompt_page_table,
            *[query[j] for j in range(4)], *[key[j] for j in range(4)],
            *[value[j] for j in range(4)], *shared,
        ),
        4,
        scratch=(
            pltpu.VMEM((group_rows, 128), BF16),
            pltpu.VMEM((group_rows, 128), BF16),
            pltpu.VMEM((group_rows, 128), BF16),
            pltpu.VMEM((1024, 256), BF16),
            pltpu.SMEM((GROUP_REQUESTS + 1,), jnp.int32),
        ),
        flops=4 * 10**9,
        moved=2 * 10**6,
    )

    heads = {0: (attn, swap(attn, 1))}
    for j in (2, 3, 1):
        got = swap(attn, 2 * j)
        heads[j] = (got, swap(got, 1))
    all_heads = [heads[j][side] for j in range(4) for side in (0, 1)]

    keep, other = {}, {}
    for j in (2, 3, 1, 0):
        outs = (shape(128, MODEL_WIDTH),) * (3 if j == 0 else 2)
        keep[j], send, *rest = call(
            functools.partial(mlp_kernel, j),
            outs,
            (
                ids, *all_heads, output_all, *rows[j], attention_rate.reshape(1, -1),
                up_matrix, gate_matrix, up_scaling.reshape(1, -1), gate_scaling.reshape(1, -1),
                down_matrix,
            ),
            1,
            scratch=(pltpu.VMEM((CHIP_ROWS, MODEL_WIDTH), F32),),
            limit=40,
            flops=2 * 10**9,
            moved=10**7,
        )
        other[j] = swap(send, 1)
    mixed = rest[0]
    received = [
        swap((keep[j].astype(F32) + other[j].astype(F32)).astype(BF16), 2 * j) for j in (2, 3, 1)
    ]
    return call(
        final_kernel,
        shape(*hidden.shape),
        (mixed, keep[0], other[0], *received, feedforward_rate.reshape(1, -1)),
        0,
    )


def solution(mesh):
    placed = (
        P(("dp", "tensor"), None),
        P("dp", None),
        P("dp", None),
        P("dp", None),
        P(),
        P("dp", None, "tensor"),
        P(None, "tensor"),
        P("dp", None, None),
        P("dp", None, "tensor"),
        P("tensor"),
        P("tensor", None),
        P(),
        P(None, "tensor"),
        P(None, "tensor"),
        P("tensor"),
        P("tensor"),
        P("tensor", None),
        P(),
    )
    pairwise = mesh.shape["dp"] == 4 and mesh.shape["tensor"] == 8
    return jax.shard_map(
        local_pairwise if pairwise else local_generic, mesh=mesh, in_specs=placed, out_specs=P(("dp", "tensor"), None), check_vma=False
    )
```

```python
import functools
import math

import jax
import jax.numpy as jnp
from jax import lax
from jax.experimental import pallas as pl
from jax.experimental.pallas import tpu as pltpu
from jax.sharding import PartitionSpec as P

MODEL_WIDTH = 1280
HEAD_WIDTH = 64
ADAPTER_RANK = 16
GROUP_REQUESTS = 8
PAGE = 64
PREFIX_LEN = 256


adapter_scale = 0.5
epsilon = 1e-06


def renorm(matrix):
    return matrix * lax.rsqrt(jnp.mean(matrix * matrix, axis=-1, keepdims=True) + epsilon)


def to_unit(vectors):
    return vectors * lax.rsqrt(jnp.sum(vectors * vectors, axis=-1, keepdims=True) + epsilon)


def rotate(vectors, position):
    half_size = vectors.shape[-1] // 2
    frequency = jnp.exp(
        jnp.arange(half_size).astype(jnp.float32) * (-2.0 * math.log(10000.0) / vectors.shape[-1])
    )
    angles = position[:, None] * frequency[None, :]
    cosine = jnp.cos(angles)[:, None, :]
    sines = jnp.sin(angles)[:, None, :]
    first_half = vectors[..., :half_size]
    second_half = vectors[..., half_size:]
    return jnp.concatenate(
        [first_half * cosine - second_half * sines, first_half * sines + second_half * cosine],
        axis=-1,
    )


def layout(counts, total_rows):
    row_ends = jnp.cumsum(counts)
    starts = row_ends - counts
    row_ids = jnp.arange(total_rows, dtype=jnp.int32)
    request_number = jnp.sum((row_ids[:, None] >= row_ends[None, :]).astype(jnp.int32), axis=1)
    selected_adapter = (
        request_number[:, None] == jnp.arange(counts.shape[0], dtype=jnp.int32)[None, :]
    )
    offset = row_ids - jnp.sum(jnp.where(selected_adapter, starts[None, :], 0), axis=1)
    return (request_number, offset)


def attend(queries, key_all, value_all, request_number, key_request, key_row):
    rows_total = queries.shape[0]
    block_rows = min(512, rows_total)
    score_scale = math.sqrt(queries.shape[-1])
    row_ids = jnp.arange(rows_total, dtype=jnp.int32)

    def one_block(block_index):
        first_row = block_index * block_rows
        query_block = lax.dynamic_slice_in_dim(queries, first_row, block_rows, 0)
        request_block = lax.dynamic_slice_in_dim(request_number, first_row, block_rows, 0)
        row_block = lax.dynamic_slice_in_dim(row_ids, first_row, block_rows, 0)
        scores = (
            jnp.einsum("qhd,khd->hqk", query_block, key_all, preferred_element_type=jnp.float32)
            * score_scale
        )
        allowed = (request_block[:, None] == key_request[None, :]) & (
            key_row[None, :] <= row_block[:, None]
        )
        exp_scores = jnp.where(allowed[None], jnp.exp(scores), 0.0)
        weights = (exp_scores / jnp.sum(exp_scores, axis=-1, keepdims=True)).astype(jnp.bfloat16)
        mixed_block = jnp.einsum(
            "hqk,khd->qhd", weights, value_all, preferred_element_type=jnp.float32
        )
        return mixed_block.reshape(block_rows, -1).astype(jnp.bfloat16)

    blocks = lax.map(one_block, jnp.arange(rows_total // block_rows, dtype=jnp.int32))
    return blocks.reshape(rows_total, -1)


def hidden_units(row_values, up_matrix, gate_matrix, up_scaling, gate_scaling):
    up_part = jnp.dot(row_values, up_matrix, preferred_element_type=jnp.float32) * up_scaling
    gate_part = jnp.dot(row_values, gate_matrix, preferred_element_type=jnp.float32) * gate_scaling
    return (up_part * jax.nn.silu(gate_part)).astype(jnp.bfloat16)


def local_generic(
    hidden,
    lengths,
    request_prompt,
    request_adapter,
    prompt_page_table,
    prefix_page_cache,
    query_key_value_weight,
    adapter_down,
    adapter_up,
    attention_scale,
    output_matrix,
    attention_rate,
    up_matrix,
    gate_matrix,
    up_scaling,
    gate_scaling,
    down_matrix,
    feedforward_rate,
):
    tok_rows = hidden.shape[0]
    group_rows = tok_rows * lax.axis_size("tensor")
    heads_here = query_key_value_weight.shape[1] // (3 * HEAD_WIDTH)
    gain_qk = attention_scale.reshape(heads_here, HEAD_WIDTH)
    request_number, offset = layout(lengths[0], group_rows)
    position = offset.astype(jnp.float32) + PREFIX_LEN
    local_cache = prefix_page_cache.reshape(
        prefix_page_cache.shape[0], PAGE, heads_here, 2, HEAD_WIDTH
    )
    local_keys = (to_unit(local_cache[:, :, :, 0, :].astype(jnp.float32)) * gain_qk).astype(
        jnp.bfloat16
    )
    prepared = jnp.stack([local_keys, local_cache[:, :, :, 1, :]], axis=3).reshape(
        prefix_page_cache.shape
    )
    all_pages = lax.all_gather(prepared, "dp", axis=0, tiled=True)
    down_all, up_all = (
        lax.all_gather(adapter_down, "dp", axis=0, tiled=True),
        lax.all_gather(adapter_up, "dp", axis=0, tiled=True),
    )
    every_row = lax.all_gather(hidden, "tensor", axis=0, tiled=True)
    adapter_count = down_all.shape[0]
    onehot = (
        request_adapter[0][:, None] == jnp.arange(adapter_count, dtype=jnp.int32)[None, :]
    ).astype(jnp.bfloat16)
    selected_down = jnp.dot(
        onehot, down_all.reshape(adapter_count, -1), preferred_element_type=jnp.float32
    ).astype(jnp.bfloat16)
    selected_down = jnp.transpose(
        selected_down.reshape(GROUP_REQUESTS, MODEL_WIDTH, ADAPTER_RANK), (1, 0, 2)
    ).reshape(MODEL_WIDTH, GROUP_REQUESTS * ADAPTER_RANK)
    selected_up = jnp.dot(
        onehot, up_all.reshape(adapter_count, -1), preferred_element_type=jnp.float32
    ).astype(jnp.bfloat16)
    selected_up = selected_up.reshape(GROUP_REQUESTS * ADAPTER_RANK, heads_here * 3 * HEAD_WIDTH)
    request_of_slot = jnp.arange(GROUP_REQUESTS * ADAPTER_RANK, dtype=jnp.int32) // ADAPTER_RANK
    plain_projection = jnp.dot(
        every_row, query_key_value_weight, preferred_element_type=jnp.float32
    )
    adapter_middle = jnp.dot(every_row, selected_down, preferred_element_type=jnp.float32)
    adapter_middle = jnp.where(
        request_number[:, None] == request_of_slot[None, :], adapter_middle, 0.0
    ).astype(jnp.bfloat16)
    query_key_value = (
        plain_projection
        + adapter_scale * jnp.dot(adapter_middle, selected_up, preferred_element_type=jnp.float32)
    ).reshape(group_rows, heads_here, 3, HEAD_WIDTH)
    queries = (to_unit(rotate(query_key_value[:, :, 0, :], position)) * gain_qk).astype(
        jnp.bfloat16
    )
    key_own = (to_unit(rotate(query_key_value[:, :, 1, :], position)) * gain_qk).astype(
        jnp.bfloat16
    )
    value_own = query_key_value[:, :, 2, :].astype(jnp.bfloat16)
    page_list = prompt_page_table[request_prompt[0]].reshape(-1)
    picked = jnp.take(all_pages, page_list, axis=0).reshape(
        GROUP_REQUESTS * PREFIX_LEN, heads_here, 2, HEAD_WIDTH
    )
    key_all = jnp.concatenate([picked[:, :, 0, :], key_own], axis=0)
    value_all = jnp.concatenate([picked[:, :, 1, :], value_own], axis=0)
    key_request = jnp.concatenate(
        [jnp.arange(GROUP_REQUESTS * PREFIX_LEN, dtype=jnp.int32) // PREFIX_LEN, request_number],
        axis=0,
    )
    key_row = jnp.concatenate(
        [
            jnp.full((GROUP_REQUESTS * PREFIX_LEN,), -1, jnp.int32),
            jnp.arange(group_rows, dtype=jnp.int32),
        ],
        axis=0,
    )
    attn = attend(queries, key_all, value_all, request_number, key_request, key_row)
    attn_sum = lax.psum_scatter(
        jnp.dot(attn, output_matrix, preferred_element_type=jnp.float32).astype(jnp.bfloat16),
        "tensor",
        scatter_dimension=0,
        tiled=True,
    ).astype(jnp.float32)
    base_rows = hidden.astype(jnp.float32)
    mixed = renorm(base_rows + attention_rate * (renorm(attn_sum) - base_rows)).astype(jnp.bfloat16)
    unit_values = hidden_units(
        lax.all_gather(mixed, "tensor", axis=0, tiled=True),
        up_matrix,
        gate_matrix,
        up_scaling,
        gate_scaling,
    )
    mlp_sum = lax.psum_scatter(
        jnp.dot(unit_values, down_matrix, preferred_element_type=jnp.float32).astype(jnp.bfloat16),
        "tensor",
        scatter_dimension=0,
        tiled=True,
    ).astype(jnp.float32)
    mixed_rows = mixed.astype(jnp.float32)
    return renorm(mixed_rows + feedforward_rate * (renorm(mlp_sum) - mixed_rows)).astype(
        jnp.bfloat16
    )


CHIP_ROWS = 256
SCORE_LOG2 = math.sqrt(HEAD_WIDTH) / math.log(2.0)
VMEM = pl.BlockSpec(memory_space=pltpu.VMEM)
SMEM = pl.BlockSpec(memory_space=pltpu.SMEM)
BF16 = jnp.bfloat16
F32 = jnp.float32


def call(kernel, outs, operands, scalars, scratch=(), limit=12, flops=0, moved=0, far=()):
    count = len(operands)
    specs = [SMEM] * scalars + [VMEM] * (count - scalars)
    for place in far:
        specs[place] = pl.BlockSpec(memory_space=pltpu.HBM)
    buffers = [pltpu.VMEM(operands[place].shape, operands[place].dtype) for place in far]
    if far:
        buffers.append(pltpu.SemaphoreType.DMA((len(far),)))

    def whole(*refs):
        refs = list(refs)
        if far:
            *near, arrivals = refs[len(refs) - len(far) - 1 :]
            refs = refs[: len(refs) - len(far) - 1]
            copies = [
                pltpu.make_async_copy(refs[place], near[i], arrivals.at[i])
                for i, place in enumerate(far)
            ]
            for copy in copies:
                copy.start()
            for copy in copies:
                copy.wait()
            for i, place in enumerate(far):
                refs[place] = near[i]
        kernel(*refs)

    return pl.pallas_call(
        whole,
        out_shape=outs,
        in_specs=specs,
        out_specs=jax.tree.map(lambda _: VMEM, outs),
        scratch_shapes=[*scratch, *buffers],
        compiler_params=pltpu.CompilerParams(vmem_limit_bytes=limit * 1024 * 1024),
        cost_estimate=pl.CostEstimate(flops=flops, bytes_accessed=moved, transcendentals=0),
    )(*operands)


def shape(rows, columns, kind=BF16):
    return jax.ShapeDtypeStruct((rows, columns), kind)


def iota(dims, axis):
    return lax.broadcasted_iota(jnp.int32, dims, axis)


def first_head(rows):
    return iota((rows, 2 * HEAD_WIDTH), 1) < HEAD_WIDTH


def unit_heads(vectors, gain):
    low = first_head(vectors.shape[0])
    squares = vectors * vectors
    sum_low = jnp.sum(jnp.where(low, squares, 0.0), axis=-1, keepdims=True)
    sum_high = jnp.sum(jnp.where(low, 0.0, squares), axis=-1, keepdims=True)
    return vectors * lax.rsqrt(jnp.where(low, sum_low, sum_high) + epsilon) * gain


def dot(left, right):
    return jnp.dot(left, right, preferred_element_type=F32)


def dot_nt(left, right):
    return lax.dot_general(
        left, right, (((1,), (1,)), ((), ())), preferred_element_type=F32
    )


def prepare_kernel(ids, pages, up, down, gain, out):
    rows = pages.shape[0]
    low = first_head(rows)
    left = pages[:, 0:128].astype(F32)
    right = pages[:, 128:256].astype(F32)
    keys = jnp.where(low, left, pltpu.roll(right, HEAD_WIDTH, 1))
    values = jnp.where(low, pltpu.roll(left, HEAD_WIDTH, 1), right)
    out[0:256, 0:128] = unit_heads(keys, gain[...]).astype(BF16)
    out[0:256, 128:256] = values.astype(BF16)
    out[0:256, 256:640] = up[...]
    row, column = iota((128, 256), 0), iota((128, 256), 1)
    source = (row // 8) * ADAPTER_RANK + 8 * (ids[0] % 2) + row % 8
    picked = dot((column == source).astype(BF16), down[...]).astype(BF16)
    out[256:384, :] = picked[:, 0:640]
    out[384:512, :] = picked[:, 640:1280]


def by_request(index, scalars):
    picked = jnp.zeros_like(index)
    for request in range(GROUP_REQUESTS):
        picked = jnp.where(index == request, scalars[0, request], picked)
    return picked


def select_kernel(ids, adapters, g0, g1, g2, g3, g4, down_out, up_out):
    core, dp = ids[0] % 2, ids[1]
    row, column = iota((64, 128), 0), iota((64, 128), 1)
    adapter = by_request(row // 8, adapters)
    source = (adapter % 16) * 8 + row % 8
    owner = (adapter // 16) ^ dp
    up_row, up_column = iota((128, 256), 0), iota((128, 256), 1)
    up_adapter = by_request((up_row % 64) // 8, adapters)
    up_source = (up_adapter % 16) * 16 + 8 * ((up_row // 64) ^ core) + up_row % 8
    up_owner = (up_adapter // 16) ^ dp
    left = right = up_total = 0.0
    for m, g in enumerate((g0, g1, g2, g3)):
        lower, first = (g4, 0) if m == 3 else (g, 256)
        hot = ((column == source) & (owner == m)).astype(BF16)
        left = left + dot(hot, lower[first : first + 128, :])
        right = right + dot(hot, lower[first + 128 : first + 256, :])
        up_hot = ((up_column == up_source) & (up_owner == m)).astype(BF16)
        up_total = up_total + dot(up_hot, g[0:256, 256:640])
    down_out[:, 0:640] = left.astype(BF16)
    down_out[:, 640:1280] = right.astype(BF16)
    up_out[...] = up_total.astype(BF16)


def middle_chip(ids):
    chip = ids[0] // 2
    return (chip == 1) | (chip == 2)


def arrived(ids, parts):
    if len(parts) == 1:
        return parts[0][0:128, :]
    return jnp.where(middle_chip(ids), parts[0][0:128, :], parts[1][0:128, :])


def piece_spots(ids, j):
    core = ids[0] % 2
    base = ((ids[0] // 2) ^ j) * CHIP_ROWS
    return [pl.multiple_of(base + side * 128, 128) for side in (core, 1 - core)]


def row_pieces(ids, refs, js):
    pieces = []
    for j in js:
        count = 2 if j == 3 else 1
        pieces += [arrived(ids, refs[:count]), arrived(ids, refs[count : 2 * count])]
        refs = refs[2 * count :]
    return pieces, refs


def request_starts(lengths):
    begins = [jnp.int32(0)]
    for i in range(GROUP_REQUESTS):
        begins.append(begins[-1] + lengths[0, i])
    return begins


def project(j, ids, begins, pieces, weight, down, down_other, up, cosines, sines, gain):
    rows = jnp.concatenate(pieces, axis=0)
    count = rows.shape[0]
    row = jnp.concatenate([spot + iota((128, 128), 0) for spot in piece_spots(ids, j)], axis=0)
    request = (iota((1, 128), 1) % 64) // 8
    first, end = jnp.zeros_like(request), jnp.zeros_like(request)
    for i in range(GROUP_REQUESTS):
        first = jnp.where(request == i, begins[i], first)
        end = jnp.where(request == i, begins[i + 1], end)
    middle = dot_nt(rows, jnp.concatenate([down[...], down_other[...]], axis=0))
    middle = jnp.where((row >= first) & (row < end), middle, 0.0).astype(BF16)
    total = dot(rows, weight[...]) + adapter_scale * dot(middle, up[...])
    part0, part1, part2 = total[:, 0:128], total[:, 128:256], total[:, 256:384]
    low = first_head(count)
    query = jnp.where(low, part0, part1)
    key = pltpu.roll(jnp.where(low, part2, part0), HEAD_WIDTH, 1)
    value = jnp.where(low, part1, part2).astype(BF16)
    cosine = jnp.concatenate([cosines[pl.ds(spot, 128), :] for spot in piece_spots(ids, j)], axis=0)
    sine = jnp.concatenate([sines[pl.ds(spot, 128), :] for spot in piece_spots(ids, j)], axis=0)
    half = HEAD_WIDTH // 2
    head_low = (iota((count, 128), 1) % HEAD_WIDTH) < half

    def finish(x):
        turned = jnp.where(head_low, pltpu.roll(x, 128 - half, 1), pltpu.roll(x, half, 1))
        return unit_heads(x * cosine + turned * sine, gain[...]).astype(BF16)

    return finish(query), finish(key), value


def attend_kernel(ids, lengths, prompts, table, *refs):
    pieces, refs = row_pieces(ids, refs, range(4))
    *constants, g0, g1, g2, g3, out, queries, keys, values, pages, starts = refs
    begins = request_starts(lengths)
    for i, begin in enumerate(begins):
        starts[i] = begin
    for j in range(4):
        parts = project(j, ids, begins, pieces[2 * j : 2 * j + 2], *constants)
        for part, target in zip(parts, (queries, keys, values)):
            for side, spot in enumerate(piece_spots(ids, j)):
                target[pl.ds(spot, 128), :] = part[side * 128 : side * 128 + 128]
    for m, g in enumerate((g0, g1, g2, g3)):
        pages[pl.ds(pl.multiple_of((ids[1] ^ m) * 256, 256), 256), :] = g[0:256, 0:256]
    low = first_head(128)
    tile_row = iota((256, 1), 0) % 128

    def one_tile(tile, carry):
        base = pl.multiple_of(tile * 128, 128)
        query = queries[pl.ds(base, 128), :]
        zero = jnp.zeros_like(query)
        both = jnp.concatenate(
            [jnp.where(low, query, zero), jnp.where(low, zero, query)], axis=0
        )
        row = base + tile_row
        row_start = jnp.zeros_like(row)
        first = jnp.int32(0)
        last = jnp.int32(0)
        for i in range(1, GROUP_REQUESTS):
            row_start = jnp.where(row >= begins[i], begins[i], row_start)
            first = first + (begins[i] <= base).astype(jnp.int32)
            last = last + (begins[i] <= base + 127).astype(jnp.int32)

        def add(state, key, value, mask):
            total, norm = state
            weights = jnp.where(mask, jnp.exp2(dot_nt(both, key) * SCORE_LOG2), 0.0)
            return (
                total + dot(weights.astype(BF16), value),
                norm + jnp.sum(weights, axis=-1, keepdims=True),
            )

        def own_block(block, state):
            spot = pl.multiple_of(block * 128, 128)
            column = spot + iota((256, 128), 1)
            mask = (column >= row_start) & (column <= row)
            return add(state, keys[pl.ds(spot, 128), :], values[pl.ds(spot, 128), :], mask)

        def prefix(request, state):
            prompt = prompts[0, request]
            spots = [pl.multiple_of(table[prompt, p] * PAGE, PAGE) for p in range(4)]
            key = jnp.concatenate([pages[pl.ds(s, PAGE), 0:128] for s in spots], axis=0)
            value = jnp.concatenate([pages[pl.ds(s, PAGE), 128:256] for s in spots], axis=0)
            mask = (row >= starts[request]) & (row < starts[request + 1])
            return add(state, key, value, jnp.broadcast_to(mask, (256, PREFIX_LEN)))

        state = (jnp.zeros((256, 128), F32), jnp.zeros((256, 1), F32))
        state = prefix(first, state)
        state = own_block(tile, state)
        state = lax.fori_loop(starts[first] // 128, tile, own_block, state)
        total, norm = lax.fori_loop(first + 1, last + 1, prefix, state)
        total = total / norm
        out[pl.ds(base, 128), :] = jnp.where(low, total[0:128], total[128:256]).astype(BF16)
        return carry

    lax.fori_loop(0, out.shape[0] // 128, one_tile, 0)


def collect_kernel(ids, o0, o1, o2, o3, out):
    for m, part in enumerate((o0, o1, o2, o3)):
        spot = pl.multiple_of((ids[1] ^ m) * 32, 32)
        for j in range(4):
            out[j, pl.ds(spot, 32), :] = part[j]


def mlp_kernel(js, ids, *refs):
    heads_in, refs = refs[:10], refs[10:]
    pieces, refs = row_pieces(ids, refs, js)
    output, output_other, rate, up, gate, up_scale, gate_scale, down, keep, send, *rest = refs
    middle = middle_chip(ids)
    for place, j in enumerate(js):
        spots = piece_spots(ids, j)

        def rows_of(heads):
            return jnp.concatenate([heads[pl.ds(spot, 128), :] for spot in spots], axis=0)

        attn_sum = 0.0
        for side, matrix in enumerate((output, output_other)):
            columns = [rows_of(heads_in[2 * distance + side]) for distance in range(4)]
            columns[3] = jnp.where(middle, columns[3], rows_of(heads_in[8 + side]))
            attn_sum = attn_sum + dot(jnp.concatenate(columns, axis=1), matrix[...])
        base = jnp.concatenate(pieces[2 * place : 2 * place + 2], axis=0).astype(F32)
        mixed = renorm(base + rate[...] * (renorm(attn_sum) - base)).astype(BF16)
        up_part = dot(mixed, up[...]) * up_scale[...]
        gate_part = dot(mixed, gate[...]) * gate_scale[...]
        unit_values = (up_part * (gate_part / (1.0 + jnp.exp(-gate_part)))).astype(BF16)
        result = dot(unit_values, down[...]).astype(BF16)
        keep[place * 128 : place * 128 + 128, :] = result[0:128]
        send[place * 128 : place * 128 + 128, :] = result[128:256]
        if j == 0:
            rest[0][...] = mixed[0:128]


def add_kernel(keep, inward, out):
    out[...] = keep[0:128, :].astype(F32) + inward[...].astype(F32)


def final_kernel(mixed, keep, got, r1, r2, r3, rate, out):
    mlp_sum = keep[256:384, :].astype(F32) + got[256:384, :].astype(F32)
    for r in (r1, r2, r3):
        mlp_sum = mlp_sum + r[...].astype(F32)
    base = mixed[...].astype(F32)
    out[...] = renorm(base + rate[...] * (renorm(mlp_sum) - base)).astype(BF16)


def swap(values, distance, axis="tensor"):
    size = lax.axis_size(axis)
    return lax.ppermute(values, axis, [(i, i ^ distance) for i in range(size)])


def chips(values, pairs):
    return lax.ppermute(
        values, "tensor", [(2 * a + core, 2 * b + core) for a, b in pairs for core in (0, 1)]
    )


MIDDLE = ((1, 2), (2, 1))
OUTWARD = ((1, 0), (2, 3))
INWARD = ((0, 1), (3, 2))


def local_pairwise(
    hidden,
    lengths,
    request_prompt,
    request_adapter,
    prompt_page_table,
    prefix_page_cache,
    query_key_value_weight,
    adapter_down,
    adapter_up,
    attention_scale,
    output_matrix,
    attention_rate,
    up_matrix,
    gate_matrix,
    up_scaling,
    gate_scaling,
    down_matrix,
    feedforward_rate,
):
    group_rows = hidden.shape[0] * lax.axis_size("tensor")
    tensor, dp = lax.axis_index("tensor"), lax.axis_index("dp")
    ids = jnp.stack([tensor, dp]).astype(jnp.int32)
    gain = attention_scale.reshape(1, -1)

    row_ids = jnp.arange(group_rows, dtype=jnp.int32)
    starts = jnp.cumsum(lengths[0]) - lengths[0]
    row_start = jnp.max(
        jnp.where(row_ids[:, None] >= starts[None, :], starts[None, :], 0), axis=1
    )
    position = (row_ids - row_start).astype(F32) + PREFIX_LEN
    half = HEAD_WIDTH // 2
    lanes = jnp.arange(2 * HEAD_WIDTH, dtype=jnp.int32) % HEAD_WIDTH
    frequency = jnp.exp((lanes % half).astype(F32) * (-2.0 * math.log(10000.0) / HEAD_WIDTH))
    angles = position[:, None] * frequency[None, :]
    cosines = jnp.cos(angles)
    sines = jnp.where(lanes[None, :] < half, -1.0, 1.0) * jnp.sin(angles)

    quarter = output_matrix.shape[0] // 4
    own_quarter = lax.dynamic_slice_in_dim(output_matrix, dp * quarter, quarter, 0)
    payload = jnp.concatenate([hidden, own_quarter], axis=0)
    far2, far1 = swap(payload, 4), swap(payload, 2)
    forwarded3, direct3 = chips(far2, OUTWARD), chips(payload, MIDDLE)

    prepared = call(
        prepare_kernel,
        shape(512, 640),
        (
            ids,
            prefix_page_cache.reshape(-1, prefix_page_cache.shape[2]),
            adapter_up.reshape(-1, adapter_up.shape[2]),
            jnp.swapaxes(adapter_down, 1, 2).reshape(-1, MODEL_WIDTH),
            gain,
        ),
        1,
        far=(1, 2, 3),
        limit=62,
    )
    near1, near2 = swap(prepared, 1, "dp"), swap(prepared, 2, "dp")
    upper3, lower3 = swap(near2[0:256], 1, "dp"), swap(near1[256:512], 2, "dp")
    shared = [prepared, near1, near2, upper3]
    down_own, up_all = call(
        select_kernel,
        (shape(64, MODEL_WIDTH), shape(128, 384)),
        (ids, request_adapter, *shared, lower3),
        2,
        flops=0,
        moved=0,
    )
    down_other = swap(down_own, 1)

    rows = {0: [payload, swap(payload, 1)]}
    rows[1] = [far1, swap(far1, 1)]
    rows[2] = [far2, swap(far2, 1)]
    constants = (query_key_value_weight, down_own, down_other, up_all, cosines, sines, gain)
    rows[3] = [direct3, forwarded3, swap(direct3, 1), swap(forwarded3, 1)]

    chip = tensor // 2
    last = jnp.where((chip == 1) | (chip == 2), direct3[128:], forwarded3[128:])
    quarters = jnp.stack([payload[128:], far1[128:], far2[128:], last])
    outputs = [quarters] + [swap(quarters, m, "dp") for m in (1, 2, 3)]

    attn = call(
        attend_kernel,
        shape(group_rows, 128),
        (
            ids, lengths, request_prompt, prompt_page_table,
            *rows[0], *rows[1], *rows[2], *rows[3], *constants, *shared,
        ),
        4,
        scratch=(
            pltpu.VMEM((group_rows, 128), BF16),
            pltpu.VMEM((group_rows, 128), BF16),
            pltpu.VMEM((group_rows, 128), BF16),
            pltpu.VMEM((1024, 256), BF16),
            pltpu.SMEM((GROUP_REQUESTS + 1,), jnp.int32),
        ),
        flops=2 * 10**10,
        moved=2 * 10**6,
        limit=24,
    )

    attn, *outputs = lax.optimization_barrier((attn, *outputs))
    heads2 = swap(attn, 4)
    heads1 = swap(attn, 2)
    heads3, heads3f = chips(attn, MIDDLE), chips(heads2, OUTWARD)
    all_heads = [attn, swap(attn, 1), heads1, swap(heads1, 1), heads2, swap(heads2, 1)]
    all_heads += [heads3, swap(heads3, 1), heads3f, swap(heads3f, 1)]

    output_own = call(
        collect_kernel,
        jax.ShapeDtypeStruct((4, 4 * quarter, MODEL_WIDTH), BF16),
        (ids, *outputs),
        1,
        flops=0,
        moved=0,
    ).reshape(-1, MODEL_WIDTH)
    weights = (
        output_own, swap(output_own, 1), attention_rate.reshape(1, -1), up_matrix, gate_matrix,
        up_scaling.reshape(1, -1), gate_scaling.reshape(1, -1), down_matrix,
    )
    results = {}
    for js in ((3,), (2, 1, 0)):
        results[js] = call(
            functools.partial(mlp_kernel, js),
            (shape(128 * len(js), MODEL_WIDTH),) * 2 + (shape(128, MODEL_WIDTH),) * (0 in js),
            (ids, *all_heads, *[piece for j in js for piece in rows[j]], *weights),
            1,
            limit=24,
            flops=2 * 10**10,
            moved=10**7,
        )
    keep3, send3 = results[(3,)]
    keep, send, mixed = results[(2, 1, 0)]
    got = swap(send, 1)

    def chunk(kept, swapped):
        return (kept.astype(F32) + swapped.astype(F32)).astype(BF16)

    chunk3 = chunk(keep3, swap(send3, 1))
    inward = chips(chunk3, INWARD)
    received3 = chips(chunk3, MIDDLE)
    received1 = swap(chunk(keep[128:256], got[128:256]), 2)
    joined = call(add_kernel, shape(128, MODEL_WIDTH, F32), (keep, inward), 0, flops=2 * 10**10)
    received2 = swap(chunk(joined, got[0:128]), 4)
    return call(
        final_kernel,
        shape(*hidden.shape),
        (mixed, keep, got, received1, received2, received3, feedforward_rate.reshape(1, -1)),
        0,
    )


def solution(mesh):
    placed = (
        P(("dp", "tensor"), None),
        P("dp", None),
        P("dp", None),
        P("dp", None),
        P(),
        P("dp", None, "tensor"),
        P(None, "tensor"),
        P("dp", None, None),
        P("dp", None, "tensor"),
        P("tensor"),
        P("tensor", None),
        P(),
        P(None, "tensor"),
        P(None, "tensor"),
        P("tensor"),
        P("tensor"),
        P("tensor", None),
        P(),
    )
    pairwise = mesh.shape["dp"] == 4 and mesh.shape["tensor"] == 8
    return jax.shard_map(
        local_pairwise if pairwise else local_generic, mesh=mesh, in_specs=placed, out_specs=P(("dp", "tensor"), None), check_vma=False
    )
```

```python
import functools
import math

import jax
import jax.numpy as jnp
from jax import lax
from jax.experimental import pallas as pl
from jax.experimental.pallas import tpu as pltpu
from jax.sharding import PartitionSpec as P

MODEL_WIDTH = 1280
HEAD_WIDTH = 64
ADAPTER_RANK = 16
GROUP_REQUESTS = 8
PAGE = 64
PREFIX_LEN = 256


adapter_scale = 0.5
epsilon = 1e-06


def renorm(matrix):
    return matrix * lax.rsqrt(jnp.mean(matrix * matrix, axis=-1, keepdims=True) + epsilon)


def to_unit(vectors):
    return vectors * lax.rsqrt(jnp.sum(vectors * vectors, axis=-1, keepdims=True) + epsilon)


def rotate(vectors, position):
    half_size = vectors.shape[-1] // 2
    frequency = jnp.exp(
        jnp.arange(half_size).astype(jnp.float32) * (-2.0 * math.log(10000.0) / vectors.shape[-1])
    )
    angles = position[:, None] * frequency[None, :]
    cosine = jnp.cos(angles)[:, None, :]
    sines = jnp.sin(angles)[:, None, :]
    first_half = vectors[..., :half_size]
    second_half = vectors[..., half_size:]
    return jnp.concatenate(
        [first_half * cosine - second_half * sines, first_half * sines + second_half * cosine],
        axis=-1,
    )


def layout(counts, total_rows):
    row_ends = jnp.cumsum(counts)
    starts = row_ends - counts
    row_ids = jnp.arange(total_rows, dtype=jnp.int32)
    request_number = jnp.sum((row_ids[:, None] >= row_ends[None, :]).astype(jnp.int32), axis=1)
    selected_adapter = (
        request_number[:, None] == jnp.arange(counts.shape[0], dtype=jnp.int32)[None, :]
    )
    offset = row_ids - jnp.sum(jnp.where(selected_adapter, starts[None, :], 0), axis=1)
    return (request_number, offset)


def attend(queries, key_all, value_all, request_number, key_request, key_row):
    rows_total = queries.shape[0]
    block_rows = min(512, rows_total)
    score_scale = math.sqrt(queries.shape[-1])
    row_ids = jnp.arange(rows_total, dtype=jnp.int32)

    def one_block(block_index):
        first_row = block_index * block_rows
        query_block = lax.dynamic_slice_in_dim(queries, first_row, block_rows, 0)
        request_block = lax.dynamic_slice_in_dim(request_number, first_row, block_rows, 0)
        row_block = lax.dynamic_slice_in_dim(row_ids, first_row, block_rows, 0)
        scores = (
            jnp.einsum("qhd,khd->hqk", query_block, key_all, preferred_element_type=jnp.float32)
            * score_scale
        )
        allowed = (request_block[:, None] == key_request[None, :]) & (
            key_row[None, :] <= row_block[:, None]
        )
        exp_scores = jnp.where(allowed[None], jnp.exp(scores), 0.0)
        weights = (exp_scores / jnp.sum(exp_scores, axis=-1, keepdims=True)).astype(jnp.bfloat16)
        mixed_block = jnp.einsum(
            "hqk,khd->qhd", weights, value_all, preferred_element_type=jnp.float32
        )
        return mixed_block.reshape(block_rows, -1).astype(jnp.bfloat16)

    blocks = lax.map(one_block, jnp.arange(rows_total // block_rows, dtype=jnp.int32))
    return blocks.reshape(rows_total, -1)


def hidden_units(row_values, up_matrix, gate_matrix, up_scaling, gate_scaling):
    up_part = jnp.dot(row_values, up_matrix, preferred_element_type=jnp.float32) * up_scaling
    gate_part = jnp.dot(row_values, gate_matrix, preferred_element_type=jnp.float32) * gate_scaling
    return (up_part * jax.nn.silu(gate_part)).astype(jnp.bfloat16)


def local_generic(
    hidden,
    lengths,
    request_prompt,
    request_adapter,
    prompt_page_table,
    prefix_page_cache,
    query_key_value_weight,
    adapter_down,
    adapter_up,
    attention_scale,
    output_matrix,
    attention_rate,
    up_matrix,
    gate_matrix,
    up_scaling,
    gate_scaling,
    down_matrix,
    feedforward_rate,
):
    tok_rows = hidden.shape[0]
    group_rows = tok_rows * lax.axis_size("tensor")
    heads_here = query_key_value_weight.shape[1] // (3 * HEAD_WIDTH)
    gain_qk = attention_scale.reshape(heads_here, HEAD_WIDTH)
    request_number, offset = layout(lengths[0], group_rows)
    position = offset.astype(jnp.float32) + PREFIX_LEN
    local_cache = prefix_page_cache.reshape(
        prefix_page_cache.shape[0], PAGE, heads_here, 2, HEAD_WIDTH
    )
    local_keys = (to_unit(local_cache[:, :, :, 0, :].astype(jnp.float32)) * gain_qk).astype(
        jnp.bfloat16
    )
    prepared = jnp.stack([local_keys, local_cache[:, :, :, 1, :]], axis=3).reshape(
        prefix_page_cache.shape
    )
    all_pages = lax.all_gather(prepared, "dp", axis=0, tiled=True)
    down_all, up_all = (
        lax.all_gather(adapter_down, "dp", axis=0, tiled=True),
        lax.all_gather(adapter_up, "dp", axis=0, tiled=True),
    )
    every_row = lax.all_gather(hidden, "tensor", axis=0, tiled=True)
    adapter_count = down_all.shape[0]
    onehot = (
        request_adapter[0][:, None] == jnp.arange(adapter_count, dtype=jnp.int32)[None, :]
    ).astype(jnp.bfloat16)
    selected_down = jnp.dot(
        onehot, down_all.reshape(adapter_count, -1), preferred_element_type=jnp.float32
    ).astype(jnp.bfloat16)
    selected_down = jnp.transpose(
        selected_down.reshape(GROUP_REQUESTS, MODEL_WIDTH, ADAPTER_RANK), (1, 0, 2)
    ).reshape(MODEL_WIDTH, GROUP_REQUESTS * ADAPTER_RANK)
    selected_up = jnp.dot(
        onehot, up_all.reshape(adapter_count, -1), preferred_element_type=jnp.float32
    ).astype(jnp.bfloat16)
    selected_up = selected_up.reshape(GROUP_REQUESTS * ADAPTER_RANK, heads_here * 3 * HEAD_WIDTH)
    request_of_slot = jnp.arange(GROUP_REQUESTS * ADAPTER_RANK, dtype=jnp.int32) // ADAPTER_RANK
    plain_projection = jnp.dot(
        every_row, query_key_value_weight, preferred_element_type=jnp.float32
    )
    adapter_middle = jnp.dot(every_row, selected_down, preferred_element_type=jnp.float32)
    adapter_middle = jnp.where(
        request_number[:, None] == request_of_slot[None, :], adapter_middle, 0.0
    ).astype(jnp.bfloat16)
    query_key_value = (
        plain_projection
        + adapter_scale * jnp.dot(adapter_middle, selected_up, preferred_element_type=jnp.float32)
    ).reshape(group_rows, heads_here, 3, HEAD_WIDTH)
    queries = (to_unit(rotate(query_key_value[:, :, 0, :], position)) * gain_qk).astype(
        jnp.bfloat16
    )
    key_own = (to_unit(rotate(query_key_value[:, :, 1, :], position)) * gain_qk).astype(
        jnp.bfloat16
    )
    value_own = query_key_value[:, :, 2, :].astype(jnp.bfloat16)
    page_list = prompt_page_table[request_prompt[0]].reshape(-1)
    picked = jnp.take(all_pages, page_list, axis=0).reshape(
        GROUP_REQUESTS * PREFIX_LEN, heads_here, 2, HEAD_WIDTH
    )
    key_all = jnp.concatenate([picked[:, :, 0, :], key_own], axis=0)
    value_all = jnp.concatenate([picked[:, :, 1, :], value_own], axis=0)
    key_request = jnp.concatenate(
        [jnp.arange(GROUP_REQUESTS * PREFIX_LEN, dtype=jnp.int32) // PREFIX_LEN, request_number],
        axis=0,
    )
    key_row = jnp.concatenate(
        [
            jnp.full((GROUP_REQUESTS * PREFIX_LEN,), -1, jnp.int32),
            jnp.arange(group_rows, dtype=jnp.int32),
        ],
        axis=0,
    )
    attn = attend(queries, key_all, value_all, request_number, key_request, key_row)
    attn_sum = lax.psum_scatter(
        jnp.dot(attn, output_matrix, preferred_element_type=jnp.float32).astype(jnp.bfloat16),
        "tensor",
        scatter_dimension=0,
        tiled=True,
    ).astype(jnp.float32)
    base_rows = hidden.astype(jnp.float32)
    mixed = renorm(base_rows + attention_rate * (renorm(attn_sum) - base_rows)).astype(jnp.bfloat16)
    unit_values = hidden_units(
        lax.all_gather(mixed, "tensor", axis=0, tiled=True),
        up_matrix,
        gate_matrix,
        up_scaling,
        gate_scaling,
    )
    mlp_sum = lax.psum_scatter(
        jnp.dot(unit_values, down_matrix, preferred_element_type=jnp.float32).astype(jnp.bfloat16),
        "tensor",
        scatter_dimension=0,
        tiled=True,
    ).astype(jnp.float32)
    mixed_rows = mixed.astype(jnp.float32)
    return renorm(mixed_rows + feedforward_rate * (renorm(mlp_sum) - mixed_rows)).astype(
        jnp.bfloat16
    )


CHIP_ROWS = 256
SCORE_LOG2 = math.sqrt(HEAD_WIDTH) / math.log(2.0)
VMEM = pl.BlockSpec(memory_space=pltpu.VMEM)
SMEM = pl.BlockSpec(memory_space=pltpu.SMEM)
BF16 = jnp.bfloat16
F32 = jnp.float32


def call(kernel, outs, operands, scalars, scratch=(), limit=12, flops=0, moved=0, far=(), unread=()):
    count = len(operands)
    specs = [SMEM] * scalars + [VMEM] * (count - scalars)
    for place in far:
        specs[place] = pl.BlockSpec(memory_space=pltpu.HBM)
    for place in unread:
        specs[place] = pl.BlockSpec(memory_space=pl.ANY)
    buffers = [pltpu.VMEM(operands[place].shape, operands[place].dtype) for place in far]
    if far:
        buffers.append(pltpu.SemaphoreType.DMA((len(far),)))

    def whole(*refs):
        refs = list(refs)
        if far:
            *near, arrivals = refs[len(refs) - len(far) - 1 :]
            refs = refs[: len(refs) - len(far) - 1]
            copies = [
                pltpu.make_async_copy(refs[place], near[i], arrivals.at[i])
                for i, place in enumerate(far)
            ]
            for copy in copies:
                copy.start()
            for copy in copies:
                copy.wait()
            for i, place in enumerate(far):
                refs[place] = near[i]
        kernel(*refs)

    return pl.pallas_call(
        whole,
        out_shape=outs,
        in_specs=specs,
        out_specs=jax.tree.map(lambda _: VMEM, outs),
        scratch_shapes=[*scratch, *buffers],
        compiler_params=pltpu.CompilerParams(vmem_limit_bytes=limit * 1024 * 1024),
        cost_estimate=pl.CostEstimate(flops=flops, bytes_accessed=moved, transcendentals=0),
    )(*operands)


def shape(rows, columns, kind=BF16):
    return jax.ShapeDtypeStruct((rows, columns), kind)


def iota(dims, axis):
    return lax.broadcasted_iota(jnp.int32, dims, axis)


def first_head(rows):
    return iota((rows, 2 * HEAD_WIDTH), 1) < HEAD_WIDTH


def unit_heads(vectors, gain):
    low = first_head(vectors.shape[0])
    squares = vectors * vectors
    sum_low = jnp.sum(jnp.where(low, squares, 0.0), axis=-1, keepdims=True)
    sum_high = jnp.sum(jnp.where(low, 0.0, squares), axis=-1, keepdims=True)
    return vectors * lax.rsqrt(jnp.where(low, sum_low, sum_high) + epsilon) * gain


def dot(left, right):
    return jnp.dot(left, right, preferred_element_type=F32)


def dot_nt(left, right):
    return lax.dot_general(
        left, right, (((1,), (1,)), ((), ())), preferred_element_type=F32
    )


def prepare_kernel(ids, pages, up, down, gain, out):
    rows = pages.shape[0]
    low = first_head(rows)
    left = pages[:, 0:128].astype(F32)
    right = pages[:, 128:256].astype(F32)
    keys = jnp.where(low, left, pltpu.roll(right, HEAD_WIDTH, 1))
    values = jnp.where(low, pltpu.roll(left, HEAD_WIDTH, 1), right)
    out[0:256, 0:128] = unit_heads(keys, gain[...]).astype(BF16)
    out[0:256, 128:256] = values.astype(BF16)
    out[0:256, 256:640] = up[...]
    row, column = iota((128, 256), 0), iota((128, 256), 1)
    source = (row // 8) * ADAPTER_RANK + 8 * (ids[0] % 2) + row % 8
    picked = dot((column == source).astype(BF16), down[...]).astype(BF16)
    out[256:384, :] = picked[:, 0:640]
    out[384:512, :] = picked[:, 640:1280]


def by_request(index, scalars):
    picked = jnp.zeros_like(index)
    for request in range(GROUP_REQUESTS):
        picked = jnp.where(index == request, scalars[0, request], picked)
    return picked


def select_kernel(ids, adapters, g0, g1, g2, g3, g4, down_out, up_out):
    core, dp = ids[0] % 2, ids[1]
    row, column = iota((64, 128), 0), iota((64, 128), 1)
    adapter = by_request(row // 8, adapters)
    source = (adapter % 16) * 8 + row % 8
    owner = (adapter // 16) ^ dp
    up_row, up_column = iota((128, 256), 0), iota((128, 256), 1)
    up_adapter = by_request((up_row % 64) // 8, adapters)
    up_source = (up_adapter % 16) * 16 + 8 * ((up_row // 64) ^ core) + up_row % 8
    up_owner = (up_adapter // 16) ^ dp
    left = right = up_total = 0.0
    for m, g in enumerate((g0, g1, g2, g3)):
        lower, first = (g4, 0) if m == 3 else (g, 256)
        hot = ((column == source) & (owner == m)).astype(BF16)
        left = left + dot(hot, lower[first : first + 128, :])
        right = right + dot(hot, lower[first + 128 : first + 256, :])
        up_hot = ((up_column == up_source) & (up_owner == m)).astype(BF16)
        up_total = up_total + dot(up_hot, g[0:256, 256:640])
    down_out[:, 0:640] = left.astype(BF16)
    down_out[:, 640:1280] = right.astype(BF16)
    up_out[...] = up_total.astype(BF16)


def middle_chip(ids):
    chip = ids[0] // 2
    return (chip == 1) | (chip == 2)


def arrived(ids, parts):
    if len(parts) == 1:
        return parts[0][0:128, :]
    return jnp.where(middle_chip(ids), parts[0][0:128, :], parts[1][0:128, :])


def piece_spots(ids, j):
    core = ids[0] % 2
    base = ((ids[0] // 2) ^ j) * CHIP_ROWS
    return [pl.multiple_of(base + side * 128, 128) for side in (core, 1 - core)]


def row_pieces(ids, refs, js):
    pieces = []
    for j in js:
        count = 2 if j == 3 else 1
        pieces += [arrived(ids, refs[:count]), arrived(ids, refs[count : 2 * count])]
        refs = refs[2 * count :]
    return pieces, refs


def request_starts(lengths):
    begins = [jnp.int32(0)]
    for i in range(GROUP_REQUESTS):
        begins.append(begins[-1] + lengths[0, i])
    return begins


def project(j, ids, begins, pieces, weight, down, down_other, up, cosines, sines, gain):
    rows = jnp.concatenate(pieces, axis=0)
    count = rows.shape[0]
    row = jnp.concatenate([spot + iota((128, 128), 0) for spot in piece_spots(ids, j)], axis=0)
    request = (iota((1, 128), 1) % 64) // 8
    first, end = jnp.zeros_like(request), jnp.zeros_like(request)
    for i in range(GROUP_REQUESTS):
        first = jnp.where(request == i, begins[i], first)
        end = jnp.where(request == i, begins[i + 1], end)
    middle = dot_nt(rows, jnp.concatenate([down[...], down_other[...]], axis=0))
    middle = jnp.where((row >= first) & (row < end), middle, 0.0).astype(BF16)
    total = dot(rows, weight[...]) + adapter_scale * dot(middle, up[...])
    part0, part1, part2 = total[:, 0:128], total[:, 128:256], total[:, 256:384]
    low = first_head(count)
    query = jnp.where(low, part0, part1)
    key = pltpu.roll(jnp.where(low, part2, part0), HEAD_WIDTH, 1)
    value = jnp.where(low, part1, part2).astype(BF16)
    cosine = jnp.concatenate([cosines[pl.ds(spot, 128), :] for spot in piece_spots(ids, j)], axis=0)
    sine = jnp.concatenate([sines[pl.ds(spot, 128), :] for spot in piece_spots(ids, j)], axis=0)
    half = HEAD_WIDTH // 2
    head_low = (iota((count, 128), 1) % HEAD_WIDTH) < half

    def finish(x):
        turned = jnp.where(head_low, pltpu.roll(x, 128 - half, 1), pltpu.roll(x, half, 1))
        return unit_heads(x * cosine + turned * sine, gain[...]).astype(BF16)

    return finish(query), finish(key), value


def attend_kernel(ids, lengths, prompts, table, *refs):
    pieces, refs = row_pieces(ids, refs, range(4))
    *constants, g0, g1, g2, g3, out, queries, keys, values, pages, starts, sums = refs
    begins = request_starts(lengths)
    for i, begin in enumerate(begins):
        starts[i] = begin
    for j in range(4):
        parts = project(j, ids, begins, pieces[2 * j : 2 * j + 2], *constants)
        for part, target in zip(parts, (queries, keys, values)):
            for side, spot in enumerate(piece_spots(ids, j)):
                target[pl.ds(spot, 128), :] = part[side * 128 : side * 128 + 128]
    for m, g in enumerate((g0, g1, g2, g3)):
        pages[pl.ds(pl.multiple_of((ids[1] ^ m) * 256, 256), 256), :] = g[0:256, 0:256]
    tiles = out.shape[0] // 128
    low = first_head(128)
    low_keys = first_head(256)
    ones = jnp.ones((256, 128), BF16)

    def tile_queries(tile):
        query = queries[pl.ds(pl.multiple_of(tile * 128, 128), 128), :]
        zero = jnp.zeros_like(query)
        both = jnp.concatenate(
            [jnp.where(low, query, zero), jnp.where(low, zero, query)], axis=0
        )
        return both, tile * 128 + iota((256, 1), 0) % 128

    def prefix(request):
        prompt = prompts[0, request]
        spots = [pl.multiple_of(table[prompt, p] * PAGE, PAGE) for p in range(PREFIX_LEN // PAGE)]
        return (
            jnp.concatenate([pages[pl.ds(s, PAGE), 0:128] for s in spots], axis=0),
            jnp.concatenate([pages[pl.ds(s, PAGE), 128:256] for s in spots], axis=0),
        )

    def window(spot):
        spot = pl.multiple_of(spot, 128)
        return keys[pl.ds(spot, 256), :], values[pl.ds(spot, 256), :], spot + iota((256, 256), 1)

    def products(both, key, value, mask):
        weights = jnp.where(mask, jnp.exp2(dot_nt(both, key) * SCORE_LOG2), 0.0).astype(BF16)
        return (
            dot(weights[:128], jnp.where(low_keys, value, ones)),
            dot(weights[128:], jnp.where(low_keys, ones, value)),
        )

    firsts = []
    for tile in range(tiles):
        base = tile * 128
        both, row = tile_queries(tile)
        first = jnp.int32(0)
        row_start = jnp.zeros_like(row)
        for begin in begins[1:GROUP_REQUESTS]:
            row_start = jnp.where(row >= begin, begin, row_start)
            first = first + (begin <= base).astype(jnp.int32)
        firsts.append(first)
        mask = jnp.broadcast_to(row < starts[first + 1], (256, PREFIX_LEN))
        shared = products(both, *prefix(first), mask)
        key, value, column = window(max(base - 128, 0))
        own = products(both, key, value, (column >= row_start) & (column <= row))
        for head in (0, 1):
            sums[tile, head] = shared[head] + own[head]
    for i in range(1, GROUP_REQUESTS):
        begin, end = begins[i], begins[i + 1]
        tile = begin // 128
        both, row = tile_queries(tile)
        mask = (row >= begin) & (row < end) & (begin % 128 != 0)
        more = products(both, *prefix(i), jnp.broadcast_to(mask, (256, PREFIX_LEN)))
        for head in (0, 1):
            sums[tile, head] += more[head]
    for tile in range(2, tiles):
        base = tile * 128
        first = firsts[tile]
        begin, end = starts[first], starts[first + 1]

        def earlier(step, carry, tile=tile, base=base, begin=begin, end=end):
            both, row = tile_queries(tile)
            stop = base - 128 - 256 * step
            key, value, column = window(jnp.maximum(stop - 256, 0))
            mask = (column >= begin) & (column < stop) & (row < end)
            more = products(both, key, value, mask)
            for head in (0, 1):
                sums[tile, head] += more[head]
            return carry

        lax.fori_loop(0, jnp.maximum(base + 127 - begin, 0) // 256, earlier, 0)
    for tile in range(tiles):
        left, right = sums[tile, 0], sums[tile, 1]
        weight = pltpu.roll(jnp.where(low, right, left), HEAD_WIDTH, 1)
        out[tile * 128 : tile * 128 + 128, :] = (jnp.where(low, left, right) / weight).astype(BF16)


def collect_kernel(ids, o0, o1, o2, o3, out):
    for m, part in enumerate((o0, o1, o2, o3)):
        spot = pl.multiple_of((ids[1] ^ m) * 32, 32)
        for j in range(4):
            out[j, pl.ds(spot, 32), :] = part[j]


def mlp_kernel(js, ids, *refs):
    heads_in, refs = refs[:10], refs[10:]
    pieces, refs = row_pieces(ids, refs, js)
    output, output_other, rate, up, gate, up_scale, gate_scale, down, _, keep, send, *rest = refs
    direct = middle_chip(ids)
    for place, j in enumerate(js):
        spots = piece_spots(ids, j)

        def rows_of(heads):
            return jnp.concatenate([heads[pl.ds(spot, 128), :] for spot in spots], axis=0)

        attn_sum = 0.0
        for side, matrix in enumerate((output, output_other)):
            columns = [rows_of(heads_in[2 * distance + side]) for distance in range(4)]
            columns[3] = jnp.where(direct, columns[3], rows_of(heads_in[8 + side]))
            attn_sum = attn_sum + dot(jnp.concatenate(columns, axis=1), matrix[...])
        base = jnp.concatenate(pieces[2 * place : 2 * place + 2], axis=0).astype(F32)
        mixed = renorm(base + rate[...] * (renorm(attn_sum) - base)).astype(BF16)
        up_part = dot(mixed, up[...]) * up_scale[...]
        gate_part = dot(mixed, gate[...]) * gate_scale[...]
        unit_values = (up_part * (gate_part / (1.0 + jnp.exp(-gate_part)))).astype(BF16)
        result = dot(unit_values, down[...]).astype(BF16)
        keep[place * 128 : place * 128 + 128, :] = result[0:128]
        send[place * 128 : place * 128 + 128, :] = result[128:256]
        if j == 0:
            rest[0][...] = mixed[0:128]


def add_kernel(ids, keep, inward, direct, out):
    more = inward[...].astype(F32)
    out[...] = keep[0:128, :].astype(F32) + jnp.where(middle_chip(ids), more, 0.0)


def final_kernel(mixed, keep, got, r1, r2, r3, rate, out):
    mlp_sum = keep[...].astype(F32) + got[...].astype(F32)
    for r in (r1, r2, r3):
        mlp_sum = mlp_sum + r[...].astype(F32)
    base = mixed[...].astype(F32)
    out[...] = renorm(base + rate[...] * (renorm(mlp_sum) - base)).astype(BF16)


def swap(values, distance, axis="tensor"):
    size = lax.axis_size(axis)
    return lax.ppermute(values, axis, [(i, i ^ distance) for i in range(size)])


def middle(values):
    return lax.ppermute(values, "tensor", [(2, 4), (3, 5), (4, 2), (5, 3)])


def local_pairwise(
    hidden,
    lengths,
    request_prompt,
    request_adapter,
    prompt_page_table,
    prefix_page_cache,
    query_key_value_weight,
    adapter_down,
    adapter_up,
    attention_scale,
    output_matrix,
    attention_rate,
    up_matrix,
    gate_matrix,
    up_scaling,
    gate_scaling,
    down_matrix,
    feedforward_rate,
):
    group_rows = hidden.shape[0] * lax.axis_size("tensor")
    tensor, dp = lax.axis_index("tensor"), lax.axis_index("dp")
    ids = jnp.stack([tensor, dp]).astype(jnp.int32)
    gain = attention_scale.reshape(1, -1)

    row_ids = jnp.arange(group_rows, dtype=jnp.int32)
    starts = jnp.cumsum(lengths[0]) - lengths[0]
    row_start = jnp.max(
        jnp.where(row_ids[:, None] >= starts[None, :], starts[None, :], 0), axis=1
    )
    position = (row_ids - row_start).astype(F32) + PREFIX_LEN
    half = HEAD_WIDTH // 2
    lanes = jnp.arange(2 * HEAD_WIDTH, dtype=jnp.int32) % HEAD_WIDTH
    frequency = jnp.exp((lanes % half).astype(F32) * (-2.0 * math.log(10000.0) / HEAD_WIDTH))
    angles = position[:, None] * frequency[None, :]
    cosines = jnp.cos(angles)
    sines = jnp.where(lanes[None, :] < half, -1.0, 1.0) * jnp.sin(angles)

    quarter = output_matrix.shape[0] // 4
    own_quarter = lax.dynamic_slice_in_dim(output_matrix, dp * quarter, quarter, 0)
    payload = jnp.concatenate([hidden, own_quarter], axis=0)
    far2, far1 = swap(payload, 4), swap(payload, 2)
    forwarded3, direct3 = swap(far2, 2), middle(payload)

    prepared = call(
        prepare_kernel,
        shape(512, 640),
        (
            ids,
            prefix_page_cache.reshape(-1, prefix_page_cache.shape[2]),
            adapter_up.reshape(-1, adapter_up.shape[2]),
            jnp.swapaxes(adapter_down, 1, 2).reshape(-1, MODEL_WIDTH),
            gain,
        ),
        1,
        far=(1, 2, 3),
        limit=62,
    )
    near1, near2 = swap(prepared, 1, "dp"), swap(prepared, 2, "dp")
    upper3, lower3 = swap(near2[0:256], 1, "dp"), swap(near1[256:512], 2, "dp")
    shared = [prepared, near1, near2, upper3]
    down_own, up_all = call(
        select_kernel,
        (shape(64, MODEL_WIDTH), shape(128, 384)),
        (ids, request_adapter, *shared, lower3),
        2,
        flops=0,
        moved=0,
    )
    down_other = swap(down_own, 1)

    rows = {0: [payload, swap(payload, 1)]}
    rows[1] = [far1, swap(far1, 1)]
    rows[2] = [far2, swap(far2, 1)]
    constants = (query_key_value_weight, down_own, down_other, up_all, cosines, sines, gain)
    rows[3] = [direct3, forwarded3, swap(direct3, 1), swap(forwarded3, 1)]

    chip = tensor // 2
    last = jnp.where((chip == 1) | (chip == 2), direct3[128:], forwarded3[128:])
    quarters = jnp.stack([payload[128:], far1[128:], far2[128:], last])
    outputs = [quarters] + [swap(quarters, m, "dp") for m in (1, 2, 3)]

    attn = call(
        attend_kernel,
        shape(group_rows, 128),
        (
            ids, lengths, request_prompt, prompt_page_table,
            *rows[0], *rows[1], *rows[2], *rows[3], *constants, *shared,
        ),
        4,
        scratch=(
            pltpu.VMEM((group_rows, 128), BF16),
            pltpu.VMEM((group_rows, 128), BF16),
            pltpu.VMEM((group_rows, 128), BF16),
            pltpu.VMEM((1024, 256), BF16),
            pltpu.SMEM((GROUP_REQUESTS + 1,), jnp.int32),
            pltpu.VMEM((group_rows // 128, 2, 128, 128), F32),
        ),
        flops=2 * 10**10,
        moved=2 * 10**6,
        limit=24,
    )

    heads2 = swap(attn, 4)
    heads1 = swap(attn, 2)
    heads1, heads2, *outputs = lax.optimization_barrier((heads1, heads2, *outputs))
    heads3, heads3f = middle(attn), swap(heads2, 2)
    all_heads = [attn, swap(attn, 1), heads1, swap(heads1, 1), heads2, swap(heads2, 1)]
    all_heads += [heads3, swap(heads3, 1), heads3f, swap(heads3f, 1)]

    output_own = call(
        collect_kernel,
        jax.ShapeDtypeStruct((4, 4 * quarter, MODEL_WIDTH), BF16),
        (ids, *outputs),
        1,
        flops=0,
        moved=0,
    ).reshape(-1, MODEL_WIDTH)
    weights = (
        output_own, swap(output_own, 1), attention_rate.reshape(1, -1), up_matrix, gate_matrix,
        up_scaling.reshape(1, -1), gate_scaling.reshape(1, -1), down_matrix,
    )
    def update(js, previous):
        operands = (ids, *all_heads, *[piece for j in js for piece in rows[j]], *weights, previous)
        return call(
            functools.partial(mlp_kernel, js),
            (shape(128 * len(js), MODEL_WIDTH),) * 2 + (shape(128, MODEL_WIDTH),) * (0 in js),
            operands,
            1,
            limit=24,
            flops=2 * 10**10,
            moved=10**7,
            unread=(len(operands) - 1,),
        )

    def chunk(kept, swapped):
        return (kept.astype(F32) + swapped.astype(F32)).astype(BF16)

    keep3, send3 = update((3,), ids)
    chunk3 = chunk(keep3, swap(send3, 1))
    inward, received3 = swap(chunk3, 2), middle(chunk3)
    keep, send = update((2, 1), keep3)
    got = swap(send, 1)
    received1 = swap(chunk(keep[128:256], got[128:256]), 2)
    joined = call(
        add_kernel,
        shape(128, MODEL_WIDTH, F32),
        (ids, keep, inward, received3),
        1,
        flops=2 * 10**10,
        unread=(3,),
    )
    received2 = swap(chunk(joined, got[0:128]), 4)
    keep0, send0, mixed = update((0,), joined)
    return call(
        final_kernel,
        shape(*hidden.shape),
        (mixed, keep0, swap(send0, 1), received1, received2, received3, feedforward_rate.reshape(1, -1)),
        0,
    )


def solution(mesh):
    placed = (
        P(("dp", "tensor"), None),
        P("dp", None),
        P("dp", None),
        P("dp", None),
        P(),
        P("dp", None, "tensor"),
        P(None, "tensor"),
        P("dp", None, None),
        P("dp", None, "tensor"),
        P("tensor"),
        P("tensor", None),
        P(),
        P(None, "tensor"),
        P(None, "tensor"),
        P("tensor"),
        P("tensor"),
        P("tensor", None),
        P(),
    )
    pairwise = mesh.shape["dp"] == 4 and mesh.shape["tensor"] == 8
    return jax.shard_map(
        local_pairwise if pairwise else local_generic, mesh=mesh, in_specs=placed, out_specs=P(("dp", "tensor"), None), check_vma=False
    )
```

```python
import functools
import math

import jax
import jax.numpy as jnp
from jax import lax
from jax.experimental import pallas as pl
from jax.experimental.pallas import tpu as pltpu
from jax.sharding import PartitionSpec as P

MODEL_WIDTH = 1280
HEAD_WIDTH = 64
ADAPTER_RANK = 16
GROUP_REQUESTS = 8
PAGE = 64
PREFIX_LEN = 256


adapter_scale = 0.5
epsilon = 1e-06


def renorm(matrix):
    return matrix * lax.rsqrt(jnp.mean(matrix * matrix, axis=-1, keepdims=True) + epsilon)


def to_unit(vectors):
    return vectors * lax.rsqrt(jnp.sum(vectors * vectors, axis=-1, keepdims=True) + epsilon)


def rotate(vectors, position):
    half_size = vectors.shape[-1] // 2
    frequency = jnp.exp(
        jnp.arange(half_size).astype(jnp.float32) * (-2.0 * math.log(10000.0) / vectors.shape[-1])
    )
    angles = position[:, None] * frequency[None, :]
    cosine = jnp.cos(angles)[:, None, :]
    sines = jnp.sin(angles)[:, None, :]
    first_half = vectors[..., :half_size]
    second_half = vectors[..., half_size:]
    return jnp.concatenate(
        [first_half * cosine - second_half * sines, first_half * sines + second_half * cosine],
        axis=-1,
    )


def layout(counts, total_rows):
    row_ends = jnp.cumsum(counts)
    starts = row_ends - counts
    row_ids = jnp.arange(total_rows, dtype=jnp.int32)
    request_number = jnp.sum((row_ids[:, None] >= row_ends[None, :]).astype(jnp.int32), axis=1)
    selected_adapter = (
        request_number[:, None] == jnp.arange(counts.shape[0], dtype=jnp.int32)[None, :]
    )
    offset = row_ids - jnp.sum(jnp.where(selected_adapter, starts[None, :], 0), axis=1)
    return (request_number, offset)


def attend(queries, key_all, value_all, request_number, key_request, key_row):
    rows_total = queries.shape[0]
    block_rows = min(512, rows_total)
    score_scale = math.sqrt(queries.shape[-1])
    row_ids = jnp.arange(rows_total, dtype=jnp.int32)

    def one_block(block_index):
        first_row = block_index * block_rows
        query_block = lax.dynamic_slice_in_dim(queries, first_row, block_rows, 0)
        request_block = lax.dynamic_slice_in_dim(request_number, first_row, block_rows, 0)
        row_block = lax.dynamic_slice_in_dim(row_ids, first_row, block_rows, 0)
        scores = (
            jnp.einsum("qhd,khd->hqk", query_block, key_all, preferred_element_type=jnp.float32)
            * score_scale
        )
        allowed = (request_block[:, None] == key_request[None, :]) & (
            key_row[None, :] <= row_block[:, None]
        )
        exp_scores = jnp.where(allowed[None], jnp.exp(scores), 0.0)
        weights = (exp_scores / jnp.sum(exp_scores, axis=-1, keepdims=True)).astype(jnp.bfloat16)
        mixed_block = jnp.einsum(
            "hqk,khd->qhd", weights, value_all, preferred_element_type=jnp.float32
        )
        return mixed_block.reshape(block_rows, -1).astype(jnp.bfloat16)

    blocks = lax.map(one_block, jnp.arange(rows_total // block_rows, dtype=jnp.int32))
    return blocks.reshape(rows_total, -1)


def hidden_units(row_values, up_matrix, gate_matrix, up_scaling, gate_scaling):
    up_part = jnp.dot(row_values, up_matrix, preferred_element_type=jnp.float32) * up_scaling
    gate_part = jnp.dot(row_values, gate_matrix, preferred_element_type=jnp.float32) * gate_scaling
    return (up_part * jax.nn.silu(gate_part)).astype(jnp.bfloat16)


def local_generic(
    hidden,
    lengths,
    request_prompt,
    request_adapter,
    prompt_page_table,
    prefix_page_cache,
    query_key_value_weight,
    adapter_down,
    adapter_up,
    attention_scale,
    output_matrix,
    attention_rate,
    up_matrix,
    gate_matrix,
    up_scaling,
    gate_scaling,
    down_matrix,
    feedforward_rate,
):
    tok_rows = hidden.shape[0]
    group_rows = tok_rows * lax.axis_size("tensor")
    heads_here = query_key_value_weight.shape[1] // (3 * HEAD_WIDTH)
    gain_qk = attention_scale.reshape(heads_here, HEAD_WIDTH)
    request_number, offset = layout(lengths[0], group_rows)
    position = offset.astype(jnp.float32) + PREFIX_LEN
    local_cache = prefix_page_cache.reshape(
        prefix_page_cache.shape[0], PAGE, heads_here, 2, HEAD_WIDTH
    )
    local_keys = (to_unit(local_cache[:, :, :, 0, :].astype(jnp.float32)) * gain_qk).astype(
        jnp.bfloat16
    )
    prepared = jnp.stack([local_keys, local_cache[:, :, :, 1, :]], axis=3).reshape(
        prefix_page_cache.shape
    )
    all_pages = lax.all_gather(prepared, "dp", axis=0, tiled=True)
    down_all, up_all = (
        lax.all_gather(adapter_down, "dp", axis=0, tiled=True),
        lax.all_gather(adapter_up, "dp", axis=0, tiled=True),
    )
    every_row = lax.all_gather(hidden, "tensor", axis=0, tiled=True)
    adapter_count = down_all.shape[0]
    onehot = (
        request_adapter[0][:, None] == jnp.arange(adapter_count, dtype=jnp.int32)[None, :]
    ).astype(jnp.bfloat16)
    selected_down = jnp.dot(
        onehot, down_all.reshape(adapter_count, -1), preferred_element_type=jnp.float32
    ).astype(jnp.bfloat16)
    selected_down = jnp.transpose(
        selected_down.reshape(GROUP_REQUESTS, MODEL_WIDTH, ADAPTER_RANK), (1, 0, 2)
    ).reshape(MODEL_WIDTH, GROUP_REQUESTS * ADAPTER_RANK)
    selected_up = jnp.dot(
        onehot, up_all.reshape(adapter_count, -1), preferred_element_type=jnp.float32
    ).astype(jnp.bfloat16)
    selected_up = selected_up.reshape(GROUP_REQUESTS * ADAPTER_RANK, heads_here * 3 * HEAD_WIDTH)
    request_of_slot = jnp.arange(GROUP_REQUESTS * ADAPTER_RANK, dtype=jnp.int32) // ADAPTER_RANK
    plain_projection = jnp.dot(
        every_row, query_key_value_weight, preferred_element_type=jnp.float32
    )
    adapter_middle = jnp.dot(every_row, selected_down, preferred_element_type=jnp.float32)
    adapter_middle = jnp.where(
        request_number[:, None] == request_of_slot[None, :], adapter_middle, 0.0
    ).astype(jnp.bfloat16)
    query_key_value = (
        plain_projection
        + adapter_scale * jnp.dot(adapter_middle, selected_up, preferred_element_type=jnp.float32)
    ).reshape(group_rows, heads_here, 3, HEAD_WIDTH)
    queries = (to_unit(rotate(query_key_value[:, :, 0, :], position)) * gain_qk).astype(
        jnp.bfloat16
    )
    key_own = (to_unit(rotate(query_key_value[:, :, 1, :], position)) * gain_qk).astype(
        jnp.bfloat16
    )
    value_own = query_key_value[:, :, 2, :].astype(jnp.bfloat16)
    page_list = prompt_page_table[request_prompt[0]].reshape(-1)
    picked = jnp.take(all_pages, page_list, axis=0).reshape(
        GROUP_REQUESTS * PREFIX_LEN, heads_here, 2, HEAD_WIDTH
    )
    key_all = jnp.concatenate([picked[:, :, 0, :], key_own], axis=0)
    value_all = jnp.concatenate([picked[:, :, 1, :], value_own], axis=0)
    key_request = jnp.concatenate(
        [jnp.arange(GROUP_REQUESTS * PREFIX_LEN, dtype=jnp.int32) // PREFIX_LEN, request_number],
        axis=0,
    )
    key_row = jnp.concatenate(
        [
            jnp.full((GROUP_REQUESTS * PREFIX_LEN,), -1, jnp.int32),
            jnp.arange(group_rows, dtype=jnp.int32),
        ],
        axis=0,
    )
    attn = attend(queries, key_all, value_all, request_number, key_request, key_row)
    attn_sum = lax.psum_scatter(
        jnp.dot(attn, output_matrix, preferred_element_type=jnp.float32).astype(jnp.bfloat16),
        "tensor",
        scatter_dimension=0,
        tiled=True,
    ).astype(jnp.float32)
    base_rows = hidden.astype(jnp.float32)
    mixed = renorm(base_rows + attention_rate * (renorm(attn_sum) - base_rows)).astype(jnp.bfloat16)
    unit_values = hidden_units(
        lax.all_gather(mixed, "tensor", axis=0, tiled=True),
        up_matrix,
        gate_matrix,
        up_scaling,
        gate_scaling,
    )
    mlp_sum = lax.psum_scatter(
        jnp.dot(unit_values, down_matrix, preferred_element_type=jnp.float32).astype(jnp.bfloat16),
        "tensor",
        scatter_dimension=0,
        tiled=True,
    ).astype(jnp.float32)
    mixed_rows = mixed.astype(jnp.float32)
    return renorm(mixed_rows + feedforward_rate * (renorm(mlp_sum) - mixed_rows)).astype(
        jnp.bfloat16
    )


CHIP_ROWS = 256
SCORE_LOG2 = math.sqrt(HEAD_WIDTH) / math.log(2.0)
VMEM = pl.BlockSpec(memory_space=pltpu.VMEM)
SMEM = pl.BlockSpec(memory_space=pltpu.SMEM)
BF16 = jnp.bfloat16
F32 = jnp.float32


def call(kernel, outs, operands, scalars, scratch=(), limit=12, flops=0, moved=0, far=(), unread=()):
    count = len(operands)
    specs = [SMEM] * scalars + [VMEM] * (count - scalars)
    for place in far:
        specs[place] = pl.BlockSpec(memory_space=pltpu.HBM)
    for place in unread:
        specs[place] = pl.BlockSpec(memory_space=pl.ANY)
    buffers = [pltpu.VMEM(operands[place].shape, operands[place].dtype) for place in far]
    if far:
        buffers.append(pltpu.SemaphoreType.DMA((len(far),)))

    def whole(*refs):
        refs = list(refs)
        if far:
            *near, arrivals = refs[len(refs) - len(far) - 1 :]
            refs = refs[: len(refs) - len(far) - 1]
            copies = [
                pltpu.make_async_copy(refs[place], near[i], arrivals.at[i])
                for i, place in enumerate(far)
            ]
            for copy in copies:
                copy.start()
            for copy in copies:
                copy.wait()
            for i, place in enumerate(far):
                refs[place] = near[i]
        kernel(*refs)

    return pl.pallas_call(
        whole,
        out_shape=outs,
        in_specs=specs,
        out_specs=jax.tree.map(lambda _: VMEM, outs),
        scratch_shapes=[*scratch, *buffers],
        compiler_params=pltpu.CompilerParams(vmem_limit_bytes=limit * 1024 * 1024),
        cost_estimate=pl.CostEstimate(flops=flops, bytes_accessed=moved, transcendentals=0),
    )(*operands)


def shape(rows, columns, kind=BF16):
    return jax.ShapeDtypeStruct((rows, columns), kind)


def iota(dims, axis):
    return lax.broadcasted_iota(jnp.int32, dims, axis)


def first_head(rows):
    return iota((rows, 2 * HEAD_WIDTH), 1) < HEAD_WIDTH


def unit_heads(vectors, gain):
    low = first_head(vectors.shape[0])
    squares = vectors * vectors
    sum_low = jnp.sum(jnp.where(low, squares, 0.0), axis=-1, keepdims=True)
    sum_high = jnp.sum(jnp.where(low, 0.0, squares), axis=-1, keepdims=True)
    return vectors * lax.rsqrt(jnp.where(low, sum_low, sum_high) + epsilon) * gain


def dot(left, right):
    return jnp.dot(left, right, preferred_element_type=F32)


def dot_nt(left, right):
    return lax.dot_general(
        left, right, (((1,), (1,)), ((), ())), preferred_element_type=F32
    )


def prepare_kernel(ids, pages, up, down, gain, out):
    rows = pages.shape[0]
    low = first_head(rows)
    left = pages[:, 0:128].astype(F32)
    right = pages[:, 128:256].astype(F32)
    keys = jnp.where(low, left, pltpu.roll(right, HEAD_WIDTH, 1))
    values = jnp.where(low, pltpu.roll(left, HEAD_WIDTH, 1), right)
    out[0:256, 0:128] = unit_heads(keys, gain[...]).astype(BF16)
    out[0:256, 128:256] = values.astype(BF16)
    out[0:256, 256:640] = up[...]
    row, column = iota((128, 256), 0), iota((128, 256), 1)
    source = (row // 8) * ADAPTER_RANK + 8 * (ids[0] % 2) + row % 8
    picked = dot((column == source).astype(BF16), down[...]).astype(BF16)
    out[256:384, :] = picked[:, 0:640]
    out[384:512, :] = picked[:, 640:1280]


def by_request(index, scalars):
    picked = jnp.zeros_like(index)
    for request in range(GROUP_REQUESTS):
        picked = jnp.where(index == request, scalars[0, request], picked)
    return picked


def select_kernel(ids, adapters, g0, g1, g2, g3, g4, down_out, up_out):
    core, dp = ids[0] % 2, ids[1]
    row, column = iota((64, 128), 0), iota((64, 128), 1)
    adapter = by_request(row // 8, adapters)
    source = (adapter % 16) * 8 + row % 8
    owner = (adapter // 16) ^ dp
    up_row, up_column = iota((128, 256), 0), iota((128, 256), 1)
    up_adapter = by_request((up_row % 64) // 8, adapters)
    up_source = (up_adapter % 16) * 16 + 8 * ((up_row // 64) ^ core) + up_row % 8
    up_owner = (up_adapter // 16) ^ dp
    left = right = up_total = 0.0
    for m, g in enumerate((g0, g1, g2, g3)):
        lower, first = (g4, 0) if m == 3 else (g, 256)
        hot = ((column == source) & (owner == m)).astype(BF16)
        left = left + dot(hot, lower[first : first + 128, :])
        right = right + dot(hot, lower[first + 128 : first + 256, :])
        up_hot = ((up_column == up_source) & (up_owner == m)).astype(BF16)
        up_total = up_total + dot(up_hot, g[0:256, 256:640])
    down_out[:, 0:640] = left.astype(BF16)
    down_out[:, 640:1280] = right.astype(BF16)
    up_out[...] = up_total.astype(BF16)


def middle_chip(ids):
    chip = ids[0] // 2
    return (chip == 1) | (chip == 2)


def arrived(ids, parts):
    if len(parts) == 1:
        return parts[0][0:128, :]
    return jnp.where(middle_chip(ids), parts[0][0:128, :], parts[1][0:128, :])


def piece_spots(ids, j):
    core = ids[0] % 2
    base = ((ids[0] // 2) ^ j) * CHIP_ROWS
    return [pl.multiple_of(base + side * 128, 128) for side in (core, 1 - core)]


def row_pieces(ids, refs, js):
    pieces = []
    for j in js:
        count = 2 if j == 3 else 1
        pieces += [arrived(ids, refs[:count]), arrived(ids, refs[count : 2 * count])]
        refs = refs[2 * count :]
    return pieces, refs


def request_starts(lengths):
    begins = [jnp.int32(0)]
    for i in range(GROUP_REQUESTS):
        begins.append(begins[-1] + lengths[0, i])
    return begins


def project(j, ids, begins, pieces, weight, down, down_other, up, cosines, sines, gain):
    rows = jnp.concatenate(pieces, axis=0)
    count = rows.shape[0]
    row = jnp.concatenate([spot + iota((128, 128), 0) for spot in piece_spots(ids, j)], axis=0)
    request = (iota((1, 128), 1) % 64) // 8
    first, end = jnp.zeros_like(request), jnp.zeros_like(request)
    for i in range(GROUP_REQUESTS):
        first = jnp.where(request == i, begins[i], first)
        end = jnp.where(request == i, begins[i + 1], end)
    middle = dot_nt(rows, jnp.concatenate([down[...], down_other[...]], axis=0))
    middle = jnp.where((row >= first) & (row < end), middle, 0.0).astype(BF16)
    total = dot(rows, weight[...]) + adapter_scale * dot(middle, up[...])
    part0, part1, part2 = total[:, 0:128], total[:, 128:256], total[:, 256:384]
    low = first_head(count)
    query = jnp.where(low, part0, part1)
    key = pltpu.roll(jnp.where(low, part2, part0), HEAD_WIDTH, 1)
    value = jnp.where(low, part1, part2).astype(BF16)
    cosine = jnp.concatenate([cosines[pl.ds(spot, 128), :] for spot in piece_spots(ids, j)], axis=0)
    sine = jnp.concatenate([sines[pl.ds(spot, 128), :] for spot in piece_spots(ids, j)], axis=0)
    half = HEAD_WIDTH // 2
    head_low = (iota((count, 128), 1) % HEAD_WIDTH) < half

    def finish(x):
        turned = jnp.where(head_low, pltpu.roll(x, 128 - half, 1), pltpu.roll(x, half, 1))
        return unit_heads(x * cosine + turned * sine, gain[...]).astype(BF16)

    return finish(query), finish(key), value


def attend_kernel(ids, lengths, prompts, table, *refs):
    pieces, refs = row_pieces(ids, refs, range(4))
    *constants, g0, g1, g2, g3, out, queries, keys, values, pages, starts, sums = refs
    begins = request_starts(lengths)
    for i, begin in enumerate(begins):
        starts[i] = begin
    for j in range(4):
        parts = project(j, ids, begins, pieces[2 * j : 2 * j + 2], *constants)
        for part, target in zip(parts, (queries, keys, values)):
            for side, spot in enumerate(piece_spots(ids, j)):
                target[pl.ds(spot, 128), :] = part[side * 128 : side * 128 + 128]
    for m, g in enumerate((g0, g1, g2, g3)):
        pages[pl.ds(pl.multiple_of((ids[1] ^ m) * 256, 256), 256), :] = g[0:256, 0:256]
    tiles = out.shape[0] // 128
    low = first_head(128)
    low_keys = first_head(256)
    ones = jnp.ones((256, 128), BF16)

    def tile_queries(tile):
        query = queries[pl.ds(pl.multiple_of(tile * 128, 128), 128), :]
        zero = jnp.zeros_like(query)
        both = jnp.concatenate(
            [jnp.where(low, query, zero), jnp.where(low, zero, query)], axis=0
        )
        return both, tile * 128 + iota((256, 1), 0) % 128

    def prefix(request):
        prompt = prompts[0, request]
        spots = [pl.multiple_of(table[prompt, p] * PAGE, PAGE) for p in range(PREFIX_LEN // PAGE)]
        return (
            jnp.concatenate([pages[pl.ds(s, PAGE), 0:128] for s in spots], axis=0),
            jnp.concatenate([pages[pl.ds(s, PAGE), 128:256] for s in spots], axis=0),
        )

    def window(spot):
        spot = pl.multiple_of(spot, 128)
        return keys[pl.ds(spot, 256), :], values[pl.ds(spot, 256), :], spot + iota((256, 256), 1)

    def products(both, key, value, mask):
        weights = jnp.where(mask, jnp.exp2(dot_nt(both, key) * SCORE_LOG2), 0.0).astype(BF16)
        return (
            dot(weights[:128], jnp.where(low_keys, value, ones)),
            dot(weights[128:], jnp.where(low_keys, ones, value)),
        )

    firsts = []
    for tile in range(tiles):
        base = tile * 128
        both, row = tile_queries(tile)
        first = jnp.int32(0)
        row_start = jnp.zeros_like(row)
        for begin in begins[1:GROUP_REQUESTS]:
            row_start = jnp.where(row >= begin, begin, row_start)
            first = first + (begin <= base).astype(jnp.int32)
        firsts.append(first)
        mask = jnp.broadcast_to(row < starts[first + 1], (256, PREFIX_LEN))
        shared = products(both, *prefix(first), mask)
        key, value, column = window(max(base - 128, 0))
        own = products(both, key, value, (column >= row_start) & (column <= row))
        for head in (0, 1):
            sums[tile, head] = shared[head] + own[head]
    for i in range(1, GROUP_REQUESTS):
        begin, end = begins[i], begins[i + 1]
        tile = begin // 128
        both, row = tile_queries(tile)
        mask = (row >= begin) & (row < end) & (begin % 128 != 0)
        more = products(both, *prefix(i), jnp.broadcast_to(mask, (256, PREFIX_LEN)))
        for head in (0, 1):
            sums[tile, head] += more[head]
    for tile in range(2, tiles):
        base = tile * 128
        first = firsts[tile]
        begin, end = starts[first], starts[first + 1]

        def earlier(step, carry, tile=tile, base=base, begin=begin, end=end):
            both, row = tile_queries(tile)
            stop = base - 128 - 256 * step
            key, value, column = window(jnp.maximum(stop - 256, 0))
            mask = (column >= begin) & (column < stop) & (row < end)
            more = products(both, key, value, mask)
            for head in (0, 1):
                sums[tile, head] += more[head]
            return carry

        lax.fori_loop(0, jnp.maximum(base + 127 - begin, 0) // 256, earlier, 0)
    for tile in range(tiles):
        left, right = sums[tile, 0], sums[tile, 1]
        weight = pltpu.roll(jnp.where(low, right, left), HEAD_WIDTH, 1)
        out[tile * 128 : tile * 128 + 128, :] = (jnp.where(low, left, right) / weight).astype(BF16)


def collect_kernel(ids, o0, o1, o2, o3, *outs):
    for m, part in enumerate((o0, o1, o2, o3)):
        spot = pl.multiple_of((ids[1] ^ m) * 32, 32)
        for j in range(4):
            outs[j // 2][j % 2, pl.ds(spot, 32), :] = part[j]


def mlp_kernel(js, ids, *refs):
    heads_in, refs = refs[:10], refs[10:]
    pieces, refs = row_pieces(ids, refs, js)
    matrices, refs = refs[:4], refs[4:]
    rate, up, gate, up_scale, gate_scale, down, _, keep, send, *rest = refs
    direct = middle_chip(ids)
    for place, j in enumerate(js):
        spots = piece_spots(ids, j)

        def rows_of(heads):
            return jnp.concatenate([heads[pl.ds(spot, 128), :] for spot in spots], axis=0)

        attn_sum = 0.0
        for side in (0, 1):
            columns = [rows_of(heads_in[2 * distance + side]) for distance in range(4)]
            columns[3] = jnp.where(direct, columns[3], rows_of(heads_in[8 + side]))
            for half in (0, 1):
                pair = jnp.concatenate(columns[2 * half : 2 * half + 2], axis=1)
                attn_sum = attn_sum + dot(pair, matrices[2 * side + half][...])
        base = jnp.concatenate(pieces[2 * place : 2 * place + 2], axis=0).astype(F32)
        mixed = renorm(base + rate[...] * (renorm(attn_sum) - base)).astype(BF16)
        up_part = dot(mixed, up[...]) * up_scale[...]
        gate_part = dot(mixed, gate[...]) * gate_scale[...]
        unit_values = (up_part * (gate_part / (1.0 + jnp.exp(-gate_part)))).astype(BF16)
        result = dot(unit_values, down[...]).astype(BF16)
        keep[place * 128 : place * 128 + 128, :] = result[0:128]
        send[place * 128 : place * 128 + 128, :] = result[128:256]
        if j == 0:
            rest[0][...] = mixed[0:128]


def add_kernel(ids, keep, inward, direct, out):
    more = inward[...].astype(F32)
    out[...] = keep[0:128, :].astype(F32) + jnp.where(middle_chip(ids), more, 0.0)


def final_kernel(mixed, keep, got0, got1, r1, r2, r3, rate, out):
    got = jnp.concatenate([got0[...], got1[...]], axis=0)
    mlp_sum = keep[...].astype(F32) + got.astype(F32)
    for r in (r1, r2, r3):
        mlp_sum = mlp_sum + r[...].astype(F32)
    base = mixed[...].astype(F32)
    out[...] = renorm(base + rate[...] * (renorm(mlp_sum) - base)).astype(BF16)


def swap(values, distance, axis="tensor"):
    size = lax.axis_size(axis)
    return lax.ppermute(values, axis, [(i, i ^ distance) for i in range(size)])


def middle(values):
    return lax.ppermute(values, "tensor", [(2, 4), (3, 5), (4, 2), (5, 3)])


def local_pairwise(
    hidden,
    lengths,
    request_prompt,
    request_adapter,
    prompt_page_table,
    prefix_page_cache,
    query_key_value_weight,
    adapter_down,
    adapter_up,
    attention_scale,
    output_matrix,
    attention_rate,
    up_matrix,
    gate_matrix,
    up_scaling,
    gate_scaling,
    down_matrix,
    feedforward_rate,
):
    group_rows = hidden.shape[0] * lax.axis_size("tensor")
    tensor, dp = lax.axis_index("tensor"), lax.axis_index("dp")
    ids = jnp.stack([tensor, dp]).astype(jnp.int32)
    gain = attention_scale.reshape(1, -1)

    row_ids = jnp.arange(group_rows, dtype=jnp.int32)
    starts = jnp.cumsum(lengths[0]) - lengths[0]
    row_start = jnp.max(
        jnp.where(row_ids[:, None] >= starts[None, :], starts[None, :], 0), axis=1
    )
    position = (row_ids - row_start).astype(F32) + PREFIX_LEN
    half = HEAD_WIDTH // 2
    lanes = jnp.arange(2 * HEAD_WIDTH, dtype=jnp.int32) % HEAD_WIDTH
    frequency = jnp.exp((lanes % half).astype(F32) * (-2.0 * math.log(10000.0) / HEAD_WIDTH))
    angles = position[:, None] * frequency[None, :]
    cosines = jnp.cos(angles)
    sines = jnp.where(lanes[None, :] < half, -1.0, 1.0) * jnp.sin(angles)

    quarter = output_matrix.shape[0] // 4
    own_quarter = lax.dynamic_slice_in_dim(output_matrix, dp * quarter, quarter, 0)
    payload = jnp.concatenate([hidden, own_quarter], axis=0)
    far2, far1 = swap(payload, 4), swap(payload, 2)
    forwarded3, direct3 = swap(far2, 2), middle(payload)

    prepared = call(
        prepare_kernel,
        shape(512, 640),
        (
            ids,
            prefix_page_cache.reshape(-1, prefix_page_cache.shape[2]),
            adapter_up.reshape(-1, adapter_up.shape[2]),
            jnp.swapaxes(adapter_down, 1, 2).reshape(-1, MODEL_WIDTH),
            gain,
        ),
        1,
        far=(1, 2, 3),
        limit=62,
    )
    near1, near2 = swap(prepared, 1, "dp"), swap(prepared, 2, "dp")
    upper3, lower3 = swap(near2[0:256], 1, "dp"), swap(near1[256:512], 2, "dp")
    shared = [prepared, near1, near2, upper3]
    down_own, up_all = call(
        select_kernel,
        (shape(64, MODEL_WIDTH), shape(128, 384)),
        (ids, request_adapter, *shared, lower3),
        2,
        flops=0,
        moved=0,
    )
    down_other = swap(down_own, 1)

    rows = {0: [payload, swap(payload, 1)]}
    rows[1] = [far1, swap(far1, 1)]
    rows[2] = [far2, swap(far2, 1)]
    constants = (query_key_value_weight, down_own, down_other, up_all, cosines, sines, gain)
    rows[3] = [direct3, forwarded3, swap(direct3, 1), swap(forwarded3, 1)]

    chip = tensor // 2
    last = jnp.where((chip == 1) | (chip == 2), direct3[128:], forwarded3[128:])
    quarters = jnp.stack([payload[128:], far1[128:], far2[128:], last])
    outputs = [quarters] + [swap(quarters, m, "dp") for m in (1, 2, 3)]

    attn = call(
        attend_kernel,
        shape(group_rows, 128),
        (
            ids, lengths, request_prompt, prompt_page_table,
            *rows[0], *rows[1], *rows[2], *rows[3], *constants, *shared,
        ),
        4,
        scratch=(
            pltpu.VMEM((group_rows, 128), BF16),
            pltpu.VMEM((group_rows, 128), BF16),
            pltpu.VMEM((group_rows, 128), BF16),
            pltpu.VMEM((1024, 256), BF16),
            pltpu.SMEM((GROUP_REQUESTS + 1,), jnp.int32),
            pltpu.VMEM((group_rows // 128, 2, 128, 128), F32),
        ),
        flops=2 * 10**10,
        moved=2 * 10**6,
        limit=24,
    )

    heads2, heads1 = swap(attn, 4), swap(attn, 2)
    heads3, heads3f = middle(attn), swap(heads2, 2)
    all_heads = [attn, swap(attn, 1), heads1, swap(heads1, 1), heads2, swap(heads2, 1)]
    all_heads += [heads3, swap(heads3, 1), heads3f, swap(heads3f, 1)]

    collected = call(
        collect_kernel,
        (jax.ShapeDtypeStruct((2, 4 * quarter, MODEL_WIDTH), BF16),) * 2,
        (ids, *outputs),
        1,
    )
    collected = [part.reshape(-1, MODEL_WIDTH) for part in collected]
    weights = (
        *collected, *[swap(part, 1) for part in collected],
        attention_rate.reshape(1, -1), up_matrix, gate_matrix,
        up_scaling.reshape(1, -1), gate_scaling.reshape(1, -1), down_matrix,
    )
    def update(js, previous):
        operands = (ids, *all_heads, *[piece for j in js for piece in rows[j]], *weights, previous)
        return call(
            functools.partial(mlp_kernel, js),
            (shape(128 * len(js), MODEL_WIDTH),) * 2 + (shape(128, MODEL_WIDTH),) * (0 in js),
            operands,
            1,
            limit=24,
            flops=2 * 10**10,
            moved=10**7,
            unread=(len(operands) - 1,),
        )

    def chunk(kept, swapped):
        return (kept.astype(F32) + swapped.astype(F32)).astype(BF16)

    keep3, send3 = update((3,), ids)
    chunk3 = chunk(keep3, swap(send3, 1))
    inward, received3 = swap(chunk3, 2), middle(chunk3)
    keep, send = update((2, 1), keep3)
    got = swap(send, 1)
    received1 = swap(chunk(keep[128:256], got[128:256]), 2)
    joined = call(
        add_kernel,
        shape(128, MODEL_WIDTH, F32),
        (ids, keep, inward, received3),
        1,
        flops=2 * 10**10,
        unread=(3,),
    )
    chunk2 = chunk(joined, got[0:128])
    received2 = swap(chunk2, 4)
    keep0, send0, mixed = update((0,), chunk2)
    return call(
        final_kernel,
        shape(*hidden.shape),
        (
            mixed, keep0, swap(send0[0:64], 1), swap(send0[64:128], 1), received1, received2, received3,
            feedforward_rate.reshape(1, -1),
        ),
        0,
    )


def solution(mesh):
    placed = (
        P(("dp", "tensor"), None),
        P("dp", None),
        P("dp", None),
        P("dp", None),
        P(),
        P("dp", None, "tensor"),
        P(None, "tensor"),
        P("dp", None, None),
        P("dp", None, "tensor"),
        P("tensor"),
        P("tensor", None),
        P(),
        P(None, "tensor"),
        P(None, "tensor"),
        P("tensor"),
        P("tensor"),
        P("tensor", None),
        P(),
    )
    pairwise = mesh.shape["dp"] == 4 and mesh.shape["tensor"] == 8
    return jax.shard_map(
        local_pairwise if pairwise else local_generic, mesh=mesh, in_specs=placed, out_specs=P(("dp", "tensor"), None), check_vma=False
    )
```

```python
import functools
import math

import jax
import jax.numpy as jnp
from jax import lax
from jax.experimental import pallas as pl
from jax.experimental.pallas import tpu as pltpu
from jax.sharding import PartitionSpec as P

MODEL_WIDTH = 1280
HEAD_WIDTH = 64
ADAPTER_RANK = 16
GROUP_REQUESTS = 8
PAGE = 64
PREFIX_LEN = 256


adapter_scale = 0.5
epsilon = 1e-06


def renorm(matrix):
    return matrix * lax.rsqrt(jnp.mean(matrix * matrix, axis=-1, keepdims=True) + epsilon)


def to_unit(vectors):
    return vectors * lax.rsqrt(jnp.sum(vectors * vectors, axis=-1, keepdims=True) + epsilon)


def rotate(vectors, position):
    half_size = vectors.shape[-1] // 2
    frequency = jnp.exp(
        jnp.arange(half_size).astype(jnp.float32) * (-2.0 * math.log(10000.0) / vectors.shape[-1])
    )
    angles = position[:, None] * frequency[None, :]
    cosine = jnp.cos(angles)[:, None, :]
    sines = jnp.sin(angles)[:, None, :]
    first_half = vectors[..., :half_size]
    second_half = vectors[..., half_size:]
    return jnp.concatenate(
        [first_half * cosine - second_half * sines, first_half * sines + second_half * cosine],
        axis=-1,
    )


def layout(counts, total_rows):
    row_ends = jnp.cumsum(counts)
    starts = row_ends - counts
    row_ids = jnp.arange(total_rows, dtype=jnp.int32)
    request_number = jnp.sum((row_ids[:, None] >= row_ends[None, :]).astype(jnp.int32), axis=1)
    selected_adapter = (
        request_number[:, None] == jnp.arange(counts.shape[0], dtype=jnp.int32)[None, :]
    )
    offset = row_ids - jnp.sum(jnp.where(selected_adapter, starts[None, :], 0), axis=1)
    return (request_number, offset)


def attend(queries, key_all, value_all, request_number, key_request, key_row):
    rows_total = queries.shape[0]
    block_rows = min(512, rows_total)
    score_scale = math.sqrt(queries.shape[-1])
    row_ids = jnp.arange(rows_total, dtype=jnp.int32)

    def one_block(block_index):
        first_row = block_index * block_rows
        query_block = lax.dynamic_slice_in_dim(queries, first_row, block_rows, 0)
        request_block = lax.dynamic_slice_in_dim(request_number, first_row, block_rows, 0)
        row_block = lax.dynamic_slice_in_dim(row_ids, first_row, block_rows, 0)
        scores = (
            jnp.einsum("qhd,khd->hqk", query_block, key_all, preferred_element_type=jnp.float32)
            * score_scale
        )
        allowed = (request_block[:, None] == key_request[None, :]) & (
            key_row[None, :] <= row_block[:, None]
        )
        exp_scores = jnp.where(allowed[None], jnp.exp(scores), 0.0)
        weights = (exp_scores / jnp.sum(exp_scores, axis=-1, keepdims=True)).astype(jnp.bfloat16)
        mixed_block = jnp.einsum(
            "hqk,khd->qhd", weights, value_all, preferred_element_type=jnp.float32
        )
        return mixed_block.reshape(block_rows, -1).astype(jnp.bfloat16)

    blocks = lax.map(one_block, jnp.arange(rows_total // block_rows, dtype=jnp.int32))
    return blocks.reshape(rows_total, -1)


def hidden_units(row_values, up_matrix, gate_matrix, up_scaling, gate_scaling):
    up_part = jnp.dot(row_values, up_matrix, preferred_element_type=jnp.float32) * up_scaling
    gate_part = jnp.dot(row_values, gate_matrix, preferred_element_type=jnp.float32) * gate_scaling
    return (up_part * jax.nn.silu(gate_part)).astype(jnp.bfloat16)


def local_generic(
    hidden,
    lengths,
    request_prompt,
    request_adapter,
    prompt_page_table,
    prefix_page_cache,
    query_key_value_weight,
    adapter_down,
    adapter_up,
    attention_scale,
    output_matrix,
    attention_rate,
    up_matrix,
    gate_matrix,
    up_scaling,
    gate_scaling,
    down_matrix,
    feedforward_rate,
):
    tok_rows = hidden.shape[0]
    group_rows = tok_rows * lax.axis_size("tensor")
    heads_here = query_key_value_weight.shape[1] // (3 * HEAD_WIDTH)
    gain_qk = attention_scale.reshape(heads_here, HEAD_WIDTH)
    request_number, offset = layout(lengths[0], group_rows)
    position = offset.astype(jnp.float32) + PREFIX_LEN
    local_cache = prefix_page_cache.reshape(
        prefix_page_cache.shape[0], PAGE, heads_here, 2, HEAD_WIDTH
    )
    local_keys = (to_unit(local_cache[:, :, :, 0, :].astype(jnp.float32)) * gain_qk).astype(
        jnp.bfloat16
    )
    prepared = jnp.stack([local_keys, local_cache[:, :, :, 1, :]], axis=3).reshape(
        prefix_page_cache.shape
    )
    all_pages = lax.all_gather(prepared, "dp", axis=0, tiled=True)
    down_all, up_all = (
        lax.all_gather(adapter_down, "dp", axis=0, tiled=True),
        lax.all_gather(adapter_up, "dp", axis=0, tiled=True),
    )
    every_row = lax.all_gather(hidden, "tensor", axis=0, tiled=True)
    adapter_count = down_all.shape[0]
    onehot = (
        request_adapter[0][:, None] == jnp.arange(adapter_count, dtype=jnp.int32)[None, :]
    ).astype(jnp.bfloat16)
    selected_down = jnp.dot(
        onehot, down_all.reshape(adapter_count, -1), preferred_element_type=jnp.float32
    ).astype(jnp.bfloat16)
    selected_down = jnp.transpose(
        selected_down.reshape(GROUP_REQUESTS, MODEL_WIDTH, ADAPTER_RANK), (1, 0, 2)
    ).reshape(MODEL_WIDTH, GROUP_REQUESTS * ADAPTER_RANK)
    selected_up = jnp.dot(
        onehot, up_all.reshape(adapter_count, -1), preferred_element_type=jnp.float32
    ).astype(jnp.bfloat16)
    selected_up = selected_up.reshape(GROUP_REQUESTS * ADAPTER_RANK, heads_here * 3 * HEAD_WIDTH)
    request_of_slot = jnp.arange(GROUP_REQUESTS * ADAPTER_RANK, dtype=jnp.int32) // ADAPTER_RANK
    plain_projection = jnp.dot(
        every_row, query_key_value_weight, preferred_element_type=jnp.float32
    )
    adapter_middle = jnp.dot(every_row, selected_down, preferred_element_type=jnp.float32)
    adapter_middle = jnp.where(
        request_number[:, None] == request_of_slot[None, :], adapter_middle, 0.0
    ).astype(jnp.bfloat16)
    query_key_value = (
        plain_projection
        + adapter_scale * jnp.dot(adapter_middle, selected_up, preferred_element_type=jnp.float32)
    ).reshape(group_rows, heads_here, 3, HEAD_WIDTH)
    queries = (to_unit(rotate(query_key_value[:, :, 0, :], position)) * gain_qk).astype(
        jnp.bfloat16
    )
    key_own = (to_unit(rotate(query_key_value[:, :, 1, :], position)) * gain_qk).astype(
        jnp.bfloat16
    )
    value_own = query_key_value[:, :, 2, :].astype(jnp.bfloat16)
    page_list = prompt_page_table[request_prompt[0]].reshape(-1)
    picked = jnp.take(all_pages, page_list, axis=0).reshape(
        GROUP_REQUESTS * PREFIX_LEN, heads_here, 2, HEAD_WIDTH
    )
    key_all = jnp.concatenate([picked[:, :, 0, :], key_own], axis=0)
    value_all = jnp.concatenate([picked[:, :, 1, :], value_own], axis=0)
    key_request = jnp.concatenate(
        [jnp.arange(GROUP_REQUESTS * PREFIX_LEN, dtype=jnp.int32) // PREFIX_LEN, request_number],
        axis=0,
    )
    key_row = jnp.concatenate(
        [
            jnp.full((GROUP_REQUESTS * PREFIX_LEN,), -1, jnp.int32),
            jnp.arange(group_rows, dtype=jnp.int32),
        ],
        axis=0,
    )
    attn = attend(queries, key_all, value_all, request_number, key_request, key_row)
    attn_sum = lax.psum_scatter(
        jnp.dot(attn, output_matrix, preferred_element_type=jnp.float32).astype(jnp.bfloat16),
        "tensor",
        scatter_dimension=0,
        tiled=True,
    ).astype(jnp.float32)
    base_rows = hidden.astype(jnp.float32)
    mixed = renorm(base_rows + attention_rate * (renorm(attn_sum) - base_rows)).astype(jnp.bfloat16)
    unit_values = hidden_units(
        lax.all_gather(mixed, "tensor", axis=0, tiled=True),
        up_matrix,
        gate_matrix,
        up_scaling,
        gate_scaling,
    )
    mlp_sum = lax.psum_scatter(
        jnp.dot(unit_values, down_matrix, preferred_element_type=jnp.float32).astype(jnp.bfloat16),
        "tensor",
        scatter_dimension=0,
        tiled=True,
    ).astype(jnp.float32)
    mixed_rows = mixed.astype(jnp.float32)
    return renorm(mixed_rows + feedforward_rate * (renorm(mlp_sum) - mixed_rows)).astype(
        jnp.bfloat16
    )


CHIP_ROWS = 256
SCORE_LOG2 = math.sqrt(HEAD_WIDTH) / math.log(2.0)
VMEM = pl.BlockSpec(memory_space=pltpu.VMEM)
SMEM = pl.BlockSpec(memory_space=pltpu.SMEM)
BF16 = jnp.bfloat16
F32 = jnp.float32


def call(kernel, outs, operands, scalars, scratch=(), limit=12, flops=0, moved=0, far=(), unread=()):
    count = len(operands)
    specs = [SMEM] * scalars + [VMEM] * (count - scalars)
    for place in far:
        specs[place] = pl.BlockSpec(memory_space=pltpu.HBM)
    for place in unread:
        specs[place] = pl.BlockSpec(memory_space=pl.ANY)
    buffers = [pltpu.VMEM(operands[place].shape, operands[place].dtype) for place in far]
    if far:
        buffers.append(pltpu.SemaphoreType.DMA((len(far),)))

    def whole(*refs):
        refs = list(refs)
        if far:
            *near, arrivals = refs[len(refs) - len(far) - 1 :]
            refs = refs[: len(refs) - len(far) - 1]
            copies = [
                pltpu.make_async_copy(refs[place], near[i], arrivals.at[i])
                for i, place in enumerate(far)
            ]
            for copy in copies:
                copy.start()
            for copy in copies:
                copy.wait()
            for i, place in enumerate(far):
                refs[place] = near[i]
        kernel(*refs)

    return pl.pallas_call(
        whole,
        out_shape=outs,
        in_specs=specs,
        out_specs=jax.tree.map(lambda _: VMEM, outs),
        scratch_shapes=[*scratch, *buffers],
        compiler_params=pltpu.CompilerParams(vmem_limit_bytes=limit * 1024 * 1024),
        cost_estimate=pl.CostEstimate(flops=flops, bytes_accessed=moved, transcendentals=0),
    )(*operands)


def shape(rows, columns, kind=BF16):
    return jax.ShapeDtypeStruct((rows, columns), kind)


def iota(dims, axis):
    return lax.broadcasted_iota(jnp.int32, dims, axis)


def first_head(rows):
    return iota((rows, 2 * HEAD_WIDTH), 1) < HEAD_WIDTH


def unit_heads(vectors, gain):
    low = first_head(vectors.shape[0])
    squares = vectors * vectors
    sum_low = jnp.sum(jnp.where(low, squares, 0.0), axis=-1, keepdims=True)
    sum_high = jnp.sum(jnp.where(low, 0.0, squares), axis=-1, keepdims=True)
    return vectors * lax.rsqrt(jnp.where(low, sum_low, sum_high) + epsilon) * gain


def dot(left, right):
    return jnp.dot(left, right, preferred_element_type=F32)


def dot_nt(left, right):
    return lax.dot_general(
        left, right, (((1,), (1,)), ((), ())), preferred_element_type=F32
    )


def prepare_kernel(ids, pages, up, down, gain, out):
    rows = pages.shape[0]
    low = first_head(rows)
    left = pages[:, 0:128].astype(F32)
    right = pages[:, 128:256].astype(F32)
    keys = jnp.where(low, left, pltpu.roll(right, HEAD_WIDTH, 1))
    values = jnp.where(low, pltpu.roll(left, HEAD_WIDTH, 1), right)
    out[0:256, 0:128] = unit_heads(keys, gain[...]).astype(BF16)
    out[0:256, 128:256] = values.astype(BF16)
    out[0:256, 256:640] = up[...]
    row, column = iota((128, 256), 0), iota((128, 256), 1)
    source = (row // 8) * ADAPTER_RANK + 8 * (ids[0] % 2) + row % 8
    picked = dot((column == source).astype(BF16), down[...]).astype(BF16)
    out[256:384, :] = picked[:, 0:640]
    out[384:512, :] = picked[:, 640:1280]


def by_request(index, scalars):
    picked = jnp.zeros_like(index)
    for request in range(GROUP_REQUESTS):
        picked = jnp.where(index == request, scalars[0, request], picked)
    return picked


def select_kernel(ids, adapters, g0, g1, g2, g3, g4, down_out, up_out):
    core, dp = ids[0] % 2, ids[1]
    row, column = iota((64, 128), 0), iota((64, 128), 1)
    adapter = by_request(row // 8, adapters)
    source = (adapter % 16) * 8 + row % 8
    owner = (adapter // 16) ^ dp
    up_row, up_column = iota((128, 256), 0), iota((128, 256), 1)
    up_adapter = by_request((up_row % 64) // 8, adapters)
    up_source = (up_adapter % 16) * 16 + 8 * ((up_row // 64) ^ core) + up_row % 8
    up_owner = (up_adapter // 16) ^ dp
    left = right = up_total = 0.0
    for m, g in enumerate((g0, g1, g2, g3)):
        lower, first = (g4, 0) if m == 3 else (g, 256)
        hot = ((column == source) & (owner == m)).astype(BF16)
        left = left + dot(hot, lower[first : first + 128, :])
        right = right + dot(hot, lower[first + 128 : first + 256, :])
        up_hot = ((up_column == up_source) & (up_owner == m)).astype(BF16)
        up_total = up_total + dot(up_hot, g[0:256, 256:640])
    down_out[:, 0:640] = left.astype(BF16)
    down_out[:, 640:1280] = right.astype(BF16)
    up_out[...] = up_total.astype(BF16)


def middle_chip(ids):
    chip = ids[0] // 2
    return (chip == 1) | (chip == 2)


def arrived(ids, parts):
    if len(parts) == 1:
        return parts[0][0:128, :]
    return jnp.where(middle_chip(ids), parts[0][0:128, :], parts[1][0:128, :])


def piece_spots(ids, j):
    core = ids[0] % 2
    base = ((ids[0] // 2) ^ j) * CHIP_ROWS
    return [pl.multiple_of(base + side * 128, 128) for side in (core, 1 - core)]


def row_pieces(ids, refs, js):
    pieces = []
    for j in js:
        count = 2 if j == 3 else 1
        pieces += [arrived(ids, refs[:count]), arrived(ids, refs[count : 2 * count])]
        refs = refs[2 * count :]
    return pieces, refs


def request_starts(lengths):
    begins = [jnp.int32(0)]
    for i in range(GROUP_REQUESTS):
        begins.append(begins[-1] + lengths[0, i])
    return begins


def project(j, ids, begins, pieces, weight, down, up, cosines, sines, gain):
    rows = jnp.concatenate(pieces, axis=0)
    count = rows.shape[0]
    row = jnp.concatenate([spot + iota((128, 128), 0) for spot in piece_spots(ids, j)], axis=0)
    request = (iota((1, 128), 1) % 64) // 8
    first, end = jnp.zeros_like(request), jnp.zeros_like(request)
    for i in range(GROUP_REQUESTS):
        first = jnp.where(request == i, begins[i], first)
        end = jnp.where(request == i, begins[i + 1], end)
    total = dot(rows, jnp.concatenate([weight[...], down[...]], axis=1))
    total, middle = total[:, 0:384], total[:, 384:512]
    middle = jnp.where((row >= first) & (row < end), middle, 0.0).astype(BF16)
    total = total + adapter_scale * dot(middle, up[...])
    part0, part1, part2 = total[:, 0:128], total[:, 128:256], total[:, 256:384]
    low = first_head(count)
    query = jnp.where(low, part0, part1)
    key = pltpu.roll(jnp.where(low, part2, part0), HEAD_WIDTH, 1)
    value = jnp.where(low, part1, part2).astype(BF16)
    cosine = jnp.concatenate([cosines[pl.ds(spot, 128), :] for spot in piece_spots(ids, j)], axis=0)
    sine = jnp.concatenate([sines[pl.ds(spot, 128), :] for spot in piece_spots(ids, j)], axis=0)
    half = HEAD_WIDTH // 2
    head_low = (iota((count, 128), 1) % HEAD_WIDTH) < half

    def finish(x):
        turned = jnp.where(head_low, pltpu.roll(x, 128 - half, 1), pltpu.roll(x, half, 1))
        return unit_heads(x * cosine + turned * sine, gain[...]).astype(BF16)

    return finish(query), finish(key), value


def attend_kernel(ids, lengths, prompts, table, *refs):
    pieces, refs = row_pieces(ids, refs, range(4))
    weight, down, down_other, *constants, g0, g1, g2, g3, out = refs[:-7]
    queries, keys, values, pages, starts, sums, turned = refs[-7:]
    turned[:, 0:64] = jnp.transpose(down[...])
    turned[:, 64:128] = jnp.transpose(down_other[...])
    begins = request_starts(lengths)
    for i, begin in enumerate(begins):
        starts[i] = begin
    for j in range(4):
        rows = pieces[2 * j : 2 * j + 2]
        parts = project(j, ids, begins, rows, weight, turned, *constants)
        for part, target in zip(parts, (queries, keys, values)):
            for side, spot in enumerate(piece_spots(ids, j)):
                target[pl.ds(spot, 128), :] = part[side * 128 : side * 128 + 128]
    for m, g in enumerate((g0, g1, g2, g3)):
        pages[pl.ds(pl.multiple_of((ids[1] ^ m) * 256, 256), 256), :] = g[0:256, 0:256]
    tiles = out.shape[0] // 128
    low = first_head(128)
    low_keys = first_head(256)
    ones = jnp.ones((256, 128), BF16)

    def tile_queries(tile):
        query = queries[pl.ds(pl.multiple_of(tile * 128, 128), 128), :]
        zero = jnp.zeros_like(query)
        both = jnp.concatenate(
            [jnp.where(low, query, zero), jnp.where(low, zero, query)], axis=0
        )
        return both, tile * 128 + iota((256, 1), 0) % 128

    def prefix(request):
        prompt = prompts[0, request]
        spots = [pl.multiple_of(table[prompt, p] * PAGE, PAGE) for p in range(PREFIX_LEN // PAGE)]
        return (
            jnp.concatenate([pages[pl.ds(s, PAGE), 0:128] for s in spots], axis=0),
            jnp.concatenate([pages[pl.ds(s, PAGE), 128:256] for s in spots], axis=0),
        )

    def window(spot):
        spot = pl.multiple_of(spot, 128)
        return keys[pl.ds(spot, 256), :], values[pl.ds(spot, 256), :], spot + iota((256, 256), 1)

    def products(both, key, value, mask):
        weights = jnp.where(mask, jnp.exp2(dot_nt(both, key) * SCORE_LOG2), 0.0).astype(BF16)
        return (
            dot(weights[:128], jnp.where(low_keys, value, ones)),
            dot(weights[128:], jnp.where(low_keys, ones, value)),
        )

    firsts = []
    for tile in range(tiles):
        base = tile * 128
        both, row = tile_queries(tile)
        first = jnp.int32(0)
        row_start = jnp.zeros_like(row)
        for begin in begins[1:GROUP_REQUESTS]:
            row_start = jnp.where(row >= begin, begin, row_start)
            first = first + (begin <= base).astype(jnp.int32)
        firsts.append(first)
        mask = jnp.broadcast_to(row < starts[first + 1], (256, PREFIX_LEN))
        shared = products(both, *prefix(first), mask)
        key, value, column = window(max(base - 128, 0))
        own = products(both, key, value, (column >= row_start) & (column <= row))
        for head in (0, 1):
            sums[tile, head] = shared[head] + own[head]
    for i in range(1, GROUP_REQUESTS):
        begin, end = begins[i], begins[i + 1]
        tile = begin // 128
        both, row = tile_queries(tile)
        mask = (row >= begin) & (row < end) & (begin % 128 != 0)
        more = products(both, *prefix(i), jnp.broadcast_to(mask, (256, PREFIX_LEN)))
        for head in (0, 1):
            sums[tile, head] += more[head]
    for tile in range(2, tiles):
        base = tile * 128
        first = firsts[tile]
        begin, end = starts[first], starts[first + 1]

        def earlier(step, carry, tile=tile, base=base, begin=begin, end=end):
            both, row = tile_queries(tile)
            stop = base - 128 - 256 * step
            key, value, column = window(jnp.maximum(stop - 256, 0))
            mask = (column >= begin) & (column < stop) & (row < end)
            more = products(both, key, value, mask)
            for head in (0, 1):
                sums[tile, head] += more[head]
            return carry

        lax.fori_loop(0, jnp.maximum(base + 127 - begin, 0) // 256, earlier, 0)
    for tile in range(tiles):
        left, right = sums[tile, 0], sums[tile, 1]
        weight = pltpu.roll(jnp.where(low, right, left), HEAD_WIDTH, 1)
        out[tile * 128 : tile * 128 + 128, :] = (jnp.where(low, left, right) / weight).astype(BF16)


def collect_kernel(ids, o0, o1, o2, o3, *outs):
    for m, part in enumerate((o0, o1, o2, o3)):
        spot = pl.multiple_of((ids[1] ^ m) * 32, 32)
        for j in range(4):
            outs[j // 2][j % 2, pl.ds(spot, 32), :] = part[j]


def mlp_kernel(js, ids, *refs):
    heads_in, refs = refs[:10], refs[10:]
    pieces, refs = row_pieces(ids, refs, js)
    matrices, refs = refs[:4], refs[4:]
    rate, up, gate, up_scale, gate_scale, down, _, keep, send, *rest = refs
    direct = middle_chip(ids)
    for place, j in enumerate(js):
        spots = piece_spots(ids, j)

        def rows_of(heads):
            return jnp.concatenate([heads[pl.ds(spot, 128), :] for spot in spots], axis=0)

        columns = []
        for side in (0, 1):
            for distance in range(4):
                columns.append(rows_of(heads_in[2 * distance + side]))
            columns[-1] = jnp.where(direct, columns[-1], rows_of(heads_in[8 + side]))
        output = jnp.concatenate([matrix[...] for matrix in matrices], axis=0)
        attn_sum = dot(jnp.concatenate(columns, axis=1), output)
        base = jnp.concatenate(pieces[2 * place : 2 * place + 2], axis=0).astype(F32)
        mixed = renorm(base + rate[...] * (renorm(attn_sum) - base)).astype(BF16)
        both = dot(mixed, jnp.concatenate([up[...], gate[...]], axis=1))
        up_part = both[:, : up.shape[1]] * up_scale[...]
        gate_part = both[:, up.shape[1] :] * gate_scale[...]
        unit_values = (up_part * (gate_part / (1.0 + jnp.exp(-gate_part)))).astype(BF16)
        result = dot(unit_values, down[...]).astype(BF16)
        keep[place * 128 : place * 128 + 128, :] = result[0:128]
        send[place * 128 : place * 128 + 128, :] = result[128:256]
        if j == 0:
            rest[0][...] = mixed[0:128]


def add_kernel(ids, keep, inward, direct, out):
    more = inward[...].astype(F32)
    out[...] = keep[0:128, :].astype(F32) + jnp.where(middle_chip(ids), more, 0.0)


def final_kernel(mixed, keep, got0, got1, r1, r2, r3, rate, out):
    got = jnp.concatenate([got0[...], got1[...]], axis=0)
    mlp_sum = keep[...].astype(F32) + got.astype(F32)
    for r in (r1, r2, r3):
        mlp_sum = mlp_sum + r[...].astype(F32)
    base = mixed[...].astype(F32)
    out[...] = renorm(base + rate[...] * (renorm(mlp_sum) - base)).astype(BF16)


def swap(values, distance, axis="tensor"):
    size = lax.axis_size(axis)
    return lax.ppermute(values, axis, [(i, i ^ distance) for i in range(size)])


def middle(values):
    return lax.ppermute(values, "tensor", [(2, 4), (3, 5), (4, 2), (5, 3)])


def local_pairwise(
    hidden,
    lengths,
    request_prompt,
    request_adapter,
    prompt_page_table,
    prefix_page_cache,
    query_key_value_weight,
    adapter_down,
    adapter_up,
    attention_scale,
    output_matrix,
    attention_rate,
    up_matrix,
    gate_matrix,
    up_scaling,
    gate_scaling,
    down_matrix,
    feedforward_rate,
):
    group_rows = hidden.shape[0] * lax.axis_size("tensor")
    tensor, dp = lax.axis_index("tensor"), lax.axis_index("dp")
    ids = jnp.stack([tensor, dp]).astype(jnp.int32)
    gain = attention_scale.reshape(1, -1)

    row_ids = jnp.arange(group_rows, dtype=jnp.int32)
    starts = jnp.cumsum(lengths[0]) - lengths[0]
    row_start = jnp.max(
        jnp.where(row_ids[:, None] >= starts[None, :], starts[None, :], 0), axis=1
    )
    position = (row_ids - row_start).astype(F32) + PREFIX_LEN
    half = HEAD_WIDTH // 2
    lanes = jnp.arange(2 * HEAD_WIDTH, dtype=jnp.int32) % HEAD_WIDTH
    frequency = jnp.exp((lanes % half).astype(F32) * (-2.0 * math.log(10000.0) / HEAD_WIDTH))
    angles = position[:, None] * frequency[None, :]
    cosines = jnp.cos(angles)
    sines = jnp.where(lanes[None, :] < half, -1.0, 1.0) * jnp.sin(angles)

    quarter = output_matrix.shape[0] // 4
    own_quarter = lax.dynamic_slice_in_dim(output_matrix, dp * quarter, quarter, 0)
    payload = jnp.concatenate([hidden, own_quarter], axis=0)
    far2, far1 = swap(payload, 4), swap(payload, 2)
    forwarded3, direct3 = swap(far2, 2), middle(payload)

    prepared = call(
        prepare_kernel,
        shape(512, 640),
        (
            ids,
            prefix_page_cache.reshape(-1, prefix_page_cache.shape[2]),
            adapter_up.reshape(-1, adapter_up.shape[2]),
            jnp.swapaxes(adapter_down, 1, 2).reshape(-1, MODEL_WIDTH),
            gain,
        ),
        1,
        far=(1, 2, 3),
        limit=62,
    )
    near1, near2 = swap(prepared, 1, "dp"), swap(prepared, 2, "dp")
    upper3, lower3 = swap(near2[0:256], 1, "dp"), swap(near1[256:512], 2, "dp")
    shared = [prepared, near1, near2, upper3]
    down_own, up_all = call(
        select_kernel,
        (shape(64, MODEL_WIDTH), shape(128, 384)),
        (ids, request_adapter, *shared, lower3),
        2,
        flops=0,
        moved=0,
    )
    down_other = swap(down_own, 1)

    rows = {0: [payload, swap(payload, 1)]}
    rows[1] = [far1, swap(far1, 1)]
    rows[2] = [far2, swap(far2, 1)]
    constants = (query_key_value_weight, down_own, down_other, up_all, cosines, sines, gain)
    rows[3] = [direct3, forwarded3, swap(direct3, 1), swap(forwarded3, 1)]

    chip = tensor // 2
    last = jnp.where((chip == 1) | (chip == 2), direct3[128:], forwarded3[128:])
    quarters = jnp.stack([payload[128:], far1[128:], far2[128:], last])
    outputs = [quarters] + [swap(quarters, m, "dp") for m in (1, 2, 3)]

    attn = call(
        attend_kernel,
        shape(group_rows, 128),
        (
            ids, lengths, request_prompt, prompt_page_table,
            *rows[0], *rows[1], *rows[2], *rows[3], *constants, *shared,
        ),
        4,
        scratch=(
            pltpu.VMEM((group_rows, 128), BF16),
            pltpu.VMEM((group_rows, 128), BF16),
            pltpu.VMEM((group_rows, 128), BF16),
            pltpu.VMEM((1024, 256), BF16),
            pltpu.SMEM((GROUP_REQUESTS + 1,), jnp.int32),
            pltpu.VMEM((group_rows // 128, 2, 128, 128), F32),
            pltpu.VMEM((MODEL_WIDTH, 128), BF16),
        ),
        flops=2 * 10**10,
        moved=2 * 10**6,
        limit=24,
    )

    heads2, heads1 = swap(attn, 4), swap(attn, 2)
    heads3, heads3f = middle(attn), swap(heads2, 2)
    all_heads = [attn, swap(attn, 1), heads1, swap(heads1, 1), heads2, swap(heads2, 1)]
    all_heads += [heads3, swap(heads3, 1), heads3f, swap(heads3f, 1)]

    collected = call(
        collect_kernel,
        (jax.ShapeDtypeStruct((2, 4 * quarter, MODEL_WIDTH), BF16),) * 2,
        (ids, *outputs),
        1,
    )
    collected = [part.reshape(-1, MODEL_WIDTH) for part in collected]
    weights = (
        *collected, *[swap(part, 1) for part in collected],
        attention_rate.reshape(1, -1), up_matrix, gate_matrix,
        up_scaling.reshape(1, -1), gate_scaling.reshape(1, -1), down_matrix,
    )
    def update(js, previous):
        operands = (ids, *all_heads, *[piece for j in js for piece in rows[j]], *weights, previous)
        return call(
            functools.partial(mlp_kernel, js),
            (shape(128 * len(js), MODEL_WIDTH),) * 2 + (shape(128, MODEL_WIDTH),) * (0 in js),
            operands,
            1,
            limit=24,
            flops=2 * 10**10,
            moved=10**7,
            unread=(len(operands) - 1,),
        )

    def chunk(kept, swapped):
        return (kept.astype(F32) + swapped.astype(F32)).astype(BF16)

    keep3, send3 = update((3,), ids)
    chunk3 = chunk(keep3, swap(send3, 1))
    inward, received3 = swap(chunk3, 2), middle(chunk3)
    keep, send = update((2, 1), keep3)
    got = swap(send, 1)
    received1 = swap(chunk(keep[128:256], got[128:256]), 2)
    joined = call(
        add_kernel,
        shape(128, MODEL_WIDTH, F32),
        (ids, keep, inward, received3),
        1,
        flops=2 * 10**10,
        unread=(3,),
    )
    chunk2 = chunk(joined, got[0:128])
    received2 = swap(chunk2, 4)
    keep0, send0, mixed = update((0,), chunk2)
    return call(
        final_kernel,
        shape(*hidden.shape),
        (
            mixed, keep0, swap(send0[0:64], 1), swap(send0[64:128], 1), received1, received2, received3,
            feedforward_rate.reshape(1, -1),
        ),
        0,
    )


def solution(mesh):
    placed = (
        P(("dp", "tensor"), None),
        P("dp", None),
        P("dp", None),
        P("dp", None),
        P(),
        P("dp", None, "tensor"),
        P(None, "tensor"),
        P("dp", None, None),
        P("dp", None, "tensor"),
        P("tensor"),
        P("tensor", None),
        P(),
        P(None, "tensor"),
        P(None, "tensor"),
        P("tensor"),
        P("tensor"),
        P("tensor", None),
        P(),
    )
    pairwise = mesh.shape["dp"] == 4 and mesh.shape["tensor"] == 8
    return jax.shard_map(
        local_pairwise if pairwise else local_generic, mesh=mesh, in_specs=placed, out_specs=P(("dp", "tensor"), None), check_vma=False
    )
```

```python
import functools
import math

import jax
import jax.numpy as jnp
from jax import lax
from jax.experimental import pallas as pl
from jax.experimental.pallas import tpu as pltpu
from jax.sharding import PartitionSpec as P

MODEL_WIDTH = 1280
HEAD_WIDTH = 64
ADAPTER_RANK = 16
GROUP_REQUESTS = 8
PAGE = 64
PREFIX_LEN = 256


adapter_scale = 0.5
epsilon = 1e-06


def renorm(matrix):
    return matrix * lax.rsqrt(jnp.mean(matrix * matrix, axis=-1, keepdims=True) + epsilon)


def to_unit(vectors):
    return vectors * lax.rsqrt(jnp.sum(vectors * vectors, axis=-1, keepdims=True) + epsilon)


def rotate(vectors, position):
    half_size = vectors.shape[-1] // 2
    frequency = jnp.exp(
        jnp.arange(half_size).astype(jnp.float32) * (-2.0 * math.log(10000.0) / vectors.shape[-1])
    )
    angles = position[:, None] * frequency[None, :]
    cosine = jnp.cos(angles)[:, None, :]
    sines = jnp.sin(angles)[:, None, :]
    first_half = vectors[..., :half_size]
    second_half = vectors[..., half_size:]
    return jnp.concatenate(
        [first_half * cosine - second_half * sines, first_half * sines + second_half * cosine],
        axis=-1,
    )


def layout(counts, total_rows):
    row_ends = jnp.cumsum(counts)
    starts = row_ends - counts
    row_ids = jnp.arange(total_rows, dtype=jnp.int32)
    request_number = jnp.sum((row_ids[:, None] >= row_ends[None, :]).astype(jnp.int32), axis=1)
    selected_adapter = (
        request_number[:, None] == jnp.arange(counts.shape[0], dtype=jnp.int32)[None, :]
    )
    offset = row_ids - jnp.sum(jnp.where(selected_adapter, starts[None, :], 0), axis=1)
    return (request_number, offset)


def attend(queries, key_all, value_all, request_number, key_request, key_row):
    rows_total = queries.shape[0]
    block_rows = min(512, rows_total)
    score_scale = math.sqrt(queries.shape[-1])
    row_ids = jnp.arange(rows_total, dtype=jnp.int32)

    def one_block(block_index):
        first_row = block_index * block_rows
        query_block = lax.dynamic_slice_in_dim(queries, first_row, block_rows, 0)
        request_block = lax.dynamic_slice_in_dim(request_number, first_row, block_rows, 0)
        row_block = lax.dynamic_slice_in_dim(row_ids, first_row, block_rows, 0)
        scores = (
            jnp.einsum("qhd,khd->hqk", query_block, key_all, preferred_element_type=jnp.float32)
            * score_scale
        )
        allowed = (request_block[:, None] == key_request[None, :]) & (
            key_row[None, :] <= row_block[:, None]
        )
        exp_scores = jnp.where(allowed[None], jnp.exp(scores), 0.0)
        weights = (exp_scores / jnp.sum(exp_scores, axis=-1, keepdims=True)).astype(jnp.bfloat16)
        mixed_block = jnp.einsum(
            "hqk,khd->qhd", weights, value_all, preferred_element_type=jnp.float32
        )
        return mixed_block.reshape(block_rows, -1).astype(jnp.bfloat16)

    blocks = lax.map(one_block, jnp.arange(rows_total // block_rows, dtype=jnp.int32))
    return blocks.reshape(rows_total, -1)


def hidden_units(row_values, up_matrix, gate_matrix, up_scaling, gate_scaling):
    up_part = jnp.dot(row_values, up_matrix, preferred_element_type=jnp.float32) * up_scaling
    gate_part = jnp.dot(row_values, gate_matrix, preferred_element_type=jnp.float32) * gate_scaling
    return (up_part * jax.nn.silu(gate_part)).astype(jnp.bfloat16)


def local_generic(
    hidden,
    lengths,
    request_prompt,
    request_adapter,
    prompt_page_table,
    prefix_page_cache,
    query_key_value_weight,
    adapter_down,
    adapter_up,
    attention_scale,
    output_matrix,
    attention_rate,
    up_matrix,
    gate_matrix,
    up_scaling,
    gate_scaling,
    down_matrix,
    feedforward_rate,
):
    tok_rows = hidden.shape[0]
    group_rows = tok_rows * lax.axis_size("tensor")
    heads_here = query_key_value_weight.shape[1] // (3 * HEAD_WIDTH)
    gain_qk = attention_scale.reshape(heads_here, HEAD_WIDTH)
    request_number, offset = layout(lengths[0], group_rows)
    position = offset.astype(jnp.float32) + PREFIX_LEN
    local_cache = prefix_page_cache.reshape(
        prefix_page_cache.shape[0], PAGE, heads_here, 2, HEAD_WIDTH
    )
    local_keys = (to_unit(local_cache[:, :, :, 0, :].astype(jnp.float32)) * gain_qk).astype(
        jnp.bfloat16
    )
    prepared = jnp.stack([local_keys, local_cache[:, :, :, 1, :]], axis=3).reshape(
        prefix_page_cache.shape
    )
    all_pages = lax.all_gather(prepared, "dp", axis=0, tiled=True)
    down_all, up_all = (
        lax.all_gather(adapter_down, "dp", axis=0, tiled=True),
        lax.all_gather(adapter_up, "dp", axis=0, tiled=True),
    )
    every_row = lax.all_gather(hidden, "tensor", axis=0, tiled=True)
    adapter_count = down_all.shape[0]
    onehot = (
        request_adapter[0][:, None] == jnp.arange(adapter_count, dtype=jnp.int32)[None, :]
    ).astype(jnp.bfloat16)
    selected_down = jnp.dot(
        onehot, down_all.reshape(adapter_count, -1), preferred_element_type=jnp.float32
    ).astype(jnp.bfloat16)
    selected_down = jnp.transpose(
        selected_down.reshape(GROUP_REQUESTS, MODEL_WIDTH, ADAPTER_RANK), (1, 0, 2)
    ).reshape(MODEL_WIDTH, GROUP_REQUESTS * ADAPTER_RANK)
    selected_up = jnp.dot(
        onehot, up_all.reshape(adapter_count, -1), preferred_element_type=jnp.float32
    ).astype(jnp.bfloat16)
    selected_up = selected_up.reshape(GROUP_REQUESTS * ADAPTER_RANK, heads_here * 3 * HEAD_WIDTH)
    request_of_slot = jnp.arange(GROUP_REQUESTS * ADAPTER_RANK, dtype=jnp.int32) // ADAPTER_RANK
    plain_projection = jnp.dot(
        every_row, query_key_value_weight, preferred_element_type=jnp.float32
    )
    adapter_middle = jnp.dot(every_row, selected_down, preferred_element_type=jnp.float32)
    adapter_middle = jnp.where(
        request_number[:, None] == request_of_slot[None, :], adapter_middle, 0.0
    ).astype(jnp.bfloat16)
    query_key_value = (
        plain_projection
        + adapter_scale * jnp.dot(adapter_middle, selected_up, preferred_element_type=jnp.float32)
    ).reshape(group_rows, heads_here, 3, HEAD_WIDTH)
    queries = (to_unit(rotate(query_key_value[:, :, 0, :], position)) * gain_qk).astype(
        jnp.bfloat16
    )
    key_own = (to_unit(rotate(query_key_value[:, :, 1, :], position)) * gain_qk).astype(
        jnp.bfloat16
    )
    value_own = query_key_value[:, :, 2, :].astype(jnp.bfloat16)
    page_list = prompt_page_table[request_prompt[0]].reshape(-1)
    picked = jnp.take(all_pages, page_list, axis=0).reshape(
        GROUP_REQUESTS * PREFIX_LEN, heads_here, 2, HEAD_WIDTH
    )
    key_all = jnp.concatenate([picked[:, :, 0, :], key_own], axis=0)
    value_all = jnp.concatenate([picked[:, :, 1, :], value_own], axis=0)
    key_request = jnp.concatenate(
        [jnp.arange(GROUP_REQUESTS * PREFIX_LEN, dtype=jnp.int32) // PREFIX_LEN, request_number],
        axis=0,
    )
    key_row = jnp.concatenate(
        [
            jnp.full((GROUP_REQUESTS * PREFIX_LEN,), -1, jnp.int32),
            jnp.arange(group_rows, dtype=jnp.int32),
        ],
        axis=0,
    )
    attn = attend(queries, key_all, value_all, request_number, key_request, key_row)
    attn_sum = lax.psum_scatter(
        jnp.dot(attn, output_matrix, preferred_element_type=jnp.float32).astype(jnp.bfloat16),
        "tensor",
        scatter_dimension=0,
        tiled=True,
    ).astype(jnp.float32)
    base_rows = hidden.astype(jnp.float32)
    mixed = renorm(base_rows + attention_rate * (renorm(attn_sum) - base_rows)).astype(jnp.bfloat16)
    unit_values = hidden_units(
        lax.all_gather(mixed, "tensor", axis=0, tiled=True),
        up_matrix,
        gate_matrix,
        up_scaling,
        gate_scaling,
    )
    mlp_sum = lax.psum_scatter(
        jnp.dot(unit_values, down_matrix, preferred_element_type=jnp.float32).astype(jnp.bfloat16),
        "tensor",
        scatter_dimension=0,
        tiled=True,
    ).astype(jnp.float32)
    mixed_rows = mixed.astype(jnp.float32)
    return renorm(mixed_rows + feedforward_rate * (renorm(mlp_sum) - mixed_rows)).astype(
        jnp.bfloat16
    )


CHIP_ROWS = 256
SCORE_LOG2 = math.sqrt(HEAD_WIDTH) / math.log(2.0)
VMEM = pl.BlockSpec(memory_space=pltpu.VMEM)
SMEM = pl.BlockSpec(memory_space=pltpu.SMEM)
BF16 = jnp.bfloat16
F32 = jnp.float32


def call(kernel, outs, operands, scalars, scratch=(), limit=12, flops=0, moved=0, far=(), unread=()):
    count = len(operands)
    specs = [SMEM] * scalars + [VMEM] * (count - scalars)
    for place in far:
        specs[place] = pl.BlockSpec(memory_space=pltpu.HBM)
    for place in unread:
        specs[place] = pl.BlockSpec(memory_space=pl.ANY)
    buffers = [pltpu.VMEM(operands[place].shape, operands[place].dtype) for place in far]
    if far:
        buffers.append(pltpu.SemaphoreType.DMA((len(far),)))

    def whole(*refs):
        refs = list(refs)
        if far:
            *near, arrivals = refs[len(refs) - len(far) - 1 :]
            refs = refs[: len(refs) - len(far) - 1]
            copies = [
                pltpu.make_async_copy(refs[place], near[i], arrivals.at[i])
                for i, place in enumerate(far)
            ]
            for copy in copies:
                copy.start()
            for copy in copies:
                copy.wait()
            for i, place in enumerate(far):
                refs[place] = near[i]
        kernel(*refs)

    return pl.pallas_call(
        whole,
        out_shape=outs,
        in_specs=specs,
        out_specs=jax.tree.map(lambda _: VMEM, outs),
        scratch_shapes=[*scratch, *buffers],
        compiler_params=pltpu.CompilerParams(vmem_limit_bytes=limit * 1024 * 1024),
        cost_estimate=pl.CostEstimate(flops=flops, bytes_accessed=moved, transcendentals=0),
    )(*operands)


def shape(rows, columns, kind=BF16):
    return jax.ShapeDtypeStruct((rows, columns), kind)


def iota(dims, axis):
    return lax.broadcasted_iota(jnp.int32, dims, axis)


def first_head(rows):
    return iota((rows, 2 * HEAD_WIDTH), 1) < HEAD_WIDTH


def unit_heads(vectors, gain):
    low = first_head(vectors.shape[0])
    squares = vectors * vectors
    sum_low = jnp.sum(jnp.where(low, squares, 0.0), axis=-1, keepdims=True)
    sum_high = jnp.sum(jnp.where(low, 0.0, squares), axis=-1, keepdims=True)
    return vectors * lax.rsqrt(jnp.where(low, sum_low, sum_high) + epsilon) * gain


def dot(left, right):
    return jnp.dot(left, right, preferred_element_type=F32)


def dot_nt(left, right):
    return lax.dot_general(
        left, right, (((1,), (1,)), ((), ())), preferred_element_type=F32
    )


def prepare_kernel(ids, pages, up, down, gain, out):
    rows = pages.shape[0]
    low = first_head(rows)
    left = pages[:, 0:128].astype(F32)
    right = pages[:, 128:256].astype(F32)
    keys = jnp.where(low, left, pltpu.roll(right, HEAD_WIDTH, 1))
    values = jnp.where(low, pltpu.roll(left, HEAD_WIDTH, 1), right)
    out[0:256, 0:128] = unit_heads(keys, gain[...]).astype(BF16)
    out[0:256, 128:256] = values.astype(BF16)
    out[0:256, 256:640] = up[...]
    row, column = iota((128, 256), 0), iota((128, 256), 1)
    source = (row // 8) * ADAPTER_RANK + 8 * (ids[0] % 2) + row % 8
    picked = dot((column == source).astype(BF16), down[...]).astype(BF16)
    out[256:384, :] = picked[:, 0:640]
    out[384:512, :] = picked[:, 640:1280]


def by_request(index, scalars):
    picked = jnp.zeros_like(index)
    for request in range(GROUP_REQUESTS):
        picked = jnp.where(index == request, scalars[0, request], picked)
    return picked


def select_kernel(ids, adapters, g0, g1, g2, g3, g4, down_out, up_out):
    core, dp = ids[0] % 2, ids[1]
    row, column = iota((64, 128), 0), iota((64, 128), 1)
    adapter = by_request(row // 8, adapters)
    source = (adapter % 16) * 8 + row % 8
    owner = (adapter // 16) ^ dp
    up_row, up_column = iota((128, 256), 0), iota((128, 256), 1)
    up_adapter = by_request((up_row % 64) // 8, adapters)
    up_source = (up_adapter % 16) * 16 + 8 * ((up_row // 64) ^ core) + up_row % 8
    up_owner = (up_adapter // 16) ^ dp
    left = right = up_total = 0.0
    for m, g in enumerate((g0, g1, g2, g3)):
        lower, first = (g4, 0) if m == 3 else (g, 256)
        hot = ((column == source) & (owner == m)).astype(BF16)
        left = left + dot(hot, lower[first : first + 128, :])
        right = right + dot(hot, lower[first + 128 : first + 256, :])
        up_hot = ((up_column == up_source) & (up_owner == m)).astype(BF16)
        up_total = up_total + dot(up_hot, g[0:256, 256:640])
    down_out[:, 0:640] = left.astype(BF16)
    down_out[:, 640:1280] = right.astype(BF16)
    up_out[...] = up_total.astype(BF16)


def middle_chip(ids):
    chip = ids[0] // 2
    return (chip == 1) | (chip == 2)


def arrived(ids, parts):
    if len(parts) == 1:
        return parts[0][0:128, :]
    return jnp.where(middle_chip(ids), parts[0][0:128, :], parts[1][0:128, :])


def piece_spots(ids, j):
    core = ids[0] % 2
    base = ((ids[0] // 2) ^ j) * CHIP_ROWS
    return [pl.multiple_of(base + side * 128, 128) for side in (core, 1 - core)]


def row_pieces(ids, refs, js):
    pieces = []
    for j in js:
        count = 2 if j == 3 else 1
        pieces += [arrived(ids, refs[:count]), arrived(ids, refs[count : 2 * count])]
        refs = refs[2 * count :]
    return pieces, refs


def request_starts(lengths):
    begins = [jnp.int32(0)]
    for i in range(GROUP_REQUESTS):
        begins.append(begins[-1] + lengths[0, i])
    return begins


def project(j, ids, begins, pieces, weight, down, up, cosines, sines, gain):
    rows = jnp.concatenate(pieces, axis=0)
    count = rows.shape[0]
    row = jnp.concatenate([spot + iota((128, 128), 0) for spot in piece_spots(ids, j)], axis=0)
    request = (iota((1, 128), 1) % 64) // 8
    first, end = jnp.zeros_like(request), jnp.zeros_like(request)
    for i in range(GROUP_REQUESTS):
        first = jnp.where(request == i, begins[i], first)
        end = jnp.where(request == i, begins[i + 1], end)
    total = dot(rows, jnp.concatenate([weight[...], down[...]], axis=1))
    total, middle = total[:, 0:384], total[:, 384:512]
    middle = jnp.where((row >= first) & (row < end), middle, 0.0).astype(BF16)
    total = total + adapter_scale * dot(middle, up[...])
    part0, part1, part2 = total[:, 0:128], total[:, 128:256], total[:, 256:384]
    low = first_head(count)
    query = jnp.where(low, part0, part1)
    key = pltpu.roll(jnp.where(low, part2, part0), HEAD_WIDTH, 1)
    value = jnp.where(low, part1, part2).astype(BF16)
    cosine = jnp.concatenate([cosines[pl.ds(spot, 128), :] for spot in piece_spots(ids, j)], axis=0)
    sine = jnp.concatenate([sines[pl.ds(spot, 128), :] for spot in piece_spots(ids, j)], axis=0)
    half = HEAD_WIDTH // 2
    head_low = (iota((count, 128), 1) % HEAD_WIDTH) < half

    def finish(x):
        turned = jnp.where(head_low, pltpu.roll(x, 128 - half, 1), pltpu.roll(x, half, 1))
        return unit_heads(x * cosine + turned * sine, gain[...]).astype(BF16)

    return finish(query), finish(key), value


def attend_kernel(ids, lengths, prompts, table, *refs):
    pieces, refs = row_pieces(ids, refs, range(4))
    weight, down, down_other, *constants, g0, g1, g2, g3, out = refs[:-7]
    queries, keys, values, pages, starts, sums, turned = refs[-7:]
    turned[:, 0:64] = jnp.transpose(down[...])
    turned[:, 64:128] = jnp.transpose(down_other[...])
    begins = request_starts(lengths)
    for i, begin in enumerate(begins):
        starts[i] = begin
    for j in range(4):
        rows = pieces[2 * j : 2 * j + 2]
        parts = project(j, ids, begins, rows, weight, turned, *constants)
        for part, target in zip(parts, (queries, keys, values)):
            for side, spot in enumerate(piece_spots(ids, j)):
                target[pl.ds(spot, 128), :] = part[side * 128 : side * 128 + 128]
    for m, g in enumerate((g0, g1, g2, g3)):
        pages[pl.ds(pl.multiple_of((ids[1] ^ m) * 256, 256), 256), :] = g[0:256, 0:256]
    tiles = out.shape[0] // 128
    low = first_head(128)
    low_keys = first_head(256)
    ones = jnp.ones((256, 128), BF16)

    def tile_queries(tile):
        query = queries[pl.ds(pl.multiple_of(tile * 128, 128), 128), :]
        zero = jnp.zeros_like(query)
        both = jnp.concatenate(
            [jnp.where(low, query, zero), jnp.where(low, zero, query)], axis=0
        )
        return both, tile * 128 + iota((256, 1), 0) % 128

    def prefix(request):
        prompt = prompts[0, request]
        spots = [pl.multiple_of(table[prompt, p] * PAGE, PAGE) for p in range(PREFIX_LEN // PAGE)]
        return (
            jnp.concatenate([pages[pl.ds(s, PAGE), 0:128] for s in spots], axis=0),
            jnp.concatenate([pages[pl.ds(s, PAGE), 128:256] for s in spots], axis=0),
        )

    def window(spot):
        spot = pl.multiple_of(spot, 128)
        return keys[pl.ds(spot, 256), :], values[pl.ds(spot, 256), :], spot + iota((256, 256), 1)

    def products(both, key, value, mask):
        weights = jnp.where(mask, jnp.exp2(dot_nt(both, key) * SCORE_LOG2), 0.0).astype(BF16)
        return (
            dot(weights[:128], jnp.where(low_keys, value, ones)),
            dot(weights[128:], jnp.where(low_keys, ones, value)),
        )

    firsts = []
    for tile in range(tiles):
        base = tile * 128
        both, row = tile_queries(tile)
        first = jnp.int32(0)
        row_start = jnp.zeros_like(row)
        for begin in begins[1:GROUP_REQUESTS]:
            row_start = jnp.where(row >= begin, begin, row_start)
            first = first + (begin <= base).astype(jnp.int32)
        firsts.append(first)
        mask = jnp.broadcast_to(row < starts[first + 1], (256, PREFIX_LEN))
        shared = products(both, *prefix(first), mask)
        key, value, column = window(max(base - 128, 0))
        own = products(both, key, value, (column >= row_start) & (column <= row))
        for head in (0, 1):
            sums[tile, head] = shared[head] + own[head]
    for i in range(1, GROUP_REQUESTS):
        begin, end = begins[i], begins[i + 1]
        tile = begin // 128
        both, row = tile_queries(tile)
        mask = (row >= begin) & (row < end) & (begin % 128 != 0)
        more = products(both, *prefix(i), jnp.broadcast_to(mask, (256, PREFIX_LEN)))
        for head in (0, 1):
            sums[tile, head] += more[head]
    for tile in range(2, tiles):
        base = tile * 128
        first = firsts[tile]
        begin, end = starts[first], starts[first + 1]

        def earlier(step, carry, tile=tile, base=base, begin=begin, end=end):
            both, row = tile_queries(tile)
            stop = base - 128 - 256 * step
            key, value, column = window(jnp.maximum(stop - 256, 0))
            mask = (column >= begin) & (column < stop) & (row < end)
            more = products(both, key, value, mask)
            for head in (0, 1):
                sums[tile, head] += more[head]
            return carry

        lax.fori_loop(0, jnp.maximum(base + 127 - begin, 0) // 256, earlier, 0)
    for tile in range(tiles):
        left, right = sums[tile, 0], sums[tile, 1]
        weight = pltpu.roll(jnp.where(low, right, left), HEAD_WIDTH, 1)
        out[tile * 128 : tile * 128 + 128, :] = (jnp.where(low, left, right) / weight).astype(BF16)


def collect_kernel(ids, o0, o1, o2, o3, *outs):
    for m, part in enumerate((o0, o1, o2, o3)):
        spot = pl.multiple_of((ids[1] ^ m) * 32, 32)
        for j in range(4):
            outs[j // 2][j % 2, pl.ds(spot, 32), :] = part[j]


def mlp_kernel(js, ids, *refs):
    heads_in, refs = refs[:10], refs[10:]
    pieces, refs = row_pieces(ids, refs, js)
    matrices, refs = refs[:4], refs[4:]
    rate, up, gate, up_scale, gate_scale, down, _, keep, send, *rest = refs
    direct = middle_chip(ids)
    for place, j in enumerate(js):
        spots = piece_spots(ids, j)

        def rows_of(heads):
            return jnp.concatenate([heads[pl.ds(spot, 128), :] for spot in spots], axis=0)

        columns = []
        for side in (0, 1):
            for distance in range(4):
                columns.append(rows_of(heads_in[2 * distance + side]))
            columns[-1] = jnp.where(direct, columns[-1], rows_of(heads_in[8 + side]))
        output = jnp.concatenate([matrix[...] for matrix in matrices], axis=0)
        attn_sum = dot(jnp.concatenate(columns, axis=1), output)
        base = jnp.concatenate(pieces[2 * place : 2 * place + 2], axis=0).astype(F32)
        mixed = renorm(base + rate[...] * (renorm(attn_sum) - base)).astype(BF16)
        both = dot(mixed, jnp.concatenate([up[...], gate[...]], axis=1))
        up_part = both[:, : up.shape[1]] * up_scale[...]
        gate_part = both[:, up.shape[1] :] * gate_scale[...]
        unit_values = (up_part * (gate_part / (1.0 + jnp.exp(-gate_part)))).astype(BF16)
        result = dot(unit_values, down[...]).astype(BF16)
        keep[place * 128 : place * 128 + 128, :] = result[0:128]
        send[place * 128 : place * 128 + 128, :] = result[128:256]
        if j == 0:
            rest[0][...] = mixed[0:128]


def add_kernel(ids, keep, inward, direct, out):
    more = inward[...].astype(F32)
    out[...] = keep[0:128, :].astype(F32) + jnp.where(middle_chip(ids), more, 0.0)


def final_kernel(mixed, keep, got0, got1, r1, r2, r3, rate, out):
    got = jnp.concatenate([got0[...], got1[...]], axis=0)
    mlp_sum = keep[...].astype(F32) + got.astype(F32)
    for r in (r1, r2, r3):
        mlp_sum = mlp_sum + r[...].astype(F32)
    base = mixed[...].astype(F32)
    out[...] = renorm(base + rate[...] * (renorm(mlp_sum) - base)).astype(BF16)


def swap(values, distance, axis="tensor"):
    size = lax.axis_size(axis)
    return lax.ppermute(values, axis, [(i, i ^ distance) for i in range(size)])


def middle(values):
    return lax.ppermute(values, "tensor", [(2, 4), (3, 5), (4, 2), (5, 3)])


def local_pairwise(
    hidden,
    lengths,
    request_prompt,
    request_adapter,
    prompt_page_table,
    prefix_page_cache,
    query_key_value_weight,
    adapter_down,
    adapter_up,
    attention_scale,
    output_matrix,
    attention_rate,
    up_matrix,
    gate_matrix,
    up_scaling,
    gate_scaling,
    down_matrix,
    feedforward_rate,
):
    group_rows = hidden.shape[0] * lax.axis_size("tensor")
    tensor, dp = lax.axis_index("tensor"), lax.axis_index("dp")
    ids = jnp.stack([tensor, dp]).astype(jnp.int32)
    gain = attention_scale.reshape(1, -1)

    row_ids = jnp.arange(group_rows, dtype=jnp.int32)
    starts = jnp.cumsum(lengths[0]) - lengths[0]
    row_start = jnp.max(
        jnp.where(row_ids[:, None] >= starts[None, :], starts[None, :], 0), axis=1
    )
    position = (row_ids - row_start).astype(F32) + PREFIX_LEN
    half = HEAD_WIDTH // 2
    lanes = jnp.arange(2 * HEAD_WIDTH, dtype=jnp.int32) % HEAD_WIDTH
    frequency = jnp.exp((lanes % half).astype(F32) * (-2.0 * math.log(10000.0) / HEAD_WIDTH))
    angles = position[:, None] * frequency[None, :]
    cosines = jnp.cos(angles)
    sines = jnp.where(lanes[None, :] < half, -1.0, 1.0) * jnp.sin(angles)

    quarter = output_matrix.shape[0] // 4
    own_quarter = lax.dynamic_slice_in_dim(output_matrix, dp * quarter, quarter, 0)
    payload = jnp.concatenate([hidden, own_quarter], axis=0)
    far2, far1 = swap(payload, 4), swap(payload, 2)
    forwarded3, direct3 = swap(far2, 2), middle(payload)

    prepared = call(
        prepare_kernel,
        shape(512, 640),
        (
            ids,
            prefix_page_cache.reshape(-1, prefix_page_cache.shape[2]),
            adapter_up.reshape(-1, adapter_up.shape[2]),
            jnp.swapaxes(adapter_down, 1, 2).reshape(-1, MODEL_WIDTH),
            gain,
        ),
        1,
        far=(1, 2, 3),
        limit=62,
    )
    near1, near2 = swap(prepared, 1, "dp"), swap(prepared, 2, "dp")
    upper3, lower3 = swap(near2[0:256], 1, "dp"), swap(near1[256:512], 2, "dp")
    shared = [prepared, near1, near2, upper3]
    down_own, up_all = call(
        select_kernel,
        (shape(64, MODEL_WIDTH), shape(128, 384)),
        (ids, request_adapter, *shared, lower3),
        2,
        flops=0,
        moved=0,
    )
    down_other = swap(down_own, 1)

    rows = {0: [hidden, swap(hidden, 1)]}
    rows[1] = [far1, swap(far1, 1)]
    rows[2] = [far2, swap(far2, 1)]
    constants = (query_key_value_weight, down_own, down_other, up_all, cosines, sines, gain)
    rows[3] = [direct3, forwarded3, swap(direct3, 1), swap(forwarded3, 1)]

    chip = tensor // 2
    last = jnp.where((chip == 1) | (chip == 2), direct3[128:], forwarded3[128:])
    quarters = jnp.stack([payload[128:], far1[128:], far2[128:], last])
    outputs = [quarters] + [swap(quarters, m, "dp") for m in (1, 2, 3)]

    attn = call(
        attend_kernel,
        shape(group_rows, 128),
        (
            ids, lengths, request_prompt, prompt_page_table,
            *rows[0], *rows[1], *rows[2], *rows[3], *constants, *shared,
        ),
        4,
        scratch=(
            pltpu.VMEM((group_rows, 128), BF16),
            pltpu.VMEM((group_rows, 128), BF16),
            pltpu.VMEM((group_rows, 128), BF16),
            pltpu.VMEM((1024, 256), BF16),
            pltpu.SMEM((GROUP_REQUESTS + 1,), jnp.int32),
            pltpu.VMEM((group_rows // 128, 2, 128, 128), F32),
            pltpu.VMEM((MODEL_WIDTH, 128), BF16),
        ),
        flops=2 * 10**10,
        moved=2 * 10**6,
        limit=24,
    )

    heads2, heads1 = swap(attn, 4), swap(attn, 2)
    heads3, heads3f = middle(attn), swap(heads2, 2)
    all_heads = [attn, swap(attn, 1), heads1, swap(heads1, 1), heads2, swap(heads2, 1)]
    all_heads += [heads3, swap(heads3, 1), heads3f, swap(heads3f, 1)]

    collected = call(
        collect_kernel,
        (jax.ShapeDtypeStruct((2, 4 * quarter, MODEL_WIDTH), BF16),) * 2,
        (ids, *outputs),
        1,
    )
    collected = [part.reshape(-1, MODEL_WIDTH) for part in collected]
    weights = (
        *collected, *[swap(part, 1) for part in collected],
        attention_rate.reshape(1, -1), up_matrix, gate_matrix,
        up_scaling.reshape(1, -1), gate_scaling.reshape(1, -1), down_matrix,
    )
    def update(js, previous):
        operands = (ids, *all_heads, *[piece for j in js for piece in rows[j]], *weights, previous)
        return call(
            functools.partial(mlp_kernel, js),
            (shape(128 * len(js), MODEL_WIDTH),) * 2 + (shape(128, MODEL_WIDTH),) * (0 in js),
            operands,
            1,
            limit=24,
            flops=2 * 10**10,
            moved=10**7,
            unread=(len(operands) - 1,),
        )

    def chunk(kept, swapped):
        return (kept.astype(F32) + swapped.astype(F32)).astype(BF16)

    keep3, send3 = update((3,), ids)
    chunk3 = chunk(keep3, swap(send3, 1))
    inward, received3 = swap(chunk3, 2), middle(chunk3)
    keep, send = update((2, 1), keep3)
    got = swap(send, 1)
    received1 = swap(chunk(keep[128:256], got[128:256]), 2)
    joined = call(
        add_kernel,
        shape(128, MODEL_WIDTH, F32),
        (ids, keep, inward, received3),
        1,
        flops=2 * 10**10,
        unread=(3,),
    )
    chunk2 = chunk(joined, got[0:128])
    received2 = swap(chunk2, 4)
    keep0, send0, mixed = update((0,), chunk2)
    return call(
        final_kernel,
        shape(*hidden.shape),
        (
            mixed, keep0, swap(send0[0:64], 1), swap(send0[64:128], 1), received1, received2, received3,
            feedforward_rate.reshape(1, -1),
        ),
        0,
    )


def solution(mesh):
    placed = (
        P(("dp", "tensor"), None),
        P("dp", None),
        P("dp", None),
        P("dp", None),
        P(),
        P("dp", None, "tensor"),
        P(None, "tensor"),
        P("dp", None, None),
        P("dp", None, "tensor"),
        P("tensor"),
        P("tensor", None),
        P(),
        P(None, "tensor"),
        P(None, "tensor"),
        P("tensor"),
        P("tensor"),
        P("tensor", None),
        P(),
    )
    pairwise = mesh.shape["dp"] == 4 and mesh.shape["tensor"] == 8
    return jax.shard_map(
        local_pairwise if pairwise else local_generic, mesh=mesh, in_specs=placed, out_specs=P(("dp", "tensor"), None), check_vma=False
    )
```
